32 devices in a mesh: rows: 4 (over y, x), vocab: 8 (over z, core).
Axes of the slice: x: 2, y: 2, z: 4, core: 2. Of those that a mesh axis runs over, the one named last changes fastest.
Arguments:
- tokens: int32 [4096], P('rows'), may hold values from 0 to 50303
- loss_position_mask: int32 [4096], P('rows'), may hold values from 0 to 1
- lengths: int32 [4, 5], P('rows'), may hold values from 1 to 512, 1024 in all within a row
- owners: int32 [32], replicated, may hold values from 0 to 31, each once
- embed_in: bfloat16 [50304, 1024], P('vocab'), may hold values from -6 to 6
- unembedding_table: bfloat16 [50304, 1024], P('vocab'), may hold values from -0.375 to 0.375
- frozen_qkv: bfloat16 [1024, 3072], replicated, may hold values from -0.1875 to 0.1875
- frozen_out: bfloat16 [1024, 1024], replicated, may hold values from -1.5 to 1.5
- frozen_up: bfloat16 [1024, 4096], replicated, may hold values from -0.1875 to 0.1875
- frozen_down: bfloat16 [4096, 1024], replicated, may hold values from -0.09375 to 0.09375
- frozen_bias: float32 [9216], replicated, may hold values from -0.6 to 0.6
- norm_gain: float32 [3, 1024], replicated, may hold values from 0.5 to 1.5
- norm_shift: float32 [3, 1024], replicated, may hold values from -0.6 to 0.6
- master_matrix: float32 [32, 256, 256], P('vocab'), may hold values from -0.06 to 0.06
- lens_bias: float32 [2, 1024], P(None, 'vocab'), may hold values from -0.6 to 0.6
- matrix_first: float32 [32, 256, 256], P('vocab'), may hold values from -0.2986819 to 0.2986819
- matrix_second: float32 [32, 256, 256], P('vocab'), may hold values from 0.0002048 to 0.0008192
- left_stat: float32 [32, 256, 256], P('vocab'), as said below
- right_stat: float32 [32, 256, 256], P('vocab'), as said below
- left_basis: float32 [32, 256, 256], P('vocab'), may hold values from -1 to 1, as said below
- right_basis: float32 [32, 256, 256], P('vocab'), may hold values from -1 to 1, as said below
- bias_first: float32 [2, 1024], P(None, 'vocab'), may hold values from -0.2986819 to 0.2986819
- bias_second: float32 [2, 1024], P(None, 'vocab'), may hold values from 0.0002048 to 0.0008192
Outputs:
- loss_sum: float32 [], replicated
- loss_count: float32 [], replicated
- new_matrix: float32 [32, 256, 256], P('vocab')
- new_first: float32 [32, 256, 256], P('vocab')
- new_second: float32 [32, 256, 256], P('vocab')
- new_left: float32 [32, 256, 256], P('vocab')
- new_right: float32 [32, 256, 256], P('vocab')
- renewed_left_basis: float32 [32, 256, 256], P('vocab')
- new_rbasis: float32 [32, 256, 256], P('vocab')
- new_bias: float32 [2, 1024], P(None, 'vocab')
- new_bias_first: float32 [2, 1024], P(None, 'vocab')
- new_bias_second: float32 [2, 1024], P(None, 'vocab')
The draws below stay inside these ranges and needn't reach their ends.
Inputs may be any that keep to these rules, and one draw needn't show every extreme that they name: `lengths`: each row sums to 1024, and its largest entry is exactly 512. `owners`: each block number appears once. `left_stat`: each block symmetric positive definite. `right_stat`: each block symmetric positive definite. `left_basis`: each block orthogonal. `right_basis`: each block orthogonal.
All inputs are finite; a program needn't handle non-finite values.
Results may differ from the reference program's by a relative error of at most 0.034.
Values may be sent and summed in bfloat16 or wider, within the bound.
No kernel may reach another device: no remote copies, remote signals or barrier semaphores. Data moves between devices by JAX's collectives and lax.ppermute only.
A program may use at most 576 MiB of HBM per device.

```python
import math
import jax
import jax.numpy as jnp
import numpy as np
from jax import lax

D = 1024
HEADS = 16
HEAD_DIM = 64
ROT = 16
FF = 4096
VOCAB = 50304
BS = 256
SEQS = 5
STEP = 5
GROUP = 1024
TOKENS = 4096
BLOCKS = 32
N_ROWS = 4


def draw_loss_position_mask(key, part):
    key = jax.random.fold_in(key, 11)
    drawn = jax.random.randint(key, (TOKENS,), 0, 1000000)
    frac = jnp.arange(TOKENS, dtype=jnp.int32) * 1000 // TOKENS
    limit = 20000 + 980 * (frac * frac * frac // 1000000)
    return (drawn < limit).astype(jnp.int32)


def draw_unembedding_table(key, part):
    key = jax.random.fold_in(key, 12)
    ramp = jnp.arange(VOCAB, dtype=jnp.float32) / VOCAB
    base = jnp.clip(jax.random.normal(key, (VOCAB, D), jnp.float32), -4.0, 4.0)
    spread = 1.0 + 2.0 * ramp
    return (base * spread[:, None] * D ** (-0.5)).astype(jnp.bfloat16)


def stat_matrix(noise, diag_key):
    level = BS * 0.0001 * (TOKENS // 2) / 19.0
    diagonal = jnp.exp(jax.random.uniform(diag_key, (BLOCKS, BS), jnp.float32, 0.0, 1.3862944))
    symmetric = (noise + jnp.swapaxes(noise, 1, 2)) * (0.3 / (2.0 * BS) ** 0.5)
    identity = jnp.eye(BS, dtype=jnp.float32)
    return level * (identity[None] * diagonal[:, :, None] + symmetric)


def draw_left_stat(key, part):
    key = jax.random.fold_in(key, 13)
    noise_key, diag_key = jax.random.split(key)
    noise = jnp.clip(jax.random.normal(noise_key, (BLOCKS, BS, BS), jnp.float32), -4.0, 4.0)
    return stat_matrix(noise, diag_key)


def draw_right_stat(key, part):
    key = jax.random.fold_in(key, 14)
    noise_key, diag_key = jax.random.split(key)
    noise = jnp.clip(jax.random.normal(noise_key, (BLOCKS, BS, BS), jnp.float32), -4.0, 4.0)
    return stat_matrix(noise, diag_key)


def shuffle_one(one_key):
    return jax.random.permutation(one_key, BS)


def basis_matrix(key):
    turn_key, order_key = jax.random.split(key)
    angle = jax.random.uniform(turn_key, (BLOCKS, BS // 2), jnp.float32, 0.3, 1.2)
    row_at = jnp.arange(BS)[:, None]
    column_at = jnp.arange(BS)[None, :]
    theta = jnp.repeat(angle, 2, axis=1)[:, :, None]
    cosine = jnp.cos(theta)
    sine = jnp.sin(theta)
    paired = row_at // 2 == column_at // 2
    even_row = row_at % 2 == 0
    entry = jnp.where(row_at == column_at, cosine, jnp.where(even_row, -sine, sine))
    entry = jnp.where(paired[None], entry, 0.0)
    orders = jax.vmap(shuffle_one)(jax.random.split(order_key, BLOCKS))
    return entry[jnp.arange(BLOCKS)[:, None], orders]


def draw_left_basis(key, part):
    key = jax.random.fold_in(key, 15)
    return basis_matrix(key)


def draw_right_basis(key, part):
    key = jax.random.fold_in(key, 16)
    return basis_matrix(key)


def set_ends(values, own_key, smallest, high):
    longest = values.shape.index(max(values.shape))
    spots = []
    for shift in (0, 1):
        where = [jax.random.randint(jax.random.fold_in(own_key, axis), (), 0, length) for axis, length in enumerate(values.shape)]
        where[longest] = (where[longest] + shift) % values.shape[longest]
        spots.append(tuple(where))
    return values.at[spots[0]].set(smallest).at[spots[1]].set(high)


def level_of(own_key, dims, pieces, least, high):
    loudness, own = 1.0, jax.random.fold_in(own_key, 6)
    for dim, shards_of in pieces:
        draws = jnp.exp(jax.random.uniform(jax.random.fold_in(own, dim), (shards_of,), jnp.float32, least / len(pieces), high / len(pieces)))
        loudness = loudness * jnp.repeat(draws, dims[dim] // shards_of).reshape([-1 if axis == dim else 1 for axis in range(len(dims))])
    return loudness


def length_profile(number_of, total, most, slope):
    portions = [(1 << 20) // math.isqrt(rank ** slope) + 1 for rank in range(2, number_of + 1)]
    spare, holding = total - most - (number_of - 1), [1] * (number_of - 1)
    while spare > 0:
        movable = [i for i in range(number_of - 1) if holding[i] < most]
        mass, remaining = sum([portions[i] for i in movable]), spare
        for i in movable:
            more = min(most - holding[i], max(1, remaining * portions[i] // mass), spare)
            holding[i] = holding[i] + more
            spare = spare - more
    return np.array([most] + holding)


def uneven_parts(rng, amount, total, bound, lean):
    if amount == 2:
        one = jax.random.randint(rng, (), max(1, total - bound), min(bound, total - 1) + 1)
        return jnp.stack([one, total - one])
    sizes = jnp.asarray(length_profile(amount, total, bound, lean), jnp.int32)
    pairs = (amount - 1) // 2
    source_of, sink = sizes[1:1 + 2 * pairs:2], sizes[2:2 + 2 * pairs:2]
    room = jnp.minimum(source_of - 1, bound - sink)
    shifted = jax.random.randint(jax.random.fold_in(rng, 1), (pairs,), 0, 1 << 20) % (room + 1)
    sizes = sizes.at[1:1 + 2 * pairs:2].set(source_of - shifted).at[2:2 + 2 * pairs:2].set(sink + shifted)
    return sizes[jax.random.permutation(jax.random.fold_in(rng, 2), amount)]


def normal_values(own_key, dims, deviation, most, shards=(), held_as=jnp.bfloat16):
    level = level_of(own_key, dims, shards, -0.22, 0.18) if shards else 1.0
    result = jax.random.normal(own_key, dims, jnp.float32) * deviation * level
    return jnp.minimum(jnp.maximum(result, -most), most).astype(held_as)


def setup_inputs(seed: int = 0) -> dict:
    seeds = jax.random.split(jax.random.key(seed), 24)
    return {
        "tokens": set_ends(jax.random.randint(seeds[0], (TOKENS,), 0, VOCAB), jax.random.fold_in(seeds[0], 1), 0, VOCAB - 1).astype(jnp.int32),
        "loss_position_mask": draw_loss_position_mask(jax.random.fold_in(seeds[23], 71), 0),
        "lengths": jax.vmap(lambda own: uneven_parts(own, SEQS, GROUP, GROUP // 2, 1))(jax.random.split(seeds[2], N_ROWS)).reshape((N_ROWS, SEQS)).astype(jnp.int32),
        "owners": jax.random.permutation(seeds[3], BLOCKS).astype(jnp.int32),
        "embed_in": normal_values(seeds[4], (VOCAB, D), 1.0, 6.0, ((0, 8),)),
        "unembedding_table": draw_unembedding_table(jax.random.fold_in(seeds[23], 71), 0),
        "frozen_qkv": normal_values(seeds[6], (D, 3 * D), D ** -0.5, 0.1875),
        "frozen_out": normal_values(seeds[7], (D, D), (D // 64) ** -0.5, 1.5),
        "frozen_up": normal_values(seeds[8], (D, FF), D ** -0.5, 0.1875),
        "frozen_down": normal_values(seeds[9], (FF, D), FF ** -0.5, 0.09375),
        "frozen_bias": normal_values(seeds[10], (5 * D + FF,), 0.1, 0.6, (), jnp.float32),
        "norm_gain": jnp.clip(1.0 + 0.1 * jax.random.normal(seeds[11], (3, D), jnp.float32), 0.5, 1.5),
        "norm_shift": normal_values(seeds[12], (3, D), 0.1, 0.6, (), jnp.float32),
        "master_matrix": normal_values(seeds[13], (BLOCKS, BS, BS), 0.01, 0.06, ((0, 8),), jnp.float32),
        "lens_bias": normal_values(seeds[14], (2, D), 0.1, 0.6, ((1, 8),), jnp.float32),
        "matrix_first": normal_values(seeds[15], (BLOCKS, BS, BS), (0.0011 * (TOKENS // 2) ** 0.5), 0.2986819, ((0, 8),), jnp.float32),
        "matrix_second": jnp.clip(jnp.exp(math.log(0.0008192) - 1.3862944 * jax.random.uniform(seeds[16], (BLOCKS, BS, BS), jnp.float32) ** level_of(seeds[16], (BLOCKS, BS, BS), ((0, 8),), -0.2, 0.2)), 0.0002048, 0.0008192),
        "left_stat": draw_left_stat(jax.random.fold_in(seeds[23], 71), 0),
        "right_stat": draw_right_stat(jax.random.fold_in(seeds[23], 71), 0),
        "left_basis": draw_left_basis(jax.random.fold_in(seeds[23], 71), 0),
        "right_basis": draw_right_basis(jax.random.fold_in(seeds[23], 71), 0),
        "bias_first": normal_values(seeds[21], (2, D), (0.0011 * (TOKENS // 2) ** 0.5), 0.2986819, ((1, 8),), jnp.float32),
        "bias_second": jnp.clip(jnp.exp(math.log(0.0008192) - 1.3862944 * jax.random.uniform(seeds[22], (2, D), jnp.float32) ** level_of(seeds[22], (2, D), ((1, 8),), -0.2, 0.2)), 0.0002048, 0.0008192),
    }


HIGHEST = lax.Precision.HIGHEST
NORM_EPS = 1e-05
BETA_ONE = 0.9
BETA_TWO = 0.999
BETA_STAT = 0.95
ADAM_EPS = 1e-08
MATRIX_RATE = 0.01
BIAS_RATE = 0.1
DECAY = 0.1
MASKED = -1e+30

@jax.custom_vjp
def low(v):
    return lax.optimization_barrier(v.astype(jnp.bfloat16)).astype(jnp.float32)

@jax.custom_vjp
def low_back(v):
    return v

def low_keep(v):
    return (low(v), None)

def low_pass(kept, grad):
    return (grad,)

def back_keep(v):
    return (v, None)

def back_low(kept, grad):
    return (low(grad),)
low.defvjp(low_keep, low_pass)
low_back.defvjp(back_keep, back_low)

def matmul(left, right):
    return jnp.dot(left.astype(jnp.float32), right.astype(jnp.float32), precision=HIGHEST, preferred_element_type=jnp.float32)

def layer_norm(values, gain_row, shift_row):
    centred = values - lax.optimization_barrier(jnp.mean(values, -1, keepdims=True))
    spread = lax.optimization_barrier(jnp.mean(centred * centred, -1, keepdims=True))
    return centred * lax.rsqrt(spread + NORM_EPS) * gain_row + shift_row

def places(index, seq_lens):
    ends = jnp.cumsum(seq_lens).astype(jnp.int32)
    segment = lax.optimization_barrier(jnp.sum((index[:, None] >= ends[None, :]).astype(jnp.int32), 1)).astype(jnp.int32)
    starts = (ends - seq_lens).astype(jnp.int32)
    picked = segment[:, None] == jnp.arange(seq_lens.shape[0], dtype=jnp.int32)[None, :]
    offset = lax.optimization_barrier(jnp.sum(jnp.where(picked, starts[None, :], 0), 1)).astype(jnp.int32)
    return (segment, index - offset)

def rotate(heads_in, position):
    half = ROT // 2
    freq = 10000.0 ** (-2.0 * jnp.arange(half, dtype=jnp.float32) / ROT)
    angle = position.astype(jnp.float32)[:, None] * freq[None, :]
    cosine = jnp.cos(angle)[:, None, :]
    sine = jnp.sin(angle)[:, None, :]
    first_half = heads_in[..., :half]
    second_half = heads_in[..., half:ROT]
    return jnp.concatenate([first_half * cosine - second_half * sine, second_half * cosine + first_half * sine, heads_in[..., ROT:]], -1)

def attend(queries, keys, values, segment, index):
    rows = queries.shape[0]
    size = min(512, rows)
    count = rows // size

    def block(args):
        query_blk, seg_blk, idx_blk = args
        attention_scores = jnp.einsum('qhd,khd->hqk', query_blk, keys, precision=HIGHEST) * HEAD_DIM ** (-0.5)
        allowed = (seg_blk[:, None] == segment[None, :]) & (index[None, :] <= idx_blk[:, None])
        attention_scores = jnp.where(allowed[None], attention_scores, MASKED)
        highest = lax.optimization_barrier(jnp.max(attention_scores, -1, keepdims=True))
        weights = jnp.where(allowed[None], jnp.exp(attention_scores - highest), 0.0)
        totals = lax.optimization_barrier(jnp.sum(weights, -1))
        mixed = jnp.einsum('hqk,khd->hqd', low(weights), values, precision=HIGHEST)
        return jnp.transpose(mixed / totals[..., None], (1, 0, 2))
    out = lax.map(block, (queries.reshape(count, size, HEADS, HEAD_DIM), segment.reshape(count, size), index.reshape(count, size)))
    return out.reshape(rows, D)

def frozen_layer(ids, seq_lens, table_in, w_qkv, w_out, w_up, w_down, bias_all, gains, shifts):
    rows = ids.shape[0]
    embedded = jnp.take(table_in, ids, axis=0)
    index = jnp.arange(rows, dtype=jnp.int32)
    segment, position = places(index, seq_lens)
    attn_in = low(layer_norm(embedded, gains[0], shifts[0]))
    mlp_in = low(layer_norm(embedded, gains[1], shifts[1]))
    projected = matmul(attn_in, w_qkv) + bias_all[:3 * D]
    queries = low(rotate(projected[:, :D].reshape(rows, HEADS, HEAD_DIM), position))
    keys = low(rotate(projected[:, D:2 * D].reshape(rows, HEADS, HEAD_DIM), position))
    values = low(projected[:, 2 * D:].reshape(rows, HEADS, HEAD_DIM))
    mixed = low(attend(queries, keys, values, segment, index))
    attn_out = matmul(mixed, w_out) + bias_all[3 * D:4 * D]
    activ = low(jax.nn.gelu(matmul(mlp_in, w_up) + bias_all[4 * D:4 * D + FF], approximate=False))
    layer_out = embedded + attn_out + (matmul(activ, w_down) + bias_all[4 * D + FF:])
    return (embedded, layer_out)

def block_loss(normed_blk, counted_blk, table):
    logits = jnp.einsum('kbd,vd->kbv', normed_blk, table, precision=HIGHEST)
    target = logits[0] - jax.nn.logsumexp(logits[0], -1, keepdims=True)
    probe_logits = low_back(logits[1:])
    probes = probe_logits - jax.nn.logsumexp(probe_logits, -1, keepdims=True)
    diverge = lax.optimization_barrier(jnp.sum(jnp.exp(target)[None] * (target[None] - probes), -1))
    return jnp.sum(counted_blk[None] * diverge)

def group_loss_value(matrices, biases, embedded, layer_out, counted, table, gain_row, shift_row):
    normed = [low(layer_norm(layer_out, gain_row, shift_row))]
    sources = (embedded, layer_out)
    for which in range(2):
        product = low_back(matmul(low(sources[which]), low(matrices[which])))
        lensed = sources[which] + product + biases[which]
        normed.append(low(layer_norm(lensed, gain_row, shift_row)))
    stacked = jnp.stack(normed)
    rows = embedded.shape[0]
    size = min(512, rows)
    count = rows // size
    blocks = stacked.reshape(3, count, size, D).transpose(1, 0, 2, 3)

    def one_block(args):
        return block_loss(args[0], args[1], table)
    parts = lax.map(jax.checkpoint(one_block), (blocks, counted.reshape(count, size)))
    return jnp.sum(parts)

def orthonormal(columns):
    gram = matmul(columns.T, columns)
    factor = jnp.linalg.cholesky(gram)
    return lax.linalg.triangular_solve(factor, columns, left_side=False, lower=True, transpose_a=True)

def soap(weight, grad, first, second, left, right, lbase, rbase):
    rotated = matmul(matmul(lbase.T, grad), rbase)
    first_new = BETA_ONE * first + (1.0 - BETA_ONE) * grad
    second_new = BETA_TWO * second + (1.0 - BETA_TWO) * rotated * rotated
    moment_rot = matmul(matmul(lbase.T, first_new), rbase)
    scaled = moment_rot / (1.0 - BETA_ONE ** STEP) / (jnp.sqrt(second_new / (1.0 - BETA_TWO ** STEP)) + ADAM_EPS)
    update = matmul(matmul(lbase, scaled), rbase.T)
    weight_new = weight - MATRIX_RATE * (update + DECAY * weight)
    left_new = BETA_STAT * left + (1.0 - BETA_STAT) * matmul(grad, grad.T)
    right_new = BETA_STAT * right + (1.0 - BETA_STAT) * matmul(grad.T, grad)
    return (weight_new, first_new, second_new, left_new, right_new, orthonormal(matmul(left_new, lbase)), orthonormal(matmul(right_new, rbase)))

def adam_bias(bias, grad, first, second):
    first_new = BETA_ONE * first + (1.0 - BETA_ONE) * grad
    second_new = BETA_TWO * second + (1.0 - BETA_TWO) * grad * grad
    scaled = first_new / (1.0 - BETA_ONE ** STEP) / (jnp.sqrt(second_new / (1.0 - BETA_TWO ** STEP)) + ADAM_EPS)
    return (bias - BIAS_RATE * scaled, first_new, second_new)

def reference(tokens, loss_position_mask, lengths, owners, embed_in, unembedding_table, frozen_qkv, frozen_out, frozen_up, frozen_down, frozen_bias, norm_gain, norm_shift, master_matrix, lens_bias, matrix_first, matrix_second, left_stat, right_stat, left_basis, right_basis, bias_first, bias_second):
    table_in = embed_in.astype(jnp.float32)
    table_out = unembedding_table.astype(jnp.float32)
    w_qkv = frozen_qkv.astype(jnp.float32)
    w_out = frozen_out.astype(jnp.float32)
    w_up = frozen_up.astype(jnp.float32)
    w_down = frozen_down.astype(jnp.float32)
    group = tokens.shape[0] // N_ROWS
    counted = loss_position_mask.astype(jnp.float32)
    sources_in = []
    sources_out = []
    for which in range(N_ROWS):
        embedded, layer_out = frozen_layer(tokens[which * group:(which + 1) * group], lengths[which], table_in, w_qkv, w_out, w_up, w_down, frozen_bias, norm_gain, norm_shift)
        sources_in.append(embedded)
        sources_out.append(layer_out)
    nblk = D // BS
    order = jnp.argsort(owners).astype(jnp.int32)
    matrices = jnp.take(master_matrix, order, axis=0).reshape(2, nblk, nblk, BS, BS).transpose(0, 1, 3, 2, 4).reshape(2, D, D)

    def overall_loss(mats, biases):
        total = jnp.zeros((), jnp.float32)
        for which in range(N_ROWS):
            total = total + group_loss_value(mats, biases, sources_in[which], sources_out[which], counted[which * group:(which + 1) * group], table_out, norm_gain[2], norm_shift[2])
        return total
    loss_sum, pull = jax.vjp(overall_loss, matrices, lens_bias)
    grad_matrix, grad_bias = pull(jnp.ones((), jnp.float32))
    loss_count = jnp.sum(counted)
    blocks = grad_matrix.reshape(2, nblk, BS, nblk, BS).transpose(0, 1, 3, 2, 4).reshape(BLOCKS, BS, BS)
    slot_grad = jnp.take(blocks, owners, axis=0)
    new_matrix, new_first, new_second, new_left, new_right, renewed_left_basis, new_rbasis = jax.vmap(soap)(master_matrix, slot_grad, matrix_first, matrix_second, left_stat, right_stat, left_basis, right_basis)
    new_bias, new_bias_first, new_bias_second = adam_bias(lens_bias, grad_bias, bias_first, bias_second)
    return (loss_sum, loss_count, new_matrix, new_first, new_second, new_left, new_right, renewed_left_basis, new_rbasis, new_bias, new_bias_first, new_bias_second)
```

```python
import functools

import jax
import jax.numpy as jnp
import numpy as np
from jax import lax
from jax.experimental import pallas as pl
from jax.experimental.pallas import tpu as pltpu
from jax.sharding import PartitionSpec as P

HEADS = 16
HEAD_DIM = 64
ROT = 16
BS = 256
STEP = 5

HIGHEST = lax.Precision.HIGHEST
NORM_EPS = 1e-05
BETA_ONE = 0.9
BETA_TWO = 0.999
BETA_STAT = 0.95
ADAM_EPS = 1e-08
MATRIX_RATE = 0.01
BIAS_RATE = 0.1
DECAY = 0.1
MASKED = -1e30
NB = 64
PIV = 2
VMEM_LIMIT = 56 * 2**20


def _mm(a,b,dims):
    return lax.dot_general(a,b,(dims,((),())),precision=HIGHEST,preferred_element_type=jnp.float32)
def mm_nn(a,b): return _mm(a,b,((1,),(0,)))
def mm_tn(a,b): return _mm(a,b,((0,),(0,)))
def mm_nt(a,b): return _mm(a,b,((1,),(1,)))
def _mb(a,b,dims):
    return lax.dot_general(a.astype(jnp.bfloat16),b.astype(jnp.bfloat16),(dims,((),())),preferred_element_type=jnp.float32)

def eliminate(rows, nb):
    rows=list(rows)
    def pick(i,c):
        return jnp.broadcast_to(rows[i][:,c:c+1],rows[i].shape)
    for j in range(0,nb,PIV):
        low=[[None]*PIV for _ in range(PIV)]
        roots=[None]*PIV
        inv=[[None]*PIV for _ in range(PIV)]
        cur=[[pick(j+p,j+q) if q<=p else None for q in range(PIV)] for p in range(PIV)]
        for q in range(PIV):
            guess=lax.rsqrt(cur[q][q])
            roots[q]=guess*(1.5-0.5*(cur[q][q]*guess)*guess)
            for p in range(q+1,PIV):
                low[p][q]=cur[p][q]*roots[q]
            for p in range(q+1,PIV):
                for t in range(q+1,p+1):
                    cur[p][t]=cur[p][t]-low[p][q]*low[t][q]
        lead=[]
        for p in range(PIV):
            acc=rows[j+p]
            for q in range(p):
                acc=acc-low[p][q]*lead[q]
            lead.append(acc*roots[p])
        back=[None]*PIV
        for p in reversed(range(PIV)):
            acc=lead[p]
            for q in range(p+1,PIV):
                acc=acc-low[q][p]*back[q]
            back[p]=acc*roots[p]
        for i in range(j+PIV,nb):
            cols=[pick(i,j+p) for p in range(PIV)]
            t=cols[0]*back[0]
            for p in range(1,PIV):
                t=t+cols[p]*back[p]
            rows[i]=rows[i]-t
        for p in range(PIV):
            rows[j+p]=lead[p]
    return rows

def soap_kernel(per, where_ref, w_ref,g_ref,first_ref,second_ref,left_ref,right_ref,lb_ref,rb_ref,
                nw_ref,nf_ref,ns_ref,nl_ref,nr_ref,ql_ref,qr_ref,work,prods,stage):
    xor=where_ref[0]
    nm=2*per
    nn=((1,),(0,)); tn=((0,),(0,)); nt=((1,),(1,))
    def slot(s,c):
        g=g_ref[s^xor].astype(jnp.float32)
        gb=g.astype(jnp.bfloat16)
        lb=lb_ref[s]; rb=rb_ref[s]
        lbb=lb.astype(jnp.bfloat16); rbb=rb.astype(jnp.bfloat16)
        rotated=_mb(_mb(lbb,gb,tn),rbb,nn)
        first=BETA_ONE*first_ref[s]+(1.0-BETA_ONE)*g
        second=BETA_TWO*second_ref[s]+(1.0-BETA_TWO)*rotated*rotated
        nf_ref[s]=first; ns_ref[s]=second
        moment=_mb(_mb(lbb,first,tn),rbb,nn)
        scaled=moment/(1.0-BETA_ONE**STEP)/(jnp.sqrt(second/(1.0-BETA_TWO**STEP))+ADAM_EPS)
        update=_mb(_mb(lbb,scaled,nn),rbb,nt)
        w=w_ref[s]
        nw_ref[s]=w-MATRIX_RATE*(update+DECAY*w)
        nl=BETA_STAT*left_ref[s]+(1.0-BETA_STAT)*_mb(gb,gb,nt)
        nr=BETA_STAT*right_ref[s]+(1.0-BETA_STAT)*_mb(gb,gb,tn)
        nl_ref[s]=nl; nr_ref[s]=nr
        pl_=mm_nn(nl,lb); pr_=mm_nn(nr,rb)
        prods[s]=pl_; prods[per+s]=pr_
        work[s]=mm_tn(pl_,pl_); work[per+s]=mm_tn(pr_,pr_)
        return c
    lax.fori_loop(0,per,slot,0,unroll=True)
    lane=lax.broadcasted_iota(jnp.int32,(NB,128),1)
    row=lax.broadcasted_iota(jnp.int32,(NB,128),0)
    ident=(lane==row+NB).astype(jnp.float32)
    idrow=lax.broadcasted_iota(jnp.int32,(NB,BS),0)
    col=lax.broadcasted_iota(jnp.int32,(NB,BS),1)
    colw=lax.broadcasted_iota(jnp.int32,(BS,BS),1)
    upper=lax.broadcasted_iota(jnp.int32,(NB,NB),0)<=lax.broadcasted_iota(jnp.int32,(NB,NB),1)
    def fill(k):
        r0=k*NB
        for m in range(nm):
            d=work[m,r0:r0+NB,r0//128*128:r0//128*128+128]
            if r0%128: d=pltpu.roll(d,128-r0%128,axis=1)
            stage[m*NB:(m+1)*NB,:]=jnp.where(lane<NB,d,ident)
    def trail(k):
        r0=k*NB
        end=r0+NB
        lo=end//128*128
        inside=(col>=r0)&(col<end)
        ms=range(nm)
        linv=[stage[m*NB:(m+1)*NB,NB:2*NB] for m in ms]
        rows_m=[jnp.where(inside,(col==idrow+r0).astype(jnp.float32),work[m,r0:end,:]) for m in ms]
        b=[mm_nn(linv[m],rows_m[m]) for m in ms]
        if end<BS:
            up=[jnp.where(upper,stage[m*NB:(m+1)*NB,:NB],0.0) for m in ms]
            left=[rows_m[m][:,lo:]-mm_tn(up[m],b[m][:,lo:]) for m in ms]
            fix=[b[m][:,lo:]+mm_nn(linv[m],left[m]) for m in ms]
            b=[fix[m] if lo==0 else jnp.concatenate([b[m][:,:lo],fix[m]],1) for m in ms]
            cw=colw[:BS-end]
            rest=[mm_tn(b[m][:,lo:],b[m])[end-lo:] for m in ms]
            for m in ms:
                work[m,end:,:]=jnp.where((cw>=r0)&(cw<end),0.0,work[m,end:,:])-rest[m]
        for m in ms:
            work[m,r0:end,:]=b[m]
    def step(kb,c):
        for k in range(BS//NB):
            @pl.when(kb==k)
            def _(k=k):
                fill(k)
        rows=[stage[pl.ds(i,nm,stride=NB),:] for i in range(NB)]
        rows=eliminate(rows,NB)
        for i in range(NB):
            stage[pl.ds(i,nm,stride=NB),:]=rows[i]
        for k in range(BS//NB):
            @pl.when(kb==k)
            def _(k=k):
                trail(k)
        return c
    lax.fori_loop(0,BS//NB,step,0)
    lower=lax.broadcasted_iota(jnp.int32,(BS,BS),0)>=colw
    for s in range(per):
        ql_ref[s]=mm_nt(prods[s],jnp.where(lower,work[s],0.0))
        qr_ref[s]=mm_nt(prods[per+s],jnp.where(lower,work[per+s],0.0))

def soap_call(xor,w,g,first,second,left,right,lb,rb):
    per=w.shape[0]
    sh=jax.ShapeDtypeStruct((per,BS,BS),jnp.float32)
    vm=pl.BlockSpec(memory_space=pltpu.VMEM)
    return pl.pallas_call(functools.partial(soap_kernel,per),
        out_shape=[sh]*7,
        in_specs=[pl.BlockSpec(memory_space=pltpu.SMEM)]+[vm]*8, out_specs=[vm]*7,
        scratch_shapes=[pltpu.VMEM((2*per,BS,BS),jnp.float32),pltpu.VMEM((2*per,BS,BS),jnp.float32),pltpu.VMEM((2*per*NB,128),jnp.float32)],
        compiler_params=pltpu.CompilerParams(vmem_limit_bytes=48*2**20),
        name="soap_update")(xor,w,g,first,second,left,right,lb,rb)


def adam_bias(bias, grad, first, second):
    first_new = BETA_ONE * first + (1.0 - BETA_ONE) * grad
    second_new = BETA_TWO * second + (1.0 - BETA_TWO) * grad * grad
    scaled = (
        first_new
        / (1.0 - BETA_ONE**STEP)
        / (jnp.sqrt(second_new / (1.0 - BETA_TWO**STEP)) + ADAM_EPS)
    )
    return (bias - BIAS_RATE * scaled, first_new, second_new)


def places(index, seq_lens):
    ends = jnp.cumsum(seq_lens)
    segment = jnp.sum((index[:, None] >= ends[None, :]).astype(jnp.int32), 1)
    starts = ends - seq_lens
    picked = segment[:, None] == jnp.arange(seq_lens.shape[0], dtype=jnp.int32)[None, :]
    offset = jnp.sum(jnp.where(picked, starts[None, :], 0), 1)
    return (segment, index - offset)


def swap(x, axis, bit):
    size = lax.axis_size(axis)
    return lax.ppermute(x, axis, [(i, i ^ bit) for i in range(size)])


def gather_xor(x, axis, bits):
    out = x[None]
    for bit in bits:
        out = jnp.concatenate([out, swap(out, axis, bit)], 0)
    return out


def bits_of(size):
    return [1 << i for i in range(size.bit_length() - 1)]


def chip_bits(size):
    return bits_of(size)[1:][::-1] + [1]


def entry_ids(bits):
    ids = [0]
    for bit in bits:
        ids = ids + [i ^ bit for i in ids]
    return ids


def normalize(x, gain, shift):
    centred = x - jnp.mean(x, -1, keepdims=True)
    root = lax.rsqrt(jnp.mean(centred * centred, -1, keepdims=True) + NORM_EPS)
    return centred * root * gain + shift


def layer_kernel(
    chunks, where_ref, emb, cosines, sines, key_meta, query_meta, bias, gain, shift,
    qkv, w_out, w_up, w_down, out, w_qkv, wo, up, down, k_all, v_all, q_own, mix, sems,
):
    group, width = emb.shape
    own = out.shape[0]
    units = w_up.shape[1]
    part = units // chunks
    nbuf = up.shape[0]

    def load_up(j):
        return (
            pltpu.make_async_copy(
                w_up.at[:, j * part : (j + 1) * part], up.at[j % nbuf], sems.at[4 + j % nbuf]
            ),
            pltpu.make_async_copy(
                w_down.at[j * part : (j + 1) * part, :],
                down.at[j % nbuf],
                sems.at[4 + nbuf + j % nbuf],
            ),
        )

    loads = [
        pltpu.make_async_copy(
            qkv.at[:, i * width : (i + 1) * width], w_qkv.at[i], sems.at[i]
        )
        for i in range(3)
    ]
    load_out = pltpu.make_async_copy(w_out, wo, sems.at[3])
    for i in (1, 2, 0):
        loads[i].start()
    load_out.start()
    for j in range(nbuf):
        for copy in load_up(j):
            copy.start()

    lane = lax.broadcasted_iota(jnp.int32, (1, width), 1)
    first_half = lane % HEAD_DIM < ROT // 2

    def rotated(x, cos, sin):
        turned = jnp.where(
            first_half,
            pltpu.roll(x, width - ROT // 2, axis=1),
            pltpu.roll(x, ROT // 2, axis=1),
        )
        reps = width // cos.shape[1]
        return x * jnp.concatenate([cos] * reps, 1) + turned * jnp.concatenate([sin] * reps, 1)

    def attn_in(x):
        return normalize(x.astype(jnp.float32), gain[0:1, :], shift[0:1, :]).astype(jnp.bfloat16)

    loads[1].wait()
    loads[2].wait()
    rows = 256

    def project(i, c):
        at = pl.ds(pl.multiple_of(i * rows, rows), rows)
        x = attn_in(emb[at, :])
        k = jnp.dot(x, w_qkv[1], preferred_element_type=jnp.float32) + bias[:, width : 2 * width]
        k_all[at, :] = rotated(k, cosines[at, :], sines[at, :]).astype(jnp.bfloat16)
        v = jnp.dot(x, w_qkv[2], preferred_element_type=jnp.float32)
        v_all[at, :] = (v + bias[:, 2 * width : 3 * width]).astype(jnp.bfloat16)
        return c

    lax.fori_loop(0, group // rows, project, 0)
    mine = pl.ds(pl.multiple_of(where_ref[0] * own, own), own)
    x_own = emb[mine, :].astype(jnp.float32)
    loads[0].wait()
    q = jnp.dot(attn_in(x_own), w_qkv[0], preferred_element_type=jnp.float32) + bias[:, :width]
    q_own[...] = rotated(q, cosines[mine, :], sines[mine, :]).astype(jnp.bfloat16)

    allowed = (query_meta[:, 0:1] == key_meta[0:1, :]) & (key_meta[1:2, :] <= query_meta[:, 1:2])
    half = lax.broadcasted_iota(jnp.int32, (1, 2 * HEAD_DIM), 1) // HEAD_DIM

    def pair(hp, c):
        at = pl.ds(pl.multiple_of(hp * 2 * HEAD_DIM, 2 * HEAD_DIM), 2 * HEAD_DIM)
        qp, kp, vp = q_own[:, at], k_all[:, at], v_all[:, at]
        outs = []
        for h in range(2):
            qh = jnp.where(half == h, qp, jnp.zeros((), jnp.bfloat16))
            scores = lax.dot_general(
                qh, kp, (((1,), (1,)), ((), ())), preferred_element_type=jnp.float32
            )
            scores = jnp.where(allowed, scores * HEAD_DIM ** (-0.5), MASKED)
            weights = jnp.exp(scores - jnp.max(scores, -1, keepdims=True))
            total = jnp.sum(weights, -1, keepdims=True)
            got = jnp.dot(weights.astype(jnp.bfloat16), vp, preferred_element_type=jnp.float32)
            outs.append(got / total)
        mix[:, at] = jnp.where(half == 0, outs[0], outs[1]).astype(jnp.bfloat16)
        return c

    lax.fori_loop(0, HEADS // 2, pair, 0)
    load_out.wait()
    total = x_own + (
        jnp.dot(mix[...], wo[...], preferred_element_type=jnp.float32)
        + bias[:, 3 * width : 4 * width]
    )
    mlp_in = normalize(x_own, gain[1:2, :], shift[1:2, :]).astype(jnp.bfloat16)
    acc = jnp.zeros((own, width), jnp.float32)
    for j in range(chunks):
        for copy in load_up(j):
            copy.wait()
        lo = 4 * width + j * part
        pre = jnp.dot(mlp_in, up[j % nbuf], preferred_element_type=jnp.float32)
        pre = pre + bias[:, lo : lo + part]
        activ = (0.5 * pre * (1.0 + lax.erf(pre * 0.7071067811865476))).astype(jnp.bfloat16)
        acc = acc + jnp.dot(activ, down[j % nbuf], preferred_element_type=jnp.float32)
        if j + nbuf < chunks:
            for copy in load_up(j + nbuf):
                copy.start()
    total = total + (acc + bias[:, 4 * width + units :])
    out[:, :width] = x_own.astype(jnp.bfloat16)
    out[:, width:] = total.astype(jnp.bfloat16)


def layer_call(where, emb, cosines, sines, key_meta, query_meta, bias, gain, shift, qkv, w_out, w_up, w_down):
    group, width = emb.shape
    own = query_meta.shape[0]
    units = w_up.shape[1]
    chunks = units // width
    nbuf = chunks if group <= 1024 else 2
    vm = pl.BlockSpec(memory_space=pltpu.VMEM)
    hbm = pl.BlockSpec(memory_space=pl.ANY)
    bf = jnp.bfloat16
    return pl.pallas_call(
        functools.partial(layer_kernel, chunks),
        out_shape=jax.ShapeDtypeStruct((own, 2 * width), bf),
        in_specs=[pl.BlockSpec(memory_space=pltpu.SMEM)] + [vm] * 8 + [hbm] * 4,
        out_specs=vm,
        scratch_shapes=[
            pltpu.VMEM((3, width, width), bf),
            pltpu.VMEM((width, width), bf),
            pltpu.VMEM((nbuf, width, units // chunks), bf),
            pltpu.VMEM((nbuf, units // chunks, width), bf),
            pltpu.VMEM((group, width), bf),
            pltpu.VMEM((group, width), bf),
            pltpu.VMEM((own, width), bf),
            pltpu.VMEM((own, width), bf),
            pltpu.SemaphoreType.DMA((4 + 2 * nbuf,)),
        ],
        compiler_params=pltpu.CompilerParams(vmem_limit_bytes=VMEM_LIMIT),
        name="frozen_layer",
    )(where, emb, cosines, sines, key_meta, query_meta, bias, gain, shift, qkv, w_out, w_up, w_down)


def probe_kernel(
    limit, loc_ref, x, slots, bias, gain, shift, table,
    sums, stats, hats, normed, peak, mass, cross,
):
    step = pl.program_id(0)
    steps = pl.num_programs(0)
    count, width = x.shape[0], x.shape[1] // 2
    tile = table.shape[0]
    nblk = width // BS

    @pl.when(step == 0)
    def _():
        def save(i, v):
            centred = v - jnp.mean(v, -1, keepdims=True)
            root = lax.rsqrt(jnp.mean(centred * centred, -1, keepdims=True) + NORM_EPS)
            hat = centred * root
            normed[i * count : (i + 1) * count, :] = (hat * gain[2:3, :] + shift[2:3, :]).astype(
                jnp.bfloat16
            )
            return hat, root

        save(0, x[:, width:].astype(jnp.float32))
        for k in range(2):
            cols = []
            for j in range(nblk):
                total = None
                for i in range(nblk):
                    lo = k * width + i * BS
                    term = jnp.dot(
                        x[:, lo : lo + BS],
                        slots[loc_ref[(k * nblk + i) * nblk + j]],
                        preferred_element_type=jnp.float32,
                    )
                    total = term if total is None else total + term
                cols.append(total)
            v = x[:, k * width : (k + 1) * width].astype(jnp.float32)
            hat, root = save(k + 1, v + jnp.concatenate(cols, 1) + bias[k : k + 1, :])
            hats[k, :, :width] = hat
            hats[k, :, width:] = jnp.broadcast_to(root, (count, 128))
        peak[...] = jnp.full(peak.shape, MASKED, jnp.float32)
        mass[...] = jnp.zeros(mass.shape, jnp.float32)
        cross[...] = jnp.zeros(cross.shape, jnp.float32)
        sums[...] = jnp.zeros(sums.shape, jnp.float32)

    def visit(last):
        w = table[...]
        logits = lax.dot_general(
            normed[...], w, (((1,), (1,)), ((), ())), preferred_element_type=jnp.float32
        )
        if last:
            left = limit - step * tile
            at = lax.broadcasted_iota(jnp.int32, (1, tile), 1)
            logits = jnp.where(at < left, logits, MASKED)
            down = lax.broadcasted_iota(jnp.int32, (tile, 1), 0)
            w = jnp.where(down < left, w, jnp.zeros((), jnp.bfloat16))
        old = peak[...]
        new = jnp.maximum(old, jnp.max(logits, -1, keepdims=True))
        fade = jnp.exp(old - new)
        powers = jnp.exp(logits - new)
        peak[...] = new
        mass[...] = mass[...] * fade + jnp.sum(powers, -1, keepdims=True)
        base, base_fade = powers[:count], fade[:count]
        for k in range(2):
            gap = logits[:count] - logits[(k + 1) * count : (k + 2) * count]
            at = pl.ds(k * count, count)
            cross[at, :] = cross[at, :] * base_fade + jnp.sum(base * gap, -1, keepdims=True)
        sums[...] = sums[...] * fade + jnp.dot(
            powers.astype(jnp.bfloat16), w, preferred_element_type=jnp.float32
        )

    @pl.when(step < steps - 1)
    def _():
        visit(False)

    @pl.when(step == steps - 1)
    def _():
        visit(True)
        at = lax.broadcasted_iota(jnp.int32, (count, 128), 1)
        packed = jnp.zeros((count, 128), jnp.float32)
        for j in range(3):
            packed = jnp.where(at == j, peak[j * count : (j + 1) * count, :], packed)
            packed = jnp.where(at == 3 + j, mass[j * count : (j + 1) * count, :], packed)
        for k in range(2):
            packed = jnp.where(at == 6 + k, cross[k * count : (k + 1) * count, :], packed)
        stats[...] = jnp.transpose(packed)[:8, :]


def probe_call(loc, x, slots, bias, gain, shift, table):
    count, width = x.shape[0], x.shape[1] // 2
    vocab = table.shape[0]
    tile = 640
    steps = -(-vocab // tile)
    f32 = jnp.float32
    vm = pl.BlockSpec(memory_space=pltpu.VMEM)
    return pl.pallas_call(
        functools.partial(probe_kernel, vocab),
        grid=(steps,),
        out_shape=[
            jax.ShapeDtypeStruct((3 * count, width), f32),
            jax.ShapeDtypeStruct((8, count), f32),
            jax.ShapeDtypeStruct((2, count, width + 128), f32),
        ],
        in_specs=[pl.BlockSpec(memory_space=pltpu.SMEM)]
        + [vm] * 5
        + [pl.BlockSpec((tile, width), lambda i: (i, 0))],
        out_specs=[vm, vm, vm],
        scratch_shapes=[
            pltpu.VMEM((3 * count, width), jnp.bfloat16),
            pltpu.VMEM((3 * count, 1), f32),
            pltpu.VMEM((3 * count, 1), f32),
            pltpu.VMEM((2 * count, 1), f32),
        ],
        compiler_params=pltpu.CompilerParams(vmem_limit_bytes=VMEM_LIMIT),
        name="probe_pass",
    )(loc, x, slots, bias, gain, shift, table)


def grad_kernel(dest_ref, x, sums, scale, hats, gain, grads, bias_grad):
    count, width = x.shape[0], x.shape[1] // 2
    nblk = width // BS
    pieces = dest_ref.shape[1]
    rows = BS // pieces
    cols = jnp.transpose(jnp.concatenate([scale[...]] * (128 // scale.shape[0]), 0))
    base = sums[:count, :] * cols[:, 0:1]
    for k in range(2):
        e = (sums[(k + 1) * count : (k + 2) * count, :] * cols[:, k + 1 : k + 2] - base) * gain[2:3, :]
        hat = hats[k, :, :width]
        root = hats[k, :, width : width + 1]
        pulled = e - jnp.mean(e, -1, keepdims=True)
        pulled = (pulled - hat * jnp.mean(e * hat, -1, keepdims=True)) * root
        bias_grad[k : k + 1, :] = jnp.sum(pulled, 0, keepdims=True)
        low = pulled.astype(jnp.bfloat16)
        for i in range(nblk):
            lo = k * width + i * BS
            full = lax.dot_general(
                x[:, lo : lo + BS], low, (((0,), (0,)), ((), ())), preferred_element_type=jnp.float32
            ).astype(jnp.bfloat16)
            for j in range(nblk):
                b = (k * nblk + i) * nblk + j
                for p in range(pieces):
                    grads[dest_ref[b, p]] = full[p * rows : (p + 1) * rows, j * BS : (j + 1) * BS]


def grad_call(dest, x, sums, scale, hats, gain):
    width = x.shape[1] // 2
    pieces = dest.shape[1]
    vm = pl.BlockSpec(memory_space=pltpu.VMEM)
    return pl.pallas_call(
        grad_kernel,
        out_shape=[
            jax.ShapeDtypeStruct((dest.shape[0] * pieces, BS // pieces, BS), jnp.bfloat16),
            jax.ShapeDtypeStruct((2, width), jnp.float32),
        ],
        in_specs=[pl.BlockSpec(memory_space=pltpu.SMEM)] + [vm] * 5,
        out_specs=[vm, vm],
        compiler_params=pltpu.CompilerParams(vmem_limit_bytes=VMEM_LIMIT),
        name="lens_gradient",
    )(dest, x, sums, scale, hats, gain)


def merge(a, b):
    peak = jnp.maximum(a[:3], b[:3])
    fa, fb = jnp.exp(a[:3] - peak), jnp.exp(b[:3] - peak)
    return jnp.concatenate(
        [peak, a[3:6] * fa + b[3:6] * fb, a[6:8] * fa[:1] + b[6:8] * fb[:1]], 0
    )


def halve(x, axis, bit):
    return (x[0].astype(jnp.float32) + swap(x[1], axis, bit).astype(jnp.float32)).astype(x[0].dtype)


def body(
    tokens, loss_position_mask, lengths, owners, embed_in, unembedding_table, frozen_qkv, frozen_out,
    frozen_up, frozen_down, frozen_bias, norm_gain, norm_shift, master_matrix, lens_bias, matrix_first,
    matrix_second, left_stat, right_stat, left_basis, right_basis, bias_first, bias_second,
):
    bf, f32, i32 = jnp.bfloat16, jnp.float32, jnp.int32
    shards, rows = lax.axis_size("vocab"), lax.axis_size("rows")
    where, row = lax.axis_index("vocab"), lax.axis_index("rows")
    group, width = tokens.shape[0], embed_in.shape[1]
    own = group // shards
    nblk = width // BS
    per = master_matrix.shape[0]
    blocks = shards * per
    chips = shards // 2
    vbits, rbits = chip_bits(shards), bits_of(rows)
    entries = np.array(entry_ids(vbits), np.int32)
    entry_at = jnp.array(np.argsort(entries), i32)
    every = jnp.arange(shards, dtype=i32)

    slots = lax.all_gather(master_matrix.astype(bf), "vocab", axis=0, tiled=True)
    biases = gather_xor(lens_bias, "vocab", vbits)
    biases = jnp.take(biases, jnp.take(entry_at, where ^ every), axis=0)
    biases = biases.transpose(1, 0, 2).reshape(2, width)

    def by_class(a):
        return a.reshape(own, shards).T.reshape(-1)

    ids = by_class(tokens)
    index = by_class(jnp.arange(group, dtype=i32))
    mask = by_class(loss_position_mask)
    table_rows = embed_in.shape[0]
    owner = ids // table_rows
    local = ids - where * table_rows
    holds = (owner[:, None] == jnp.arange(shards, dtype=i32)[None, :]).astype(bf)
    before = (jnp.arange(group)[:, None] > jnp.arange(group)[None, :]).astype(bf)
    ahead = jnp.dot(before, holds, preferred_element_type=f32)
    rank = jnp.sum(ahead * holds.astype(f32), 1).astype(i32)
    most = jnp.max(jnp.sum(holds.astype(f32), 0)).astype(i32)
    shared = gather_xor(jnp.concatenate([mask, jnp.full((8,), most, i32)]), "rows", rbits)
    masks = shared[:, :group].reshape(rows, shards, own)
    most = jnp.max(shared[:, group:])

    take = 176 if group <= 1024 else 64
    chip, core = where // 2, where % 2
    apart = (chip - owner // 2) % chips + chips * ((owner % 2) ^ core)
    to_right = [(i, i + 2) for i in range(shards - 2)]
    to_left = [(i + 2, i) for i in range(shards - 2)]

    def fetch(k):
        slot = jnp.arange(take, dtype=i32)[:, None] + k * take
        hit = (owner == where)[None, :] & (rank[None, :] == slot)
        picked = jnp.sum(jnp.where(hit, local[None, :], 0), 1)
        mine = jnp.take(embed_in, picked, axis=0, mode="clip")
        right, left = [mine], [mine]
        for _ in range(1, chips):
            right.append(lax.ppermute(right[-1], "vocab", to_right))
            left.append(lax.ppermute(left[-1], "vocab", to_left))
        near = jnp.concatenate([mine] + [right[o] + left[chips - o] for o in range(1, chips)], 0)
        both = jnp.concatenate([near, swap(near, "vocab", 1)], 0)
        place = rank - k * take
        column = jnp.where((place >= 0) & (place < take), apart * take + place, -1)
        spread = (column[:, None] == jnp.arange(shards * take, dtype=i32)[None, :]).astype(bf)
        return jnp.dot(spread, both, preferred_element_type=f32).astype(bf)

    embedded = fetch(0)
    _, embedded = lax.while_loop(
        lambda c: c[0] * take < most, lambda c: (c[0] + 1, c[1] + fetch(c[0])), (jnp.int32(1), embedded)
    )

    seq_lens = lengths[0]
    segment, position = places(index, seq_lens)
    half = ROT // 2
    lane = jnp.arange(2 * HEAD_DIM) % HEAD_DIM
    freq = 10000.0 ** (-2.0 * (lane % half).astype(f32) / ROT)
    angle = position.astype(f32)[:, None] * freq[None, :]
    turns = (lane < ROT)[None, :]
    cosines = jnp.where(turns, jnp.cos(angle), 1.0)
    sines = jnp.where(turns, jnp.sin(angle) * jnp.where(lane < half, -1.0, 1.0)[None, :], 0.0)
    key_meta = jnp.concatenate([segment[None], index[None], jnp.zeros((6, group), i32)], 0)
    own_seg = lax.dynamic_slice_in_dim(segment, where * own, own)
    own_idx = lax.dynamic_slice_in_dim(index, where * own, own)
    query_meta = jnp.stack([own_seg, own_idx], 1)
    states = layer_call(
        where.reshape(1), embedded, cosines, sines, key_meta, query_meta, frozen_bias.reshape(1, -1),
        norm_gain, norm_shift, frozen_qkv, frozen_out, frozen_up, frozen_down,
    )

    take_rows = max(16, 384 // shards)
    count = take_rows * shards
    mine_masks = lax.dynamic_index_in_dim(masks, where, 1, keepdims=False)
    per_row = jnp.sum(mine_masks, 1)
    lower = (row ^ jnp.arange(rows)) < row
    base = jnp.sum(jnp.where(lower, per_row, 0))
    dealt = base + jnp.cumsum(mine_masks[0]) - mine_masks[0]
    per_class = jnp.sum(masks, (0, 2))
    per_entry = jnp.take(per_class, where ^ entries)
    share = (per_entry - row + rows - 1) // rows
    rounds = -(-jnp.max((per_class + rows - 1) // rows) // take_rows)

    numbers = jnp.arange(blocks, dtype=i32)
    pieces = max(1, rows // per)
    span = per * pieces // rows
    slot_of = jnp.sum(jnp.where(owners[None, :] == numbers[:, None], numbers[None, :], 0), 1)
    device, inner = slot_of // per, slot_of % per
    piece = inner[:, None] * pieces + jnp.arange(pieces, dtype=i32)[None, :]
    part = (piece // span) ^ row
    dest = (jnp.take(entry_at, device ^ where)[:, None] * rows + part) * span + piece % span

    def deal(k):
        target = jnp.arange(rows, dtype=i32) ^ row
        place = jnp.arange(take_rows, dtype=i32) + k * take_rows
        wanted = (place[None, :] * rows + target[:, None]).reshape(-1)
        pick = ((dealt[None, :] == wanted[:, None]) & (mine_masks[0] > 0)[None, :]).astype(bf)
        sent = jnp.dot(pick, states, preferred_element_type=f32).astype(bf)
        sent = sent.reshape(rows, take_rows, 2 * width)
        got = sent[0]
        for e in range(1, rows):
            got = got + swap(sent[e], "rows", e)
        return gather_xor(got, "vocab", vbits).reshape(count, 2 * width)

    def pass_over(k):
        x = deal(k)
        sums, local_stats, hats = probe_call(slot_of, x, slots, biases, norm_gain, norm_shift, unembedding_table)
        stats = local_stats
        for at, bit in enumerate(vbits):
            theirs = swap(stats, "vocab", bit)
            axes = [2] * len(vbits)
            flipped = jnp.flip(theirs.reshape([8] + axes + [take_rows]), len(vbits) - at)
            stats = merge(stats, flipped.reshape(8, count))
        valid = (jnp.arange(take_rows, dtype=i32)[None, :] + k * take_rows < share[:, None]).reshape(-1)
        valid = valid.astype(f32)
        logtot = stats[:3] + jnp.log(stats[3:6])
        diverge = stats[6:8] / stats[3:4] - logtot[:1] + logtot[1:]
        loss = jnp.sum(valid[None, :] * diverge)
        scale = valid[None, :] * jnp.exp(local_stats[:3] - stats[:3]) / stats[3:6]
        scale = jnp.concatenate([scale, jnp.zeros((5, count), f32)], 0)
        grads, bias_grad = grad_call(dest, x, sums, scale, hats, norm_gain)
        return grads, bias_grad, loss

    grads, bias_grad, loss = pass_over(jnp.int32(0))

    def again(c):
        g, b, s = pass_over(c[0])
        return (c[0] + 1, c[1] + g, c[2] + b, c[3] + s)

    _, grads, bias_grad, loss = lax.while_loop(
        lambda c: c[0] < rounds, again, (jnp.int32(1), grads, bias_grad, loss)
    )
    loss_count = jnp.sum(masks).astype(f32)

    small = jnp.concatenate([bias_grad, jnp.full((1, width), jnp.where(where == 0, loss, 0.0))], 0)
    for axis, bits in (("rows", rbits), ("vocab", vbits)):
        for bit in bits:
            small = small + swap(small, axis, bit)
    loss_sum = small[2, 0]
    bias_grad = small[:2]
    bias_cols = lens_bias.shape[1]
    bias_grad = lax.dynamic_slice_in_dim(bias_grad, where * bias_cols, bias_cols, 1)

    g = grads.reshape(2, chips, rows, -1, BS)
    g = halve(g, "vocab", 1)
    cut = [g[..., : BS // 2], g[..., BS // 2 :]]
    for side, bits in enumerate((rbits[::-1], rbits)):
        h = cut[side]
        live = list(range(rows))
        for bit in bits:
            stay = [e for e in live if not e & bit]
            go = [live.index(e | bit) for e in stay]
            keep = [live.index(e) for e in stay]
            h = halve((jnp.stack([h[:, e] for e in keep], 1), jnp.stack([h[:, e] for e in go], 1)), "rows", bit)
            live = stay
        cut[side] = h[:, 0]
    g = jnp.concatenate(cut, -1)
    for bit in vbits[:-1][::-1]:
        n = g.shape[0] // 2
        g = halve((g[:n], g[n:]), "vocab", bit)
    g = g[0]
    full = gather_xor(g, "rows", rbits)
    if per >= rows:
        slot_grad = full.reshape(per, BS, BS)
        turn = row * (per // rows)
    else:
        slot_grad = jnp.take(full, row ^ jnp.arange(rows), axis=0).reshape(per, BS, BS)
        turn = jnp.int32(0)

    (new_matrix, new_first, new_second, new_left, new_right, renewed_left_basis, new_rbasis) = soap_call(
        turn.reshape(1), master_matrix, slot_grad, matrix_first, matrix_second, left_stat, right_stat,
        left_basis, right_basis,
    )
    new_bias, new_bias_first, new_bias_second = adam_bias(lens_bias, bias_grad, bias_first, bias_second)
    return (
        loss_sum, loss_count, new_matrix, new_first, new_second, new_left, new_right, renewed_left_basis,
        new_rbasis, new_bias, new_bias_first, new_bias_second,
    )


def solution(mesh):
    in_specs = (
        P("rows"),
        P("rows"),
        P("rows", None),
        P(),
        P("vocab", None),
        P("vocab", None),
        P(),
        P(),
        P(),
        P(),
        P(),
        P(),
        P(),
        P("vocab", None, None),
        P(None, "vocab"),
        P("vocab", None, None),
        P("vocab", None, None),
        P("vocab", None, None),
        P("vocab", None, None),
        P("vocab", None, None),
        P("vocab", None, None),
        P(None, "vocab"),
        P(None, "vocab"),
    )
    out_specs = (
        P(),
        P(),
        P("vocab", None, None),
        P("vocab", None, None),
        P("vocab", None, None),
        P("vocab", None, None),
        P("vocab", None, None),
        P("vocab", None, None),
        P("vocab", None, None),
        P(None, "vocab"),
        P(None, "vocab"),
        P(None, "vocab"),
    )
    return jax.shard_map(body, mesh=mesh, in_specs=in_specs, out_specs=out_specs, check_vma=False)
```

```python
import functools

import jax
import jax.numpy as jnp
import numpy as np
from jax import lax
from jax.experimental import pallas as pl
from jax.experimental.pallas import tpu as pltpu
from jax.sharding import PartitionSpec as P

HEADS = 16
HEAD_DIM = 64
ROT = 16
BS = 256
STEP = 5

HIGHEST = lax.Precision.HIGHEST
NORM_EPS = 1e-05
BETA_ONE = 0.9
BETA_TWO = 0.999
BETA_STAT = 0.95
ADAM_EPS = 1e-08
MATRIX_RATE = 0.01
BIAS_RATE = 0.1
DECAY = 0.1
MASKED = -1e30
NB = 64
PIV = 2
VMEM_LIMIT = 56 * 2**20


def _mm(a,b,dims):
    return lax.dot_general(a,b,(dims,((),())),precision=HIGHEST,preferred_element_type=jnp.float32)
def mm_nn(a,b): return _mm(a,b,((1,),(0,)))
def mm_tn(a,b): return _mm(a,b,((0,),(0,)))
def mm_nt(a,b): return _mm(a,b,((1,),(1,)))
def _mb(a,b,dims):
    return lax.dot_general(a.astype(jnp.bfloat16),b.astype(jnp.bfloat16),(dims,((),())),preferred_element_type=jnp.float32)

def eliminate(rows, nb):
    rows=list(rows)
    def pick(i,c):
        return jnp.broadcast_to(rows[i][:,c:c+1],rows[i].shape)
    for j in range(0,nb,PIV):
        low=[[None]*PIV for _ in range(PIV)]
        roots=[None]*PIV
        inv=[[None]*PIV for _ in range(PIV)]
        cur=[[pick(j+p,j+q) if q<=p else None for q in range(PIV)] for p in range(PIV)]
        for q in range(PIV):
            guess=lax.rsqrt(cur[q][q])
            roots[q]=guess*(1.5-0.5*(cur[q][q]*guess)*guess)
            for p in range(q+1,PIV):
                low[p][q]=cur[p][q]*roots[q]
            for p in range(q+1,PIV):
                for t in range(q+1,p+1):
                    cur[p][t]=cur[p][t]-low[p][q]*low[t][q]
        lead=[]
        for p in range(PIV):
            acc=rows[j+p]
            for q in range(p):
                acc=acc-low[p][q]*lead[q]
            lead.append(acc*roots[p])
        back=[None]*PIV
        for p in reversed(range(PIV)):
            acc=lead[p]
            for q in range(p+1,PIV):
                acc=acc-low[q][p]*back[q]
            back[p]=acc*roots[p]
        for i in range(j+PIV,nb):
            cols=[pick(i,j+p) for p in range(PIV)]
            t=cols[0]*back[0]
            for p in range(1,PIV):
                t=t+cols[p]*back[p]
            rows[i]=rows[i]-t
        for p in range(PIV):
            rows[j+p]=lead[p]
    return rows

def soap_kernel(per, where_ref, w_ref,g_ref,first_ref,second_ref,left_ref,right_ref,lb_ref,rb_ref,
                nw_ref,nf_ref,ns_ref,nl_ref,nr_ref,ql_ref,qr_ref,work,prods,stage):
    xor=where_ref[0]
    nm=2*per
    nn=((1,),(0,)); tn=((0,),(0,)); nt=((1,),(1,))
    def slot(s,c):
        g=g_ref[s^xor].astype(jnp.float32)
        gb=g.astype(jnp.bfloat16)
        lb=lb_ref[s]; rb=rb_ref[s]
        lbb=lb.astype(jnp.bfloat16); rbb=rb.astype(jnp.bfloat16)
        rotated=_mb(_mb(lbb,gb,tn),rbb,nn)
        first=BETA_ONE*first_ref[s]+(1.0-BETA_ONE)*g
        second=BETA_TWO*second_ref[s]+(1.0-BETA_TWO)*rotated*rotated
        nf_ref[s]=first; ns_ref[s]=second
        moment=_mb(_mb(lbb,first,tn),rbb,nn)
        scaled=moment/(1.0-BETA_ONE**STEP)/(jnp.sqrt(second/(1.0-BETA_TWO**STEP))+ADAM_EPS)
        update=_mb(_mb(lbb,scaled,nn),rbb,nt)
        w=w_ref[s]
        nw_ref[s]=w-MATRIX_RATE*(update+DECAY*w)
        nl=BETA_STAT*left_ref[s]+(1.0-BETA_STAT)*_mb(gb,gb,nt)
        nr=BETA_STAT*right_ref[s]+(1.0-BETA_STAT)*_mb(gb,gb,tn)
        nl_ref[s]=nl; nr_ref[s]=nr
        pl_=mm_nn(nl,lb); pr_=mm_nn(nr,rb)
        prods[s]=pl_; prods[per+s]=pr_
        work[s]=mm_tn(pl_,pl_); work[per+s]=mm_tn(pr_,pr_)
        return c
    lax.fori_loop(0,per,slot,0,unroll=True)
    lane=lax.broadcasted_iota(jnp.int32,(NB,128),1)
    row=lax.broadcasted_iota(jnp.int32,(NB,128),0)
    ident=(lane==row+NB).astype(jnp.float32)
    idrow=lax.broadcasted_iota(jnp.int32,(NB,BS),0)
    col=lax.broadcasted_iota(jnp.int32,(NB,BS),1)
    colw=lax.broadcasted_iota(jnp.int32,(BS,BS),1)
    upper=lax.broadcasted_iota(jnp.int32,(NB,NB),0)<=lax.broadcasted_iota(jnp.int32,(NB,NB),1)
    def fill(k):
        r0=k*NB
        for m in range(nm):
            d=work[m,r0:r0+NB,r0//128*128:r0//128*128+128]
            if r0%128: d=pltpu.roll(d,128-r0%128,axis=1)
            stage[m*NB:(m+1)*NB,:]=jnp.where(lane<NB,d,ident)
    def trail(k):
        r0=k*NB
        end=r0+NB
        lo=end//128*128
        inside=(col>=r0)&(col<end)
        ms=range(nm)
        linv=[stage[m*NB:(m+1)*NB,NB:2*NB] for m in ms]
        rows_m=[jnp.where(inside,(col==idrow+r0).astype(jnp.float32),work[m,r0:end,:]) for m in ms]
        b=[mm_nn(linv[m],rows_m[m]) for m in ms]
        if end<BS:
            up=[jnp.where(upper,stage[m*NB:(m+1)*NB,:NB],0.0) for m in ms]
            left=[rows_m[m][:,lo:]-mm_tn(up[m],b[m][:,lo:]) for m in ms]
            fix=[b[m][:,lo:]+mm_nn(linv[m],left[m]) for m in ms]
            b=[fix[m] if lo==0 else jnp.concatenate([b[m][:,:lo],fix[m]],1) for m in ms]
            cw=colw[:BS-end]
            rest=[mm_tn(b[m][:,lo:],b[m])[end-lo:] for m in ms]
            for m in ms:
                work[m,end:,:]=jnp.where((cw>=r0)&(cw<end),0.0,work[m,end:,:])-rest[m]
        for m in ms:
            work[m,r0:end,:]=b[m]
    def step(kb,c):
        for k in range(BS//NB):
            @pl.when(kb==k)
            def _(k=k):
                fill(k)
        rows=[stage[pl.ds(i,nm,stride=NB),:] for i in range(NB)]
        rows=eliminate(rows,NB)
        for i in range(NB):
            stage[pl.ds(i,nm,stride=NB),:]=rows[i]
        for k in range(BS//NB):
            @pl.when(kb==k)
            def _(k=k):
                trail(k)
        return c
    lax.fori_loop(0,BS//NB,step,0)
    roww=lax.broadcasted_iota(jnp.int32,(BS,BS),0)
    weight=jnp.where(roww>colw,1.0,jnp.where(roww==colw,0.5,0.0))
    unit=(roww==colw).astype(jnp.float32)
    outs=[(ql_ref,s) for s in range(per)]+[(qr_ref,s) for s in range(per)]
    bases=[mm_nt(prods[m],jnp.where(roww>=colw,work[m],0.0)) for m in range(nm)]
    for turn in range(2):
        gaps=[(mm_tn(q,q)-unit)*weight for q in bases]
        bases=[q-_mb(q,gap,nt) for q,gap in zip(bases,gaps)]
    for (ref,s),q in zip(outs,bases):
        ref[s]=q

def soap_call(xor,w,g,first,second,left,right,lb,rb):
    per=w.shape[0]
    sh=jax.ShapeDtypeStruct((per,BS,BS),jnp.float32)
    vm=pl.BlockSpec(memory_space=pltpu.VMEM)
    return pl.pallas_call(functools.partial(soap_kernel,per),
        out_shape=[sh]*7,
        in_specs=[pl.BlockSpec(memory_space=pltpu.SMEM)]+[vm]*8, out_specs=[vm]*7,
        scratch_shapes=[pltpu.VMEM((2*per,BS,BS),jnp.float32),pltpu.VMEM((2*per,BS,BS),jnp.float32),pltpu.VMEM((2*per*NB,128),jnp.float32)],
        compiler_params=pltpu.CompilerParams(vmem_limit_bytes=48*2**20),
        name="soap_update")(xor,w,g,first,second,left,right,lb,rb)


def adam_bias(bias, grad, first, second):
    first_new = BETA_ONE * first + (1.0 - BETA_ONE) * grad
    second_new = BETA_TWO * second + (1.0 - BETA_TWO) * grad * grad
    scaled = (
        first_new
        / (1.0 - BETA_ONE**STEP)
        / (jnp.sqrt(second_new / (1.0 - BETA_TWO**STEP)) + ADAM_EPS)
    )
    return (bias - BIAS_RATE * scaled, first_new, second_new)


def places(index, seq_lens):
    ends = jnp.cumsum(seq_lens)
    segment = jnp.sum((index[:, None] >= ends[None, :]).astype(jnp.int32), 1)
    starts = ends - seq_lens
    picked = segment[:, None] == jnp.arange(seq_lens.shape[0], dtype=jnp.int32)[None, :]
    offset = jnp.sum(jnp.where(picked, starts[None, :], 0), 1)
    return (segment, index - offset)


def swap(x, axis, bit):
    size = lax.axis_size(axis)
    return lax.ppermute(x, axis, [(i, i ^ bit) for i in range(size)])


def gather_xor(x, axis, bits):
    out = x[None]
    for bit in bits:
        out = jnp.concatenate([out, swap(out, axis, bit)], 0)
    return out


def bits_of(size):
    return [1 << i for i in range(size.bit_length() - 1)]


def chip_bits(size):
    return bits_of(size)[1:][::-1] + [1]


def entry_ids(bits):
    ids = [0]
    for bit in bits:
        ids = ids + [i ^ bit for i in ids]
    return ids


def normalize(x, gain, shift):
    centred = x - jnp.mean(x, -1, keepdims=True)
    root = lax.rsqrt(jnp.mean(centred * centred, -1, keepdims=True) + NORM_EPS)
    return centred * root * gain + shift


def turned(x, cos, sin):
    width = x.shape[1]
    lane = lax.broadcasted_iota(jnp.int32, (1, width), 1)
    swapped = jnp.where(
        lane % HEAD_DIM < ROT // 2,
        pltpu.roll(x, width - ROT // 2, axis=1),
        pltpu.roll(x, ROT // 2, axis=1),
    )
    reps = width // cos.shape[1]
    return x * jnp.concatenate([cos] * reps, 1) + swapped * jnp.concatenate([sin] * reps, 1)


def fill_pool(bufs, pool, sems):
    take = bufs[0].shape[0]
    return [
        pltpu.make_async_copy(buf, pool.at[i * take : (i + 1) * take, :], sems.at[i])
        for i, buf in enumerate(bufs)
    ]


def placed(pool, column):
    spread = lax.broadcasted_iota(jnp.int32, (column.shape[0], pool.shape[0]), 1) == column
    return jnp.dot(spread.astype(jnp.bfloat16), pool[...], preferred_element_type=jnp.float32)


def place_kernel(parts, where_ref, *refs):
    bufs = refs[:parts]
    meta, more, pick, own_out, sent_out, pool, rest, sems = refs[parts:]
    own = own_out.shape[0]
    fills = fill_pool(bufs, pool, sems)
    for fill in fills:
        fill.start()
    for fill in fills:
        fill.wait()
    mine = pl.ds(pl.multiple_of(where_ref[0] * own, own), own)
    x = placed(pool, meta[mine, 0:1])
    rest[...] = jnp.zeros(rest.shape, rest.dtype)

    @pl.when(where_ref[1] > 0)
    def _():
        copy = pltpu.make_async_copy(more.at[mine, :], rest, sems.at[parts])
        copy.start()
        copy.wait()

    x = x.astype(jnp.bfloat16) + rest[...]
    own_out[...] = x
    sent_out[...] = jnp.dot(pick[...], x, preferred_element_type=jnp.float32).astype(jnp.bfloat16)


def place_call(where, bufs, meta, more, pick):
    take, width = bufs[0].shape
    parts = len(bufs)
    own = pick.shape[1]
    vm = pl.BlockSpec(memory_space=pltpu.VMEM)
    hbm = pl.BlockSpec(memory_space=pl.ANY)
    bf = jnp.bfloat16
    return pl.pallas_call(
        functools.partial(place_kernel, parts),
        out_shape=[
            jax.ShapeDtypeStruct((own, width), bf),
            jax.ShapeDtypeStruct((pick.shape[0], width), bf),
        ],
        in_specs=[pl.BlockSpec(memory_space=pltpu.SMEM)] + [hbm] * parts + [vm, hbm, vm],
        out_specs=[vm] * 2,
        scratch_shapes=[
            pltpu.VMEM((parts * take, width), bf),
            pltpu.VMEM((own, width), bf),
            pltpu.SemaphoreType.DMA((parts + 1,)),
        ],
        compiler_params=pltpu.CompilerParams(vmem_limit_bytes=VMEM_LIMIT),
        cost_estimate=pl.CostEstimate(flops=10**9, bytes_accessed=4 * 2**20, transcendentals=0),
        name="place_rows",
    )(where, *bufs, meta, more, pick)


def project_kernel(parts, where_ref, *refs):
    bufs = refs[:parts]
    (meta, more, cosines, sines, bias, gain, shift, qkv, k_out, v_out, q_out, pool, rest, emb, w_qkv,
     sems) = refs[parts:]
    group, width = k_out.shape
    own = q_out.shape[0]
    fills = fill_pool(bufs, pool, sems)
    loads = [
        pltpu.make_async_copy(qkv.at[:, i * width : (i + 1) * width], w_qkv.at[i], sems.at[parts + i])
        for i in range(3)
    ]
    for fill in fills:
        fill.start()
    for i in (1, 2, 0):
        loads[i].start()
    for fill in fills:
        fill.wait()
    rows = 256
    rest[...] = jnp.zeros(rest.shape, rest.dtype)

    def attn_in(x):
        return normalize(x.astype(jnp.float32), gain[0:1, :], shift[0:1, :]).astype(jnp.bfloat16)

    loads[1].wait()
    loads[2].wait()

    def project(i, c):
        at = pl.ds(pl.multiple_of(i * rows, rows), rows)

        @pl.when(where_ref[1] > 0)
        def _():
            copy = pltpu.make_async_copy(more.at[at, :], rest, sems.at[parts + 3])
            copy.start()
            copy.wait()

        x = placed(pool, meta[at, 0:1]).astype(jnp.bfloat16) + rest[...]
        emb[at, :] = x
        y = attn_in(x)
        k = jnp.dot(y, w_qkv[1], preferred_element_type=jnp.float32) + bias[:, width : 2 * width]
        k_out[at, :] = turned(k, cosines[at, :], sines[at, :]).astype(jnp.bfloat16)
        v = jnp.dot(y, w_qkv[2], preferred_element_type=jnp.float32)
        v_out[at, :] = (v + bias[:, 2 * width : 3 * width]).astype(jnp.bfloat16)
        return c

    lax.fori_loop(0, group // rows, project, 0)
    mine = pl.ds(pl.multiple_of(where_ref[0] * own, own), own)
    loads[0].wait()
    q = jnp.dot(attn_in(emb[mine, :]), w_qkv[0], preferred_element_type=jnp.float32)
    q = turned(q + bias[:, :width], cosines[mine, :], sines[mine, :])
    q_out[...] = q.astype(jnp.bfloat16)


def project_call(own, where, bufs, meta, more, cosines, sines, bias, gain, shift, qkv):
    group = meta.shape[0]
    take, width = bufs[0].shape
    parts = len(bufs)
    vm = pl.BlockSpec(memory_space=pltpu.VMEM)
    hbm = pl.BlockSpec(memory_space=pl.ANY)
    bf = jnp.bfloat16
    return pl.pallas_call(
        functools.partial(project_kernel, parts),
        out_shape=[
            jax.ShapeDtypeStruct((group, width), bf),
            jax.ShapeDtypeStruct((group, width), bf),
            jax.ShapeDtypeStruct((own, width), bf),
        ],
        in_specs=[pl.BlockSpec(memory_space=pltpu.SMEM)] + [hbm] * parts + [vm, hbm] + [vm] * 5 + [hbm],
        out_specs=[vm] * 3,
        scratch_shapes=[
            pltpu.VMEM((parts * take, width), bf),
            pltpu.VMEM((256, width), bf),
            pltpu.VMEM((group, width), bf),
            pltpu.VMEM((3, width, width), bf),
            pltpu.SemaphoreType.DMA((parts + 4,)),
        ],
        compiler_params=pltpu.CompilerParams(vmem_limit_bytes=VMEM_LIMIT),
        cost_estimate=pl.CostEstimate(flops=12 * 10**9, bytes_accessed=16 * 2**20, transcendentals=0),
        name="project_group",
    )(where, *bufs, meta, more, cosines, sines, bias, gain, shift, qkv)


def layer_kernel(
    chunks, where_ref, k_all, v_all, q_own, emb, meta, key_meta, bias, gain, shift, pick,
    w_out, w_up, w_down, out, sent_out, wo, up, down, mix, sems,
):
    own, width = emb.shape
    units = w_up.shape[1]
    part = units // chunks
    nbuf = up.shape[0]

    def load(j):
        n = j % nbuf
        return (
            pltpu.make_async_copy(w_up.at[:, j * part : (j + 1) * part], up.at[n], sems.at[1 + n]),
            pltpu.make_async_copy(
                w_down.at[j * part : (j + 1) * part, :], down.at[n], sems.at[1 + nbuf + n]
            ),
        )

    load_out = pltpu.make_async_copy(w_out, wo, sems.at[0])
    load_out.start()
    for j in range(nbuf):
        for copy in load(j):
            copy.start()

    mine = pl.ds(pl.multiple_of(where_ref[0] * own, own), own)
    allowed = (meta[mine, 1:2] == key_meta[0:1, :]) & (key_meta[1:2, :] <= meta[mine, 2:3])
    half = lax.broadcasted_iota(jnp.int32, (1, 2 * HEAD_DIM), 1) // HEAD_DIM

    def pair(hp, c):
        at = pl.ds(pl.multiple_of(hp * 2 * HEAD_DIM, 2 * HEAD_DIM), 2 * HEAD_DIM)
        qp, kp, vp = q_own[:, at], k_all[:, at], v_all[:, at]
        outs = []
        for h in range(2):
            qh = jnp.where(half == h, qp, jnp.zeros((), jnp.bfloat16))
            scores = lax.dot_general(
                qh, kp, (((1,), (1,)), ((), ())), preferred_element_type=jnp.float32
            )
            scores = jnp.where(allowed, scores * HEAD_DIM ** (-0.5), MASKED)
            weights = jnp.exp(scores - jnp.max(scores, -1, keepdims=True))
            total = jnp.sum(weights, -1, keepdims=True)
            got = jnp.dot(weights.astype(jnp.bfloat16), vp, preferred_element_type=jnp.float32)
            outs.append(got / total)
        mix[:, at] = jnp.where(half == 0, outs[0], outs[1]).astype(jnp.bfloat16)
        return c

    lax.fori_loop(0, HEADS // 2, pair, 0)
    x_own = emb[...].astype(jnp.float32)
    load_out.wait()
    total = x_own + (
        jnp.dot(mix[...], wo[...], preferred_element_type=jnp.float32)
        + bias[:, 3 * width : 4 * width]
    )
    mlp_in = normalize(x_own, gain[1:2, :], shift[1:2, :]).astype(jnp.bfloat16)
    acc = jnp.zeros((own, width), jnp.float32)
    for j in range(chunks):
        for copy in load(j):
            copy.wait()
        lo = 4 * width + j * part
        pre = jnp.dot(mlp_in, up[j % nbuf], preferred_element_type=jnp.float32)
        pre = pre + bias[:, lo : lo + part]
        activ = (0.5 * pre * (1.0 + lax.erf(pre * 0.7071067811865476))).astype(jnp.bfloat16)
        acc = acc + jnp.dot(activ, down[j % nbuf], preferred_element_type=jnp.float32)
        if j + nbuf < chunks:
            for copy in load(j + nbuf):
                copy.start()
    low = (total + (acc + bias[:, 4 * width + units :])).astype(jnp.bfloat16)
    out[...] = low
    sent_out[...] = jnp.dot(pick[...], low, preferred_element_type=jnp.float32).astype(jnp.bfloat16)


def layer_call(where, k, v, q, emb, meta, key_meta, bias, gain, shift, pick, w_out, w_up, w_down):
    group, width = k.shape
    own = emb.shape[0]
    units = w_up.shape[1]
    chunks = units // width
    nbuf = chunks if group <= 1024 else 2
    vm = pl.BlockSpec(memory_space=pltpu.VMEM)
    hbm = pl.BlockSpec(memory_space=pl.ANY)
    bf = jnp.bfloat16
    return pl.pallas_call(
        functools.partial(layer_kernel, chunks),
        out_shape=[
            jax.ShapeDtypeStruct((own, width), bf),
            jax.ShapeDtypeStruct((pick.shape[0], width), bf),
        ],
        in_specs=[pl.BlockSpec(memory_space=pltpu.SMEM)] + [vm] * 10 + [hbm] * 3,
        out_specs=[vm, vm],
        scratch_shapes=[
            pltpu.VMEM((width, width), bf),
            pltpu.VMEM((nbuf, width, units // chunks), bf),
            pltpu.VMEM((nbuf, units // chunks, width), bf),
            pltpu.VMEM((own, width), bf),
            pltpu.SemaphoreType.DMA((1 + 2 * nbuf,)),
        ],
        compiler_params=pltpu.CompilerParams(vmem_limit_bytes=VMEM_LIMIT),
        cost_estimate=pl.CostEstimate(flops=12 * 10**9, bytes_accessed=24 * 2**20, transcendentals=0),
        name="frozen_layer",
    )(where, k, v, q, emb, meta, key_meta, bias, gain, shift, pick, w_out, w_up, w_down)


def probe_kernel(limit, sets, chunks, kind, first, *refs):
    if kind == "rest":
        sums_in, normed, peak_in, mass_in, table, sums, stats, peak, mass = refs
    elif kind == "start":
        loc_ref, x, slots, bias, gain, shift, table, sums, hats, normed, peak, mass = refs
    else:
        loc_ref, x, slots, bias, gain, shift, table, sums, stats, hats, normed, peak, mass = refs
    begins = pl.program_id(0) == 0
    step = pl.program_id(0) + first
    tile, width = table.shape
    steps = -(-limit // tile)
    count = chunks * normed.shape[1] // len(sets)
    nblk = width // BS
    size = count // chunks
    many = len(sets)

    def start():
        def save(i, rows, v):
            centred = v - jnp.mean(v, -1, keepdims=True)
            root = lax.rsqrt(jnp.mean(centred * centred, -1, keepdims=True) + NORM_EPS)
            hat = centred * root
            normed[rows // size, i * size : (i + 1) * size, :] = (
                hat * gain[2:3, :] + shift[2:3, :]
            ).astype(jnp.bfloat16)
            return hat, root

        for c in range(chunks):
            rows = c * size
            raw = x[rows : rows + size, :]
            v = raw.astype(jnp.float32)
            for i, k in enumerate(sets):
                if k < 0:
                    hat, root = save(i, rows, v)
                else:
                    cols = []
                    for j in range(nblk):
                        total = None
                        for b in range(nblk):
                            term = jnp.dot(
                                raw[:, b * BS : (b + 1) * BS],
                                slots[loc_ref[(k * nblk + b) * nblk + j], :BS, :],
                                preferred_element_type=jnp.float32,
                            )
                            total = term if total is None else total + term
                        cols.append(total)
                    hat, root = save(i, rows, v + jnp.concatenate(cols, 1) + bias[k : k + 1, :])
                hats[i, rows : rows + size, :width] = hat
                hats[i, rows : rows + size, width:] = jnp.broadcast_to(root, (size, 128))
        peak[...] = jnp.full(peak.shape, MASKED, jnp.float32)
        mass[...] = jnp.zeros(mass.shape, jnp.float32)
        sums[...] = jnp.zeros(sums.shape, jnp.float32)

    def resume():
        peak[...] = peak_in[...]
        mass[...] = mass_in[...]
        sums[...] = sums_in[...]

    pl.when(begins)(resume if kind == "rest" else start)

    def visit(last):
        w = table[...]
        if last:
            left = limit - step * tile
            at = lax.broadcasted_iota(jnp.int32, (1, tile), 1)
            down = lax.broadcasted_iota(jnp.int32, (tile, 1), 0)
            w = jnp.where(down < left, w, jnp.zeros((), jnp.bfloat16))

        def score(c):
            return lax.dot_general(
                normed[c], w, (((1,), (1,)), ((), ())), preferred_element_type=jnp.float32
            )

        ready = score(0)
        for c in range(chunks):
            logits = ready
            if c + 1 < chunks:
                ready = score(c + 1)
            if last:
                logits = jnp.where(at < left, logits, MASKED)
            old = peak[c]
            new = jnp.maximum(old, jnp.max(logits, -1, keepdims=True))
            fade = jnp.exp(old - new)
            powers = jnp.exp(logits - new)
            peak[c] = new
            mass[c] = mass[c] * fade + jnp.sum(powers, -1, keepdims=True)
            sums[c] = sums[c] * fade + jnp.dot(
                powers.astype(jnp.bfloat16), w, preferred_element_type=jnp.float32
            )

    def finish():
        visit(True)
        lanes = -(-count // 128) * 128
        at = lax.broadcasted_iota(jnp.int32, (lanes, 128), 1)
        packed = jnp.zeros((lanes, 128), jnp.float32)
        for i in range(many):
            for n, ref in ((i, peak), (many + i, mass)):
                col = [ref[c, i * size : (i + 1) * size, :] for c in range(chunks)]
                if lanes > count:
                    col.append(jnp.zeros((lanes - count, 1), jnp.float32))
                packed = jnp.where(at == n, jnp.concatenate(col, 0), packed)
        stats[...] = jnp.transpose(packed)[:8, :]

    if kind == "start":
        visit(False)
    else:
        pl.when(step < steps - 1)(lambda: visit(False))
        pl.when(step == steps - 1)(finish)


def probe_call(sets, kind, table, *given):
    vocab, width = table.shape
    tile = 1280
    steps = -(-vocab // tile)
    ahead = -(-steps // 2)
    first, todo = {"all": (0, steps), "start": (0, ahead), "rest": (ahead, steps - ahead)}[kind]
    many = len(sets)
    f32 = jnp.float32
    if kind == "rest":
        chunks, rows = given[0].shape[:2]
        size = rows // many
    else:
        count = given[1].shape[0]
        chunks = many if count % (16 * many) == 0 else 1
        size = count // chunks
    count = chunks * size
    vm = pl.BlockSpec(memory_space=pltpu.VMEM)
    column = (chunks, many * size, 1)
    sums = jax.ShapeDtypeStruct((chunks, many * size, width), f32)
    stats = jax.ShapeDtypeStruct((8, -(-count // 128) * 128), f32)
    hats = jax.ShapeDtypeStruct((many, count, width + 128), f32)
    scratch = [pltpu.VMEM(column, f32), pltpu.VMEM(column, f32)]
    if kind == "rest":
        outs, ins = [sums, stats], [vm] * 4
    else:
        ins = [pl.BlockSpec(memory_space=pltpu.SMEM)] + [vm] * 5
        normed = (chunks, many * size, width)
        if kind == "start":
            col = jax.ShapeDtypeStruct(column, f32)
            outs, scratch = [sums, hats, jax.ShapeDtypeStruct(normed, jnp.bfloat16), col, col], []
        else:
            outs, scratch = [sums, stats, hats], [pltpu.VMEM(normed, jnp.bfloat16)] + scratch
    return pl.pallas_call(
        functools.partial(probe_kernel, vocab, sets, chunks, kind, first),
        grid=(todo,),
        out_shape=outs,
        in_specs=ins + [pl.BlockSpec((tile, width), lambda i: (i + first, 0))],
        out_specs=[vm] * len(outs),
        scratch_shapes=scratch,
        compiler_params=pltpu.CompilerParams(vmem_limit_bytes=VMEM_LIMIT),
        cost_estimate=pl.CostEstimate(
            flops=4 * many * count * todo * tile * width, bytes_accessed=2 * todo * tile * width, transcendentals=0
        ),
        name="probe_" + kind,
    )(*given, table)


def grad_kernel(
    dest_ref, x0, x1, sums1, sums02, scale, hats1, hats02, gain, shift, stay, go, small,
    grads, sems,
):
    count, width = x0.shape
    nblk = width // BS
    pieces = dest_ref.shape[1]
    rows = BS // pieces
    chunks = sums02.shape[0]
    size = count // chunks
    cols = jnp.transpose(jnp.concatenate([scale[...]] * (128 // scale.shape[0]), 0))[:count]
    gain_row, shift_row = gain[2:3, :], shift[2:3, :]

    def normed(hat):
        return (hat * gain_row + shift_row).astype(jnp.bfloat16).astype(jnp.float32)

    def parts(n):
        return jnp.concatenate([sums02[c, n * size : (n + 1) * size, :] for c in range(chunks)], 0)

    base = parts(0) * cols[:, 0:1]
    target = normed(hats02[0, :, :width])
    spread = jnp.zeros((1, width), jnp.float32)
    for k in range(2):
        own = sums1[...].reshape(count, width) if k == 0 else parts(1)
        hats = hats1.at[0] if k == 0 else hats02.at[1]
        hat = hats[:, :width]
        root = hats[:, width : width + 1]
        spread = spread + jnp.sum(base * (target - normed(hat)), 0, keepdims=True)
        e = (own * cols[:, k + 1 : k + 2] - base) * gain_row
        pulled = e - jnp.mean(e, -1, keepdims=True)
        pulled = (pulled - hat * jnp.mean(e * hat, -1, keepdims=True)) * root
        small[k : k + 1, :] = jnp.sum(pulled, 0, keepdims=True)
        low = pulled.astype(jnp.bfloat16)
        x = x0 if k == 0 else x1
        for i in range(nblk):
            full = lax.dot_general(
                x[:, i * BS : (i + 1) * BS], low, (((0,), (0,)), ((), ())),
                preferred_element_type=jnp.float32,
            ).astype(jnp.bfloat16)
            for j in range(nblk):
                b = (k * nblk + i) * nblk + j
                for p in range(pieces):
                    piece = full[p * rows : (p + 1) * rows, j * BS : (j + 1) * BS]
                    grads[dest_ref[b, p]] = piece
    half = grads.shape[0] // 2
    copies = [
        pltpu.make_async_copy(grads.at[:half], stay, sems.at[0]),
        pltpu.make_async_copy(grads.at[half:], go, sems.at[1]),
    ]
    for copy in copies[::-1]:
        copy.start()
    small[2:3, :] = spread
    small[3:, :] = jnp.zeros((5, width), jnp.float32)
    for copy in copies:
        copy.wait()


def grad_call(dest, x0, x1, sums1, sums02, scale, hats1, hats02, gain, shift):
    width = x0.shape[1]
    pieces = dest.shape[1]
    vm = pl.BlockSpec(memory_space=pltpu.VMEM)
    hbm = pl.BlockSpec(memory_space=pl.ANY)
    half = jax.ShapeDtypeStruct((dest.shape[0] * pieces // 2, BS // pieces, BS), jnp.bfloat16)
    return pl.pallas_call(
        grad_kernel,
        out_shape=[
            half,
            half,
            jax.ShapeDtypeStruct((8, width), jnp.float32),
        ],
        in_specs=[pl.BlockSpec(memory_space=pltpu.SMEM)] + [vm] * 9,
        out_specs=[hbm, hbm, vm],
        scratch_shapes=[
            pltpu.VMEM((dest.shape[0] * pieces, BS // pieces, BS), jnp.bfloat16),
            pltpu.SemaphoreType.DMA((2,)),
        ],
        compiler_params=pltpu.CompilerParams(vmem_limit_bytes=VMEM_LIMIT),
        cost_estimate=pl.CostEstimate(flops=4 * 10**9, bytes_accessed=16 * 2**20, transcendentals=0),
        name="lens_gradient",
    )(dest, x0, x1, sums1, sums02, scale, hats1, hats02, gain, shift)


def merge(a, b):
    peak = jnp.maximum(a[:3], b[:3])
    return jnp.concatenate([peak, a[3:] * jnp.exp(a[:3] - peak) + b[3:] * jnp.exp(b[:3] - peak)], 0)


def ring(x, step):
    size = lax.axis_size("vocab")
    return lax.ppermute(x, "vocab", [(i, (i + 2 * step) % size) for i in range(size)])


def add(*terms):
    total = terms[0].astype(jnp.float32)
    for term in terms[1:]:
        total = total + term.astype(jnp.float32)
    return total.astype(terms[0].dtype)


def spread_group(x):
    chips = lax.axis_size("vocab") // 2
    near = jnp.stack([x] + [ring(x, o) for o in range(1, chips)], 0)
    return jnp.stack([near, swap(near, "vocab", 1)], 0)


def tie(*values):
    return lax.optimization_barrier(values)


def reduce_slots(grads, small, later=None):
    chips, rows = lax.axis_size("vocab") // 2, lax.axis_size("rows")
    bits = bits_of(rows)
    todo = [("rows", bit) for bit in bits] + [("vocab", bit) for bit in chip_bits(2 * chips)]

    def small_step(small):
        axis, bit = todo.pop(0)
        return small + swap(small, axis, bit)

    g = add(grads[0], swap(grads[1], "vocab", 1)).reshape(2, rows, chips // 2, -1, BS)
    g, small = tie(g, small)
    extra = later(small) if later else ()
    sides = [[g[side, e] for e in range(rows)] for side in range(2)]
    for at in range(len(bits)):
        for side in range(2):
            bit = (bits[::-1], bits)[side][at]
            h = sides[side]
            keep = [e for e in range(rows) if h[e] is not None and not e & bit]
            got = swap(jnp.stack([h[e | bit] for e in keep], 0), "rows", bit)
            sides[side] = [None] * rows
            for i, e in enumerate(keep):
                sides[side][e] = add(h[e], got[i])
        if todo:
            small = small_step(small)
        live = [[e for e in range(rows) if sides[side][e] is not None] for side in range(2)]
        flat = tie(small, *extra, *[sides[side][e] for side in range(2) for e in live[side]])
        small, extra, flat = flat[0], flat[1 : 1 + len(extra)], list(flat[1 + len(extra) :])
        for side in range(2):
            for e in live[side]:
                sides[side][e] = flat.pop(0)
    g = jnp.concatenate([sides[0][0], sides[1][0]], 0)
    mine = add(g[0], *[ring(g[o], o) for o in range(1, chips)])
    small = small_step(small)
    mine, small = tie(mine, small)
    parts = jnp.stack([mine] + [swap(mine, "rows", e) for e in range(1, rows)], 0)
    small = small_step(small)
    parts, small = tie(parts, small)
    while todo:
        small = small_step(small)
    return (parts, small, *extra)


def body(
    tokens, loss_position_mask, lengths, owners, embed_in, unembedding_table, frozen_qkv, frozen_out,
    frozen_up, frozen_down, frozen_bias, norm_gain, norm_shift, master_matrix, lens_bias, matrix_first,
    matrix_second, left_stat, right_stat, left_basis, right_basis, bias_first, bias_second,
):
    bf, f32, i32 = jnp.bfloat16, jnp.float32, jnp.int32
    shards, rows = lax.axis_size("vocab"), lax.axis_size("rows")
    where, row = lax.axis_index("vocab"), lax.axis_index("rows")
    group, width = tokens.shape[0], embed_in.shape[1]
    own = group // shards
    nblk = width // BS
    per = master_matrix.shape[0]
    blocks = shards * per
    chips = shards // 2
    vbits, rbits = chip_bits(shards), bits_of(rows)
    every = jnp.arange(shards, dtype=i32)

    chip, core = where // 2, where % 2
    entry_at = (chip - every // 2) % chips + chips * ((every % 2) ^ core)

    part_rows = per * BS // rows
    held = master_matrix.astype(bf).reshape(rows, part_rows, BS)
    held = lax.dynamic_index_in_dim(held, row, 0, keepdims=False)
    top = lens_bias.astype(bf)
    middle = (lens_bias - top.astype(f32)).astype(bf)
    low = (lens_bias - top.astype(f32) - middle.astype(f32)).astype(bf)
    flat = jnp.concatenate([jnp.pad(t.reshape(-1), (0, BS - lens_bias.size))[None] for t in (top, middle, low)], 0)
    held = jnp.concatenate([held, jnp.pad(flat, ((0, 13), (0, 0)))], 0)
    held = lax.all_gather(held, ("rows", "vocab"), axis=0)
    biases = jnp.sum(held[:shards, part_rows : part_rows + 3, : lens_bias.size].astype(f32), 1)
    biases = biases.reshape(shards, 2, -1).transpose(1, 0, 2).reshape(2, width)
    slots = held
    if per != rows:
        slots = held[:, :part_rows].reshape(rows, shards, part_rows, BS).transpose(1, 0, 2, 3)
        slots = slots.reshape(blocks, BS, BS)

    def by_class(a):
        return a.reshape(own, shards).T.reshape(-1)

    ids = by_class(tokens)
    index = by_class(jnp.arange(group, dtype=i32))
    mask = by_class(loss_position_mask)
    table_rows = embed_in.shape[0]
    owner = ids // table_rows
    local = ids - where * table_rows
    holds = (owner[:, None] == jnp.arange(shards, dtype=i32)[None, :]).astype(bf)
    before = (jnp.arange(group)[:, None] > jnp.arange(group)[None, :]).astype(bf)
    ahead = jnp.dot(before, holds, preferred_element_type=f32)
    rank = jnp.sum(ahead * holds.astype(f32), 1).astype(i32)
    take = 176 if group <= 1024 else 64
    apart = (chip - owner // 2) % chips + chips * ((owner % 2) ^ core)

    def chunk(k):
        slot = jnp.arange(take, dtype=i32)[:, None] + k * take
        hit = (owner == where)[None, :] & (rank[None, :] == slot)
        picked = jnp.sum(jnp.where(hit, local[None, :], 0), 1)
        mine = jnp.take(embed_in, picked, axis=0, mode="clip")
        return mine

    def exchange(mine, k):
        near = [mine]
        for o in range(1, chips):
            near.append(lax.ppermute(mine, "vocab", [(i, (i + 2 * o) % shards) for i in range(shards)]))
        place = rank - k * take
        column = jnp.where((place >= 0) & (place < take), apart * take + place, -1)
        return near + [swap(piece, "vocab", 1) for piece in near], column

    def fetch_more(c):
        pieces, column = exchange(chunk(c[0]), c[0])
        spread = (column[:, None] == jnp.arange(shards * take, dtype=i32)[None, :]).astype(bf)
        rows_in = jnp.dot(spread, jnp.concatenate(pieces, 0), preferred_element_type=f32)
        return (c[0] + 1, c[1] + rows_in.astype(bf))

    mine, mask, index, seq_lens = tie(chunk(jnp.int32(0)), mask, index, lengths[0])
    pieces_in, column = exchange(mine, jnp.int32(0))
    most = jnp.max(jnp.sum(holds.astype(f32), 0)).astype(i32)
    shared = gather_xor(jnp.concatenate([mask, jnp.full((8,), most, i32)]), "rows", rbits)
    masks = shared[:, :group].reshape(rows, shards, own)
    most = jnp.max(shared[:, group:])

    _, more = lax.while_loop(
        lambda c: c[0] * take < most, fetch_more, (jnp.int32(1), jnp.zeros((group, width), bf))
    )

    segment, position = places(index, seq_lens)
    half = ROT // 2
    lane = jnp.arange(2 * HEAD_DIM) % HEAD_DIM
    freq = 10000.0 ** (-2.0 * (lane % half).astype(f32) / ROT)
    angle = position.astype(f32)[:, None] * freq[None, :]
    turns = (lane < ROT)[None, :]
    cosines = jnp.where(turns, jnp.cos(angle), 1.0)
    sines = jnp.where(turns, jnp.sin(angle) * jnp.where(lane < half, -1.0, 1.0)[None, :], 0.0)
    key_meta = jnp.concatenate([segment[None], index[None], jnp.zeros((6, group), i32)], 0)
    meta = jnp.stack([column, segment, index], 1)
    bias_row = frozen_bias.reshape(1, -1)
    spot = jnp.stack([where, (most > take).astype(i32)])

    take_rows = max(16, 320 // shards)
    count = take_rows * shards
    mine_masks = lax.dynamic_index_in_dim(masks, where, 1, keepdims=False)
    per_row = jnp.sum(mine_masks, 1)
    lower = (row ^ jnp.arange(rows)) < row
    base = jnp.sum(jnp.where(lower, per_row, 0))
    dealt = base + jnp.cumsum(mine_masks[0]) - mine_masks[0]
    per_class = jnp.sum(masks, (0, 2))
    entry_chip = (chip - jnp.arange(chips)) % chips
    per_entry = jnp.concatenate(
        [jnp.take(per_class, entry_chip * 2 + core), jnp.take(per_class, entry_chip * 2 + (core ^ 1))]
    )
    share = (per_entry - row + rows - 1) // rows
    rounds = -(-jnp.max((per_class + rows - 1) // rows) // take_rows)

    numbers = jnp.arange(blocks, dtype=i32)
    pieces = max(1, rows // per)
    span = per * pieces // rows
    slot_of = jnp.sum(jnp.where(owners[None, :] == numbers[:, None], numbers[None, :], 0), 1)
    device, inner = slot_of // per, slot_of % per
    away_core = (device % 2) ^ core
    ahead_by = (device // 2 - chip) % chips
    piece = inner[:, None] * pieces + jnp.arange(pieces, dtype=i32)[None, :]
    part = (piece // span) ^ row
    half_chips = chips // 2
    dest = (away_core * 2 + ahead_by // half_chips)[:, None] * rows + part
    dest = (dest * half_chips + (ahead_by % half_chips)[:, None]) * span + piece % span
    loc = inner * shards + device if per == rows else slot_of

    def pick_of(k):
        target = jnp.arange(rows, dtype=i32) ^ row
        place = jnp.arange(take_rows, dtype=i32) + k * take_rows
        wanted = (place[None, :] * rows + target[:, None]).reshape(-1)
        return ((dealt[None, :] == wanted[:, None]) & (mine_masks[0] > 0)[None, :]).astype(bf)

    def across(sent):
        sent = sent.reshape(rows, take_rows, width)
        return add(sent[0], *[swap(sent[e], "rows", e) for e in range(1, rows)])

    def spread_out(sent):
        return spread_group(across(sent)).reshape(count, width)

    def share_stats(local):
        stats = local.reshape(6, 2, chips, take_rows)
        total = stats
        for o in range(1, chips):
            total = merge(total, jnp.roll(ring(stats, o), o, 2))
        return merge(total, jnp.flip(swap(total, "vocab", 1), 1)).reshape(6, count)

    def counted_in(k):
        place = jnp.arange(take_rows, dtype=i32)[None, :] + k * take_rows
        return (place < share[:, None]).reshape(-1).astype(f32)

    def with_loss(small, valid, stats):
        logtot = stats[:3] + jnp.log(stats[3:])
        loss = jnp.sum(valid * (logtot[1] + logtot[2] - 2.0 * logtot[0]))
        first_lane = (jnp.arange(width) == 0)[None, :] & (jnp.arange(8) == 2)[:, None]
        return small + jnp.where(first_lane & (where == 0), loss, 0.0)

    def later_round(k, slots, table, loc, dest):
        p = pick_of(k)
        y = [spread_out(jnp.dot(p, own_rows, preferred_element_type=f32).astype(bf)) for own_rows in (emb_own, out_own)]
        mats = jnp.take(slots[:, :BS], loc, axis=0).reshape(2, nblk, nblk, BS, BS)
        mats = mats.transpose(0, 1, 3, 2, 4).reshape(2, width, width)
        hats, roots = [], []
        for n in range(3):
            v = y[n - 1].astype(f32)
            if n:
                v = v + jnp.dot(y[n - 1], mats[n - 1], preferred_element_type=f32) + biases[n - 1]
            v = v - jnp.mean(v, -1, keepdims=True)
            roots.append(lax.rsqrt(jnp.mean(v * v, -1, keepdims=True) + NORM_EPS))
            hats.append(v * roots[-1])
        normed = (jnp.stack(hats) * norm_gain[2] + norm_shift[2]).astype(bf)
        logits = jnp.einsum("knd,vd->knv", normed, table, preferred_element_type=f32)
        peak = jnp.max(logits, -1)
        mass = jnp.sum(jnp.exp(logits - peak[..., None]), -1)
        stats = share_stats(jnp.concatenate([peak, mass], 0))
        valid = counted_in(k)
        probs = jnp.exp(logits - (stats[:3] + jnp.log(stats[3:]))[..., None]) * valid[None, :, None]
        cross = jnp.sum(probs[0] * (2.0 * logits[0] - logits[1] - logits[2]))
        slope = (probs[1:] - probs[:1]).astype(bf)
        e = jnp.einsum("knv,vd->knd", slope, table, preferred_element_type=f32) * norm_gain[2]
        hat, root = jnp.stack(hats[1:]), jnp.stack(roots[1:])
        pulled = e - jnp.mean(e, -1, keepdims=True) - hat * jnp.mean(e * hat, -1, keepdims=True)
        pulled = pulled * root
        grad = jnp.einsum("knd,kne->kde", jnp.stack(y), pulled.astype(bf), preferred_element_type=f32)
        grad = grad.astype(bf).reshape(2, nblk, BS, nblk, BS).transpose(0, 1, 3, 2, 4)
        grad = jnp.take(grad.reshape(-1, BS // pieces, BS), jnp.argsort(dest.reshape(-1)), axis=0)
        small = jnp.concatenate([jnp.sum(pulled, 1), jnp.zeros((6, width), f32)], 0)
        first_lane = (jnp.arange(width) == 0)[None, :] & (jnp.arange(8) == 2)[:, None]
        small = small + jnp.where(first_lane, cross, 0.0)
        return reduce_slots((grad[: grad.shape[0] // 2], grad[grad.shape[0] // 2 :]), with_loss(small, valid, stats))

    pick = pick_of(jnp.int32(0))
    emb_own, sent0 = place_call(spot, pieces_in, meta, more, pick)
    got0 = across(sent0)
    k_all, v_all, q_own = project_call(
        own, spot, pieces_in, meta, more, cosines, sines, bias_row, norm_gain, norm_shift, frozen_qkv
    )
    got0, q_own = tie(got0, q_own)
    near0 = jnp.stack([got0] + [ring(got0, o) for o in range(1, chips)], 0)
    out_own, sent1 = layer_call(
        spot, k_all, v_all, q_own, emb_own, meta, key_meta, bias_row, norm_gain, norm_shift, pick,
        frozen_out, frozen_up, frozen_down,
    )
    near0, sent1 = tie(near0, sent1)
    x0 = jnp.stack([near0, swap(near0, "vocab", 1)], 0).reshape(count, width)
    got1 = across(sent1)
    held1, hats1, *kept = probe_call((0,), "start", unembedding_table, loc, x0, slots, biases, norm_gain, norm_shift)
    got1, kept[-1] = tie(got1, kept[-1])
    near1 = jnp.stack([got1] + [ring(got1, o) for o in range(1, chips)], 0)
    sums1, stats1 = probe_call((0,), "rest", unembedding_table, held1, *kept)
    near1, stats1 = tie(near1, stats1)
    x1 = jnp.stack([near1, swap(near1, "vocab", 1)], 0).reshape(count, width)
    sums02, stats02, hats02 = probe_call(
        (-1, 1), "all", unembedding_table, loc, x1, slots, biases, norm_gain, norm_shift
    )
    local_stats = jnp.concatenate([stats02[0:1], stats1[0:1], stats02[1:3], stats1[1:2], stats02[3:4]], 0)
    local_stats = local_stats[:, :count]
    stats = share_stats(local_stats)
    valid = counted_in(jnp.int32(0))
    scale = valid[None, :] * jnp.exp(local_stats[:3] - stats[:3]) / stats[3:]
    scale = jnp.pad(scale, ((0, 5), (0, -(-count // 128) * 128 - count)))
    *grads, small = grad_call(dest, x0, x1, sums1, sums02, scale, hats1, hats02, norm_gain, norm_shift)

    part_shape = (rows, span * BS // pieces, BS)

    def later(small):
        def again(c):
            k, *fixed = tie(c[0], slots, unembedding_table, loc, dest)
            g, m = later_round(k, *fixed)
            return (c[0] + 1, c[1] + g.astype(f32), c[2] + m)

        start = (jnp.int32(1), jnp.zeros(part_shape, f32), small * 0.0)
        return lax.while_loop(lambda c: c[0] < rounds, again, start)[1:]

    slot_parts, small, later_parts, later_small = reduce_slots(grads, with_loss(small, valid, stats), later)
    small = small + later_small
    full = slot_parts.astype(f32) + later_parts
    loss_count = jnp.sum(masks).astype(f32)

    loss_sum = jnp.sum(small[2])
    bias_grad = small[:2]
    bias_cols = lens_bias.shape[1]
    bias_grad = lax.dynamic_slice_in_dim(bias_grad, where * bias_cols, bias_cols, 1)

    if per >= rows:
        slot_grad = full.reshape(per, BS, BS)
        turn = row * (per // rows)
    else:
        slot_grad = jnp.take(full, row ^ jnp.arange(rows), axis=0).reshape(per, BS, BS)
        turn = jnp.int32(0)

    (new_matrix, new_first, new_second, new_left, new_right, renewed_left_basis, new_rbasis) = soap_call(
        turn.reshape(1), master_matrix, slot_grad, matrix_first, matrix_second, left_stat, right_stat,
        left_basis, right_basis,
    )
    new_bias, new_bias_first, new_bias_second = adam_bias(lens_bias, bias_grad, bias_first, bias_second)
    return (
        loss_sum, loss_count, new_matrix, new_first, new_second, new_left, new_right, renewed_left_basis,
        new_rbasis, new_bias, new_bias_first, new_bias_second,
    )


def solution(mesh):
    in_specs = (
        P("rows"),
        P("rows"),
        P("rows", None),
        P(),
        P("vocab", None),
        P("vocab", None),
        P(),
        P(),
        P(),
        P(),
        P(),
        P(),
        P(),
        P("vocab", None, None),
        P(None, "vocab"),
        P("vocab", None, None),
        P("vocab", None, None),
        P("vocab", None, None),
        P("vocab", None, None),
        P("vocab", None, None),
        P("vocab", None, None),
        P(None, "vocab"),
        P(None, "vocab"),
    )
    out_specs = (
        P(),
        P(),
        P("vocab", None, None),
        P("vocab", None, None),
        P("vocab", None, None),
        P("vocab", None, None),
        P("vocab", None, None),
        P("vocab", None, None),
        P("vocab", None, None),
        P(None, "vocab"),
        P(None, "vocab"),
        P(None, "vocab"),
    )
    return jax.shard_map(body, mesh=mesh, in_specs=in_specs, out_specs=out_specs, check_vma=False)
```

```python
import functools

import jax
import jax.numpy as jnp
import numpy as np
from jax import lax
from jax.experimental import pallas as pl
from jax.experimental.pallas import tpu as pltpu
from jax.sharding import PartitionSpec as P

HEADS = 16
HEAD_DIM = 64
ROT = 16
BS = 256
STEP = 5

HIGHEST = lax.Precision.HIGHEST
NORM_EPS = 1e-05
BETA_ONE = 0.9
BETA_TWO = 0.999
BETA_STAT = 0.95
ADAM_EPS = 1e-08
MATRIX_RATE = 0.01
BIAS_RATE = 0.1
DECAY = 0.1
MASKED = -1e30
NB = 64
PIV = 2
VMEM_LIMIT = 56 * 2**20


def _mm(a,b,dims):
    return lax.dot_general(a,b,(dims,((),())),precision=HIGHEST,preferred_element_type=jnp.float32)
def mm_nn(a,b): return _mm(a,b,((1,),(0,)))
def mm_tn(a,b): return _mm(a,b,((0,),(0,)))
def mm_nt(a,b): return _mm(a,b,((1,),(1,)))
def _mb(a,b,dims):
    return lax.dot_general(a.astype(jnp.bfloat16),b.astype(jnp.bfloat16),(dims,((),())),preferred_element_type=jnp.float32)

def eliminate(rows, nb):
    rows=list(rows)
    def pick(i,c):
        return jnp.broadcast_to(rows[i][:,c:c+1],rows[i].shape)
    for j in range(0,nb,PIV):
        low=[[None]*PIV for _ in range(PIV)]
        roots=[None]*PIV
        inv=[[None]*PIV for _ in range(PIV)]
        cur=[[pick(j+p,j+q) if q<=p else None for q in range(PIV)] for p in range(PIV)]
        for q in range(PIV):
            guess=lax.rsqrt(cur[q][q])
            roots[q]=guess*(1.5-0.5*(cur[q][q]*guess)*guess)
            for p in range(q+1,PIV):
                low[p][q]=cur[p][q]*roots[q]
            for p in range(q+1,PIV):
                for t in range(q+1,p+1):
                    cur[p][t]=cur[p][t]-low[p][q]*low[t][q]
        lead=[]
        for p in range(PIV):
            acc=rows[j+p]
            for q in range(p):
                acc=acc-low[p][q]*lead[q]
            lead.append(acc*roots[p])
        back=[None]*PIV
        for p in reversed(range(PIV)):
            acc=lead[p]
            for q in range(p+1,PIV):
                acc=acc-low[q][p]*back[q]
            back[p]=acc*roots[p]
        for i in range(j+PIV,nb):
            cols=[pick(i,j+p) for p in range(PIV)]
            t=cols[0]*back[0]
            for p in range(1,PIV):
                t=t+cols[p]*back[p]
            rows[i]=rows[i]-t
        for p in range(PIV):
            rows[j+p]=lead[p]
    return rows

def soap_kernel(per, where_ref, w_ref,g_ref,first_ref,second_ref,left_ref,right_ref,lb_ref,rb_ref,
                nw_out,nf_out,ns_out,nl_out,nr_out,ql_ref,qr_ref,nw_ref,nf_ref,ns_ref,nl_ref,nr_ref,work,prods,stage,sems):
    xor=where_ref[0]
    nm=2*per
    nn=((1,),(0,)); tn=((0,),(0,)); nt=((1,),(1,))
    def slot(s,c):
        g=g_ref[s^xor].astype(jnp.float32)
        gb=g.astype(jnp.bfloat16)
        lb=lb_ref[s]; rb=rb_ref[s]
        lbb=lb.astype(jnp.bfloat16); rbb=rb.astype(jnp.bfloat16)
        rotated=_mb(_mb(lbb,gb,tn),rbb,nn)
        first=BETA_ONE*first_ref[s]+(1.0-BETA_ONE)*g
        second=BETA_TWO*second_ref[s]+(1.0-BETA_TWO)*rotated*rotated
        nf_ref[s]=first; ns_ref[s]=second
        moment=_mb(_mb(lbb,first,tn),rbb,nn)
        scaled=moment/(1.0-BETA_ONE**STEP)/(jnp.sqrt(second/(1.0-BETA_TWO**STEP))+ADAM_EPS)
        update=_mb(_mb(lbb,scaled,nn),rbb,nt)
        w=w_ref[s]
        nw_ref[s]=w-MATRIX_RATE*(update+DECAY*w)
        nl=BETA_STAT*left_ref[s]+(1.0-BETA_STAT)*_mb(gb,gb,nt)
        nr=BETA_STAT*right_ref[s]+(1.0-BETA_STAT)*_mb(gb,gb,tn)
        nl_ref[s]=nl; nr_ref[s]=nr
        pl_=mm_nn(nl,lb); pr_=mm_nn(nr,rb)
        prods[s]=pl_; prods[per+s]=pr_
        work[s]=mm_tn(pl_,pl_); work[per+s]=mm_tn(pr_,pr_)
        return c
    lax.fori_loop(0,per,slot,0,unroll=True)
    copies=[pltpu.make_async_copy(src,dst,sems.at[i]) for i,(src,dst) in enumerate(zip((nw_ref,nf_ref,ns_ref,nl_ref,nr_ref),(nw_out,nf_out,ns_out,nl_out,nr_out)))]
    for copy in copies:
        copy.start()
    lane=lax.broadcasted_iota(jnp.int32,(NB,128),1)
    row=lax.broadcasted_iota(jnp.int32,(NB,128),0)
    ident=(lane==row+NB).astype(jnp.float32)
    idrow=lax.broadcasted_iota(jnp.int32,(NB,BS),0)
    col=lax.broadcasted_iota(jnp.int32,(NB,BS),1)
    colw=lax.broadcasted_iota(jnp.int32,(BS,BS),1)
    upper=lax.broadcasted_iota(jnp.int32,(NB,NB),0)<=lax.broadcasted_iota(jnp.int32,(NB,NB),1)
    def fill(k):
        r0=k*NB
        for m in range(nm):
            d=work[m,r0:r0+NB,r0//128*128:r0//128*128+128]
            if r0%128: d=pltpu.roll(d,128-r0%128,axis=1)
            stage[m*NB:(m+1)*NB,:]=jnp.where(lane<NB,d,ident)
    def trail(k):
        r0=k*NB
        end=r0+NB
        lo=end//128*128
        inside=(col>=r0)&(col<end)
        ms=range(nm)
        linv=[stage[m*NB:(m+1)*NB,NB:2*NB] for m in ms]
        rows_m=[jnp.where(inside,(col==idrow+r0).astype(jnp.float32),work[m,r0:end,:]) for m in ms]
        b=[mm_nn(linv[m],rows_m[m]) for m in ms]
        if end<BS:
            up=[jnp.where(upper,stage[m*NB:(m+1)*NB,:NB],0.0) for m in ms]
            left=[rows_m[m][:,lo:]-mm_tn(up[m],b[m][:,lo:]) for m in ms]
            fix=[b[m][:,lo:]+mm_nn(linv[m],left[m]) for m in ms]
            b=[fix[m] if lo==0 else jnp.concatenate([b[m][:,:lo],fix[m]],1) for m in ms]
            cw=colw[:BS-end]
            rest=[mm_tn(b[m][:,lo:],b[m])[end-lo:] for m in ms]
            for m in ms:
                work[m,end:,:]=jnp.where((cw>=r0)&(cw<end),0.0,work[m,end:,:])-rest[m]
        for m in ms:
            work[m,r0:end,:]=b[m]
    def step(kb,c):
        for k in range(BS//NB):
            @pl.when(kb==k)
            def _(k=k):
                fill(k)
        rows=[stage[pl.ds(i,nm,stride=NB),:] for i in range(NB)]
        rows=eliminate(rows,NB)
        for i in range(NB):
            stage[pl.ds(i,nm,stride=NB),:]=rows[i]
        for k in range(BS//NB):
            @pl.when(kb==k)
            def _(k=k):
                trail(k)
        return c
    lax.fori_loop(0,BS//NB,step,0)
    roww=lax.broadcasted_iota(jnp.int32,(BS,BS),0)
    weight=jnp.where(roww>colw,1.0,jnp.where(roww==colw,0.5,0.0))
    unit=(roww==colw).astype(jnp.float32)
    outs=[(ql_ref,s) for s in range(per)]+[(qr_ref,s) for s in range(per)]
    bases=[mm_nt(prods[m],jnp.where(roww>=colw,work[m],0.0)) for m in range(nm)]
    for turn in range(2):
        gaps=[((mm_tn(q,q) if turn else _mb(q,q,tn))-unit)*weight for q in bases]
        bases=[q-_mb(q,gap,nt) for q,gap in zip(bases,gaps)]
    for (ref,s),q in zip(outs,bases):
        ref[s]=q
    for copy in copies:
        copy.wait()

def soap_call(xor,w,g,first,second,left,right,lb,rb):
    per=w.shape[0]
    sh=jax.ShapeDtypeStruct((per,BS,BS),jnp.float32)
    vm=pl.BlockSpec(memory_space=pltpu.VMEM)
    return pl.pallas_call(functools.partial(soap_kernel,per),
        out_shape=[sh]*7,
        in_specs=[pl.BlockSpec(memory_space=pltpu.SMEM)]+[vm]*8, out_specs=[pl.BlockSpec(memory_space=pl.ANY)]*5+[vm]*2,
        scratch_shapes=[pltpu.VMEM((per,BS,BS),jnp.float32)]*5+[pltpu.VMEM((2*per,BS,BS),jnp.float32),pltpu.VMEM((2*per,BS,BS),jnp.float32),pltpu.VMEM((2*per*NB,128),jnp.float32),pltpu.SemaphoreType.DMA((5,))],
        compiler_params=pltpu.CompilerParams(vmem_limit_bytes=48*2**20),
        name="soap_update")(xor,w,g,first,second,left,right,lb,rb)


def adam_bias(bias, grad, first, second):
    first_new = BETA_ONE * first + (1.0 - BETA_ONE) * grad
    second_new = BETA_TWO * second + (1.0 - BETA_TWO) * grad * grad
    scaled = (
        first_new
        / (1.0 - BETA_ONE**STEP)
        / (jnp.sqrt(second_new / (1.0 - BETA_TWO**STEP)) + ADAM_EPS)
    )
    return (bias - BIAS_RATE * scaled, first_new, second_new)


def places(index, seq_lens):
    ends = jnp.cumsum(seq_lens)
    segment = jnp.sum((index[:, None] >= ends[None, :]).astype(jnp.int32), 1)
    starts = ends - seq_lens
    picked = segment[:, None] == jnp.arange(seq_lens.shape[0], dtype=jnp.int32)[None, :]
    offset = jnp.sum(jnp.where(picked, starts[None, :], 0), 1)
    return (segment, index - offset)


def swap(x, axis, bit):
    size = lax.axis_size(axis)
    return lax.ppermute(x, axis, [(i, i ^ bit) for i in range(size)])


def gather_xor(x, axis, bits):
    out = x[None]
    for bit in bits:
        out = jnp.concatenate([out, swap(out, axis, bit)], 0)
    return out


def bits_of(size):
    return [1 << i for i in range(size.bit_length() - 1)]


def chip_bits(size):
    return bits_of(size)[1:][::-1] + [1]


def entry_ids(bits):
    ids = [0]
    for bit in bits:
        ids = ids + [i ^ bit for i in ids]
    return ids


def normalize(x, gain, shift):
    centred = x - jnp.mean(x, -1, keepdims=True)
    root = lax.rsqrt(jnp.mean(centred * centred, -1, keepdims=True) + NORM_EPS)
    return centred * root * gain + shift


def turned(x, cos, sin):
    width = x.shape[1]
    lane = lax.broadcasted_iota(jnp.int32, (1, width), 1)
    swapped = jnp.where(
        lane % HEAD_DIM < ROT // 2,
        pltpu.roll(x, width - ROT // 2, axis=1),
        pltpu.roll(x, ROT // 2, axis=1),
    )
    reps = width // cos.shape[1]
    return x * jnp.concatenate([cos] * reps, 1) + swapped * jnp.concatenate([sin] * reps, 1)


def fill_pool(bufs, pool, sems):
    take = bufs[0].shape[0]
    return [
        pltpu.make_async_copy(buf, pool.at[i * take : (i + 1) * take, :], sems.at[i])
        for i, buf in enumerate(bufs)
    ]


def placed(pool, column):
    spread = lax.broadcasted_iota(jnp.int32, (column.shape[0], pool.shape[0]), 1) == column
    return jnp.dot(spread.astype(jnp.bfloat16), pool[...], preferred_element_type=jnp.float32)


def deal(pick, x, outs):
    sent = jnp.dot(pick[...], x, preferred_element_type=jnp.float32).astype(jnp.bfloat16)
    n = sent.shape[0] // len(outs)
    for e, out in enumerate(outs):
        out[...] = sent[e * n : (e + 1) * n]


def place_kernel(parts, where_ref, *refs):
    bufs = refs[:parts]
    meta, pick, own_out, *sent_out, pool, sems = refs[parts:]
    own = own_out.shape[0]
    fills = fill_pool(bufs, pool, sems)
    for fill in fills:
        fill.start()
    for fill in fills:
        fill.wait()
    mine = pl.ds(pl.multiple_of(where_ref[0] * own, own), own)
    x = placed(pool, meta[mine, 0:1])
    x = x.astype(jnp.bfloat16)
    own_out[...] = x
    deal(pick, x, sent_out)


def place_call(dealt_to, where, bufs, meta, pick):
    take, width = bufs[0].shape
    parts = len(bufs)
    own = pick.shape[1]
    vm = pl.BlockSpec(memory_space=pltpu.VMEM)
    hbm = pl.BlockSpec(memory_space=pl.ANY)
    bf = jnp.bfloat16
    return pl.pallas_call(
        functools.partial(place_kernel, parts),
        out_shape=[
            jax.ShapeDtypeStruct((own, width), bf),
            *[jax.ShapeDtypeStruct((pick.shape[0] // dealt_to, width), bf)] * dealt_to,
        ],
        in_specs=[pl.BlockSpec(memory_space=pltpu.SMEM)] + [hbm] * parts + [vm, vm],
        out_specs=[vm] * (1 + dealt_to),
        scratch_shapes=[pltpu.VMEM((parts * take, width), bf), pltpu.SemaphoreType.DMA((parts,))],
        compiler_params=pltpu.CompilerParams(vmem_limit_bytes=VMEM_LIMIT),
        cost_estimate=pl.CostEstimate(flops=10**9, bytes_accessed=4 * 2**20, transcendentals=0),
        name="place_rows",
    )(where, *bufs, meta, pick)


def project_kernel(parts, where_ref, *refs):
    bufs = refs[:parts]
    (meta, cosines, sines, bias, gain, shift, qkv, k_out, v_out, q_out, pool, emb, w_qkv,
     sems) = refs[parts:]
    group, width = k_out.shape
    own = q_out.shape[0]
    fills = fill_pool(bufs, pool, sems)
    loads = [
        pltpu.make_async_copy(qkv.at[:, i * width : (i + 1) * width], w_qkv.at[i], sems.at[parts + i])
        for i in range(3)
    ]
    for fill in fills:
        fill.start()
    for i in (1, 2, 0):
        loads[i].start()
    for fill in fills:
        fill.wait()
    rows = 256

    def attn_in(x):
        return normalize(x.astype(jnp.float32), gain[0:1, :], shift[0:1, :]).astype(jnp.bfloat16)

    loads[1].wait()
    loads[2].wait()

    def project(i, c):
        at = pl.ds(pl.multiple_of(i * rows, rows), rows)

        x = placed(pool, meta[at, 0:1]).astype(jnp.bfloat16)
        emb[at, :] = x
        y = attn_in(x)
        k = jnp.dot(y, w_qkv[1], preferred_element_type=jnp.float32) + bias[:, width : 2 * width]
        k_out[at, :] = turned(k, cosines[at, :], sines[at, :]).astype(jnp.bfloat16)
        v = jnp.dot(y, w_qkv[2], preferred_element_type=jnp.float32)
        v_out[at, :] = (v + bias[:, 2 * width : 3 * width]).astype(jnp.bfloat16)
        return c

    lax.fori_loop(0, group // rows, project, 0)
    mine = pl.ds(pl.multiple_of(where_ref[0] * own, own), own)
    loads[0].wait()
    q = jnp.dot(attn_in(emb[mine, :]), w_qkv[0], preferred_element_type=jnp.float32)
    q = turned(q + bias[:, :width], cosines[mine, :], sines[mine, :])
    q_out[...] = q.astype(jnp.bfloat16)


def project_call(own, where, bufs, meta, cosines, sines, bias, gain, shift, qkv):
    group = meta.shape[0]
    take, width = bufs[0].shape
    parts = len(bufs)
    vm = pl.BlockSpec(memory_space=pltpu.VMEM)
    hbm = pl.BlockSpec(memory_space=pl.ANY)
    bf = jnp.bfloat16
    return pl.pallas_call(
        functools.partial(project_kernel, parts),
        out_shape=[
            jax.ShapeDtypeStruct((group, width), bf),
            jax.ShapeDtypeStruct((group, width), bf),
            jax.ShapeDtypeStruct((own, width), bf),
        ],
        in_specs=[pl.BlockSpec(memory_space=pltpu.SMEM)] + [hbm] * parts + [vm] * 6 + [hbm],
        out_specs=[vm] * 3,
        scratch_shapes=[
            pltpu.VMEM((parts * take, width), bf),
            pltpu.VMEM((group, width), bf),
            pltpu.VMEM((3, width, width), bf),
            pltpu.SemaphoreType.DMA((parts + 3,)),
        ],
        compiler_params=pltpu.CompilerParams(vmem_limit_bytes=VMEM_LIMIT),
        cost_estimate=pl.CostEstimate(flops=12 * 10**9, bytes_accessed=16 * 2**20, transcendentals=0),
        name="project_group",
    )(where, *bufs, meta, cosines, sines, bias, gain, shift, qkv)


def layer_kernel(
    chunks, where_ref, k_all, v_all, q_own, emb, meta, key_meta, bias, gain, shift, pick,
    w_out, w_up, w_down, out, *refs,
):
    *sent_out, wo, up, down, mix, sems = refs
    own, width = emb.shape
    units = w_up.shape[1]
    part = units // chunks
    nbuf = up.shape[0]

    def load(j):
        n = j % nbuf
        return (
            pltpu.make_async_copy(w_up.at[:, j * part : (j + 1) * part], up.at[n], sems.at[1 + n]),
            pltpu.make_async_copy(
                w_down.at[j * part : (j + 1) * part, :], down.at[n], sems.at[1 + nbuf + n]
            ),
        )

    load_out = pltpu.make_async_copy(w_out, wo, sems.at[0])
    load_out.start()
    for j in range(nbuf):
        for copy in load(j):
            copy.start()

    mine = pl.ds(pl.multiple_of(where_ref[0] * own, own), own)
    allowed = (meta[mine, 1:2] == key_meta[0:1, :]) & (key_meta[1:2, :] <= meta[mine, 2:3])
    half = lax.broadcasted_iota(jnp.int32, (1, 2 * HEAD_DIM), 1) // HEAD_DIM

    def pair(hp, c):
        at = pl.ds(pl.multiple_of(hp * 2 * HEAD_DIM, 2 * HEAD_DIM), 2 * HEAD_DIM)
        qp, kp, vp = q_own[:, at], k_all[:, at], v_all[:, at]
        outs = []
        for h in range(2):
            qh = jnp.where(half == h, qp, jnp.zeros((), jnp.bfloat16))
            scores = lax.dot_general(
                qh, kp, (((1,), (1,)), ((), ())), preferred_element_type=jnp.float32
            )
            scores = jnp.where(allowed, scores * HEAD_DIM ** (-0.5), MASKED)
            weights = jnp.exp(scores - jnp.max(scores, -1, keepdims=True))
            total = jnp.sum(weights, -1, keepdims=True)
            got = jnp.dot(weights.astype(jnp.bfloat16), vp, preferred_element_type=jnp.float32)
            outs.append(got / total)
        mix[:, at] = jnp.where(half == 0, outs[0], outs[1]).astype(jnp.bfloat16)
        return c

    lax.fori_loop(0, HEADS // 2, pair, 0)
    x_own = emb[...].astype(jnp.float32)
    load_out.wait()
    total = x_own + (
        jnp.dot(mix[...], wo[...], preferred_element_type=jnp.float32)
        + bias[:, 3 * width : 4 * width]
    )
    mlp_in = normalize(x_own, gain[1:2, :], shift[1:2, :]).astype(jnp.bfloat16)
    acc = jnp.zeros((own, width), jnp.float32)
    for j in range(chunks):
        for copy in load(j):
            copy.wait()
        lo = 4 * width + j * part
        pre = jnp.dot(mlp_in, up[j % nbuf], preferred_element_type=jnp.float32)
        pre = pre + bias[:, lo : lo + part]
        activ = (0.5 * pre * (1.0 + lax.erf(pre * 0.7071067811865476))).astype(jnp.bfloat16)
        acc = acc + jnp.dot(activ, down[j % nbuf], preferred_element_type=jnp.float32)
        if j + nbuf < chunks:
            for copy in load(j + nbuf):
                copy.start()
    low = (total + (acc + bias[:, 4 * width + units :])).astype(jnp.bfloat16)
    out[...] = low
    deal(pick, low, sent_out)


def layer_call(dealt_to, where, k, v, q, emb, meta, key_meta, bias, gain, shift, pick, w_out, w_up, w_down):
    group, width = k.shape
    own = emb.shape[0]
    units = w_up.shape[1]
    chunks = units // width
    nbuf = chunks if group <= 1024 else 2
    vm = pl.BlockSpec(memory_space=pltpu.VMEM)
    hbm = pl.BlockSpec(memory_space=pl.ANY)
    bf = jnp.bfloat16
    return pl.pallas_call(
        functools.partial(layer_kernel, chunks),
        out_shape=[
            jax.ShapeDtypeStruct((own, width), bf),
            *[jax.ShapeDtypeStruct((pick.shape[0] // dealt_to, width), bf)] * dealt_to,
        ],
        in_specs=[pl.BlockSpec(memory_space=pltpu.SMEM)] + [vm] * 10 + [hbm] * 3,
        out_specs=[vm] * (1 + dealt_to),
        scratch_shapes=[
            pltpu.VMEM((width, width), bf),
            pltpu.VMEM((nbuf, width, units // chunks), bf),
            pltpu.VMEM((nbuf, units // chunks, width), bf),
            pltpu.VMEM((own, width), bf),
            pltpu.SemaphoreType.DMA((1 + 2 * nbuf,)),
        ],
        compiler_params=pltpu.CompilerParams(vmem_limit_bytes=VMEM_LIMIT),
        cost_estimate=pl.CostEstimate(flops=12 * 10**9, bytes_accessed=24 * 2**20, transcendentals=0),
        name="frozen_layer",
    )(where, k, v, q, emb, meta, key_meta, bias, gain, shift, pick, w_out, w_up, w_down)


def probe_kernel(limit, sets, chunks, kind, first, *refs):
    if kind == "rest":
        sums_in, normed, peak_in, mass_in, table, sums, stats, peak, mass = refs
    elif kind == "start":
        loc_ref, x, slots, bias, gain, shift, table, sums, hats, normed, peak, mass = refs
    else:
        loc_ref, x, slots, bias, gain, shift, table, sums, stats, hats, normed, peak, mass = refs
    begins = pl.program_id(0) == 0
    step = pl.program_id(0) + first
    tile, width = table.shape
    steps = -(-limit // tile)
    count = chunks * normed.shape[1] // len(sets)
    nblk = width // BS
    size = count // chunks
    many = len(sets)

    def start():
        def save(i, rows, v):
            centred = v - jnp.mean(v, -1, keepdims=True)
            root = lax.rsqrt(jnp.mean(centred * centred, -1, keepdims=True) + NORM_EPS)
            hat = centred * root
            normed[rows // size, i * size : (i + 1) * size, :] = (
                hat * gain[2:3, :] + shift[2:3, :]
            ).astype(jnp.bfloat16)
            return hat, root

        for c in range(chunks):
            rows = c * size
            raw = x[rows : rows + size, :]
            v = raw.astype(jnp.float32)
            for i, k in enumerate(sets):
                if k < 0:
                    hat, root = save(i, rows, v)
                else:
                    cols = []
                    for j in range(nblk):
                        total = None
                        for b in range(nblk):
                            term = jnp.dot(
                                raw[:, b * BS : (b + 1) * BS],
                                slots[loc_ref[(k * nblk + b) * nblk + j], :BS, :],
                                preferred_element_type=jnp.float32,
                            )
                            total = term if total is None else total + term
                        cols.append(total)
                    hat, root = save(i, rows, v + jnp.concatenate(cols, 1) + bias[k : k + 1, :])
                hats[i, rows : rows + size, :width] = hat
                hats[i, rows : rows + size, width:] = jnp.broadcast_to(root, (size, 128))
        peak[...] = jnp.full(peak.shape, MASKED, jnp.float32)
        mass[...] = jnp.zeros(mass.shape, jnp.float32)
        sums[...] = jnp.zeros(sums.shape, jnp.float32)

    def resume():
        peak[...] = peak_in[...]
        mass[...] = mass_in[...]
        sums[...] = sums_in[...]

    pl.when(begins)(resume if kind == "rest" else start)

    def visit(last):
        w = table[...]
        if last:
            left = limit - step * tile
            at = lax.broadcasted_iota(jnp.int32, (1, tile), 1)
            down = lax.broadcasted_iota(jnp.int32, (tile, 1), 0)
            w = jnp.where(down < left, w, jnp.zeros((), jnp.bfloat16))

        def score(c):
            return lax.dot_general(
                normed[c], w, (((1,), (1,)), ((), ())), preferred_element_type=jnp.float32
            )

        ready = score(0)
        for c in range(chunks):
            logits = ready
            if c + 1 < chunks:
                ready = score(c + 1)
            if last:
                logits = jnp.where(at < left, logits, MASKED)
            old = peak[c]
            new = jnp.maximum(old, jnp.max(logits, -1, keepdims=True))
            fade = jnp.exp(old - new)
            powers = jnp.exp(logits - new)
            peak[c] = new
            mass[c] = mass[c] * fade + jnp.sum(powers, -1, keepdims=True)
            sums[c] = sums[c] * fade + jnp.dot(
                powers.astype(jnp.bfloat16), w, preferred_element_type=jnp.float32
            )

    def finish():
        visit(True)
        lanes = -(-count // 128) * 128
        at = lax.broadcasted_iota(jnp.int32, (lanes, 128), 1)
        packed = jnp.zeros((lanes, 128), jnp.float32)
        for i in range(many):
            for n, ref in ((i, peak), (many + i, mass)):
                col = [ref[c, i * size : (i + 1) * size, :] for c in range(chunks)]
                if lanes > count:
                    col.append(jnp.zeros((lanes - count, 1), jnp.float32))
                packed = jnp.where(at == n, jnp.concatenate(col, 0), packed)
        stats[...] = jnp.transpose(packed)[:8, :]

    if kind == "start":
        visit(False)
    else:
        pl.when(step < steps - 1)(lambda: visit(False))
        pl.when(step == steps - 1)(finish)


def probe_call(sets, kind, table, *given):
    vocab, width = table.shape
    tile = 1280
    steps = -(-vocab // tile)
    ahead = -(-steps // 2)
    first, todo = {"all": (0, steps), "start": (0, ahead), "rest": (ahead, steps - ahead)}[kind]
    many = len(sets)
    f32 = jnp.float32
    if kind == "rest":
        chunks, rows = given[0].shape[:2]
        size = rows // many
    else:
        count = given[1].shape[0]
        chunks = many if count % (16 * many) == 0 else 1
        size = count // chunks
    count = chunks * size
    vm = pl.BlockSpec(memory_space=pltpu.VMEM)
    column = (chunks, many * size, 1)
    sums = jax.ShapeDtypeStruct((chunks, many * size, width), f32)
    stats = jax.ShapeDtypeStruct((8, -(-count // 128) * 128), f32)
    hats = jax.ShapeDtypeStruct((many, count, width + 128), f32)
    scratch = [pltpu.VMEM(column, f32), pltpu.VMEM(column, f32)]
    if kind == "rest":
        outs, ins = [sums, stats], [vm] * 4
    else:
        ins = [pl.BlockSpec(memory_space=pltpu.SMEM)] + [vm] * 5
        normed = (chunks, many * size, width)
        if kind == "start":
            col = jax.ShapeDtypeStruct(column, f32)
            outs, scratch = [sums, hats, jax.ShapeDtypeStruct(normed, jnp.bfloat16), col, col], []
        else:
            outs, scratch = [sums, stats, hats], [pltpu.VMEM(normed, jnp.bfloat16)] + scratch
    return pl.pallas_call(
        functools.partial(probe_kernel, vocab, sets, chunks, kind, first),
        grid=(todo,),
        out_shape=outs,
        in_specs=ins + [pl.BlockSpec((tile, width), lambda i: (i + first, 0))],
        out_specs=[vm] * len(outs),
        scratch_shapes=scratch,
        compiler_params=pltpu.CompilerParams(vmem_limit_bytes=VMEM_LIMIT),
        cost_estimate=pl.CostEstimate(
            flops=4 * many * count * todo * tile * width, bytes_accessed=2 * todo * tile * width, transcendentals=0
        ),
        name="probe_" + kind,
    )(*given, table)


def grad_kernel(
    dest_ref, x0, x1, sums1, sums02, scale, hats1, hats02, gain, shift, stay, go, small,
    grads, sems,
):
    count, width = x0.shape
    nblk = width // BS
    pieces = dest_ref.shape[1]
    rows = BS // pieces
    chunks = sums02.shape[0]
    size = count // chunks
    cols = jnp.transpose(jnp.concatenate([scale[...]] * (128 // scale.shape[0]), 0))[:count]
    gain_row, shift_row = gain[2:3, :], shift[2:3, :]

    def normed(hat):
        return (hat * gain_row + shift_row).astype(jnp.bfloat16).astype(jnp.float32)

    def parts(n):
        return jnp.concatenate([sums02[c, n * size : (n + 1) * size, :] for c in range(chunks)], 0)

    base = parts(0) * cols[:, 0:1]
    target = normed(hats02[0, :, :width])
    spread = jnp.zeros((1, width), jnp.float32)
    for k in range(2):
        own = sums1[...].reshape(count, width) if k == 0 else parts(1)
        hats = hats1.at[0] if k == 0 else hats02.at[1]
        hat = hats[:, :width]
        root = hats[:, width : width + 1]
        spread = spread + jnp.sum(base * (target - normed(hat)), 0, keepdims=True)
        e = (own * cols[:, k + 1 : k + 2] - base) * gain_row
        pulled = e - jnp.mean(e, -1, keepdims=True)
        pulled = (pulled - hat * jnp.mean(e * hat, -1, keepdims=True)) * root
        small[k : k + 1, :] = jnp.sum(pulled, 0, keepdims=True)
        low = pulled.astype(jnp.bfloat16)
        x = x0 if k == 0 else x1
        for i in range(nblk):
            full = lax.dot_general(
                x[:, i * BS : (i + 1) * BS], low, (((0,), (0,)), ((), ())),
                preferred_element_type=jnp.float32,
            ).astype(jnp.bfloat16)
            for j in range(nblk):
                b = (k * nblk + i) * nblk + j
                for p in range(pieces):
                    piece = full[p * rows : (p + 1) * rows, j * BS : (j + 1) * BS]
                    grads[dest_ref[b, p]] = piece
    half = grads.shape[0] // 2
    copies = [
        pltpu.make_async_copy(grads.at[:half], stay, sems.at[0]),
        pltpu.make_async_copy(grads.at[half:], go, sems.at[1]),
    ]
    for copy in copies[::-1]:
        copy.start()
    small[2:3, :] = spread
    small[3:, :] = jnp.zeros((5, width), jnp.float32)
    for copy in copies:
        copy.wait()


def grad_call(dest, x0, x1, sums1, sums02, scale, hats1, hats02, gain, shift):
    width = x0.shape[1]
    pieces = dest.shape[1]
    vm = pl.BlockSpec(memory_space=pltpu.VMEM)
    hbm = pl.BlockSpec(memory_space=pl.ANY)
    half = jax.ShapeDtypeStruct((dest.shape[0] * pieces // 2, BS // pieces, BS), jnp.bfloat16)
    return pl.pallas_call(
        grad_kernel,
        out_shape=[
            half,
            half,
            jax.ShapeDtypeStruct((8, width), jnp.float32),
        ],
        in_specs=[pl.BlockSpec(memory_space=pltpu.SMEM)] + [vm] * 9,
        out_specs=[hbm, hbm, vm],
        scratch_shapes=[
            pltpu.VMEM((dest.shape[0] * pieces, BS // pieces, BS), jnp.bfloat16),
            pltpu.SemaphoreType.DMA((2,)),
        ],
        compiler_params=pltpu.CompilerParams(vmem_limit_bytes=VMEM_LIMIT),
        cost_estimate=pl.CostEstimate(flops=4 * 10**9, bytes_accessed=16 * 2**20, transcendentals=0),
        name="lens_gradient",
    )(dest, x0, x1, sums1, sums02, scale, hats1, hats02, gain, shift)


def merge(a, b):
    peak = jnp.maximum(a[:3], b[:3])
    return jnp.concatenate([peak, a[3:] * jnp.exp(a[:3] - peak) + b[3:] * jnp.exp(b[:3] - peak)], 0)


def ring(x, step):
    size = lax.axis_size("vocab")
    return lax.ppermute(x, "vocab", [(i, (i + 2 * step) % size) for i in range(size)])


def add(*terms):
    total = terms[0].astype(jnp.float32)
    for term in terms[1:]:
        total = total + term.astype(jnp.float32)
    return total.astype(terms[0].dtype)


def pace_kernel(x, out):
    out[...] = x[...]


def pace(x):
    vm = pl.BlockSpec(memory_space=pltpu.VMEM)
    return pl.pallas_call(
        pace_kernel,
        out_shape=jax.ShapeDtypeStruct((x.size // 128, 128), x.dtype),
        in_specs=[vm],
        out_specs=vm,
        cost_estimate=pl.CostEstimate(flops=6 * 10**10, bytes_accessed=2 * 10**8, transcendentals=0),
        name="pace",
    )(x.reshape(-1, 128)).reshape(x.shape)


def spread_group(x):
    chips = lax.axis_size("vocab") // 2
    near = jnp.stack([x] + [ring(x, o) for o in range(1, chips)], 0)
    return jnp.stack([near, swap(near, "vocab", 1)], 0)


def tie(*values):
    return lax.optimization_barrier(values)


def reduce_slots(grads, small):
    chips, rows = lax.axis_size("vocab") // 2, lax.axis_size("rows")
    bits = bits_of(rows)
    todo = [("rows", bit) for bit in bits] + [("vocab", bit) for bit in chip_bits(2 * chips)]

    def small_step(small):
        axis, bit = todo.pop(0)
        return small + swap(small, axis, bit)

    g = add(grads[0], swap(grads[1], "vocab", 1)).reshape(2, rows, chips // 2, -1, BS)
    g, small = tie(g, small)
    sides = [[g[side, e] for e in range(rows)] for side in range(2)]
    for at in range(len(bits)):
        for side in range(2):
            bit = (bits[::-1], bits)[side][at]
            h = sides[side]
            keep = [e for e in range(rows) if h[e] is not None and not e & bit]
            got = swap(jnp.stack([h[e | bit] for e in keep], 0), "rows", bit)
            sides[side] = [None] * rows
            for i, e in enumerate(keep):
                sides[side][e] = add(h[e], got[i])
        if todo:
            small = small_step(small)
        live = [[e for e in range(rows) if sides[side][e] is not None] for side in range(2)]
        flat = tie(small, *[sides[side][e] for side in range(2) for e in live[side]])
        small, flat = flat[0], list(flat[1:])
        for side in range(2):
            for e in live[side]:
                sides[side][e] = flat.pop(0)
    g = jnp.concatenate([sides[0][0], sides[1][0]], 0)
    mine = add(g[0], *[ring(g[o], o) for o in range(1, chips)])
    small = small_step(small)
    mine, small = tie(mine, small)
    parts = jnp.stack([mine] + [swap(mine, "rows", e) for e in range(1, rows)], 0)
    small = small_step(small)
    parts, small = tie(parts, small)
    while todo:
        small = small_step(small)
    return parts, small


def layer_norm(values, gain_row, shift_row):
    centred = values - jnp.mean(values, -1, keepdims=True)
    spread = jnp.mean(centred * centred, -1, keepdims=True)
    return centred * lax.rsqrt(spread + NORM_EPS) * gain_row + shift_row


def rotate(heads_in, position):
    half = ROT // 2
    freq = 10000.0 ** (-2.0 * jnp.arange(half, dtype=jnp.float32) / ROT)
    angle = position.astype(jnp.float32)[:, None] * freq[None, :]
    cosine = jnp.cos(angle)[:, None, :]
    sine = jnp.sin(angle)[:, None, :]
    first_half = heads_in[..., :half]
    second_half = heads_in[..., half:ROT]
    return jnp.concatenate(
        [
            first_half * cosine - second_half * sine,
            second_half * cosine + first_half * sine,
            heads_in[..., ROT:],
        ],
        -1,
    )


def partial_sums(logits, highest):
    shifted = jnp.exp(logits - highest[..., None])
    sums = jnp.sum(shifted, -1)
    cross = jnp.sum(shifted[..., :1, :] * (logits[..., :1, :] - logits[..., 1:, :]), -1)
    return (sums, cross)


def slope_terms(part_logits, part_norms, partition_count):
    target = jnp.exp(part_logits[:, :1] - part_norms[:, :1, None])
    probes = jnp.exp(part_logits[:, 1:] - part_norms[:, 1:, None])
    return (partition_count[:, None, None] * (probes - target)).astype(jnp.bfloat16)


def dense_path(
    tokens, loss_position_mask, lengths, owners, embed_in, unembedding_table, frozen_qkv, frozen_out,
    frozen_up, frozen_down, frozen_bias, norm_gain, norm_shift, master_matrix, lens_bias,
):
    width = embed_in.shape[1]
    shards = lax.axis_size("vocab")
    where = lax.axis_index("vocab")
    group = tokens.shape[0]
    own = group // shards
    units = frozen_up.shape[1]
    nblk = width // BS
    gathered, biases = (
        lax.all_gather(master_matrix, "vocab", axis=0, tiled=True),
        lax.all_gather(lens_bias, "vocab", axis=1, tiled=True),
    )
    order = jnp.argsort(owners)
    matrices = (
        jnp.take(gathered, order, axis=0)
        .reshape(2, nblk, nblk, BS, BS)
        .transpose(0, 1, 3, 2, 4)
        .reshape(2, width, width)
    )
    table_rows = embed_in.shape[0]
    local_ids = tokens - where * table_rows
    inside = (local_ids >= 0) & (local_ids < table_rows)
    looked = jnp.take(embed_in, jnp.clip(local_ids, 0, table_rows - 1), axis=0)
    looked = jnp.where(inside[:, None], looked, jnp.zeros((), jnp.bfloat16))
    embedded = lax.psum_scatter(looked, "vocab", scatter_dimension=0, tiled=True).astype(
        jnp.float32
    )
    seq_lens = lengths[0]
    index = where * own + jnp.arange(own, dtype=jnp.int32)
    segment, position = places(index, seq_lens)
    attn_in = layer_norm(embedded, norm_gain[0], norm_shift[0]).astype(jnp.bfloat16)
    mlp_in = layer_norm(embedded, norm_gain[1], norm_shift[1]).astype(jnp.bfloat16)
    projected = (
        jnp.dot(attn_in, frozen_qkv, preferred_element_type=jnp.float32) + frozen_bias[: 3 * width]
    )
    queries = rotate(projected[:, :width].reshape(own, HEADS, HEAD_DIM), position).astype(
        jnp.bfloat16
    )
    keys = rotate(projected[:, width : 2 * width].reshape(own, HEADS, HEAD_DIM), position).astype(
        jnp.bfloat16
    )
    values = projected[:, 2 * width :].astype(jnp.bfloat16)
    key_value = jnp.concatenate([keys.reshape(own, width), values], 1)
    piece = lax.all_gather(key_value, "vocab", axis=0, tiled=True)
    highest = jnp.full((HEADS, own), MASKED, jnp.float32)
    count = piece.shape[0]
    key_index = jnp.arange(count, dtype=jnp.int32)
    key_segment, _ = places(key_index, seq_lens)
    piece_keys = piece[:, :width].reshape(count, HEADS, HEAD_DIM)
    piece_values = piece[:, width:].reshape(count, HEADS, HEAD_DIM)
    attention_scores = jnp.einsum(
        "qhd,khd->hqk", queries, piece_keys, preferred_element_type=jnp.float32
    ) * HEAD_DIM ** (-0.5)
    allowed = (segment[:, None] == key_segment[None, :]) & (key_index[None, :] <= index[:, None])
    attention_scores = jnp.where(allowed[None], attention_scores, MASKED)
    new_high = jnp.maximum(highest, jnp.max(attention_scores, -1))
    weights = jnp.where(allowed[None], jnp.exp(attention_scores - new_high[..., None]), 0.0)
    totals = jnp.sum(weights, -1)
    accum = jnp.einsum(
        "hqk,khd->hqd",
        weights.astype(jnp.bfloat16),
        piece_values,
        preferred_element_type=jnp.float32,
    )
    highest, totals, accum = (new_high, totals, accum)
    mixed = (
        jnp.transpose(accum / totals[..., None], (1, 0, 2)).reshape(own, width).astype(jnp.bfloat16)
    )
    attn_out = (
        jnp.dot(mixed, frozen_out, preferred_element_type=jnp.float32)
        + frozen_bias[3 * width : 4 * width]
    )
    activ = jax.nn.gelu(
        jnp.dot(mlp_in, frozen_up, preferred_element_type=jnp.float32)
        + frozen_bias[4 * width : 4 * width + units],
        approximate=False,
    ).astype(jnp.bfloat16)
    layer_out = (
        embedded
        + attn_out
        + (
            jnp.dot(activ, frozen_down, preferred_element_type=jnp.float32)
            + frozen_bias[4 * width + units :]
        )
    )

    def final_norm(values_in):
        return layer_norm(values_in, norm_gain[2], norm_shift[2])

    sources = (embedded.astype(jnp.bfloat16), layer_out.astype(jnp.bfloat16))
    residual = (embedded, layer_out)
    normed = [final_norm(layer_out).astype(jnp.bfloat16)]
    pulls = []
    for which in range(2):
        product = jnp.dot(
            sources[which], matrices[which].astype(jnp.bfloat16), preferred_element_type=jnp.float32
        )
        lensed = residual[which] + product + biases[which]
        normed_out, pull = jax.vjp(final_norm, lensed)
        normed.append(normed_out.astype(jnp.bfloat16))
        pulls.append(pull)
    counted = loss_position_mask.astype(jnp.float32)
    vocab_cols = unembedding_table.shape[0]
    every = lax.all_gather(jnp.stack(normed), "vocab", axis=1, tiled=True)
    size = min(512, group)
    count = group // size
    blocks = every.reshape(3, count, size, width).transpose(1, 0, 2, 3)

    def block_high(normed_blk):
        logits_blk = jnp.einsum(
            "kbd,vd->bkv", normed_blk, unembedding_table, preferred_element_type=jnp.float32
        )
        return (logits_blk, jnp.max(logits_blk, -1))

    logits, highest = lax.map(block_high, blocks)
    highest = lax.pmax(highest.reshape(group, 3), "vocab")

    def block_sums(args):
        return partial_sums(args[0], args[1])

    sums, cross = lax.map(block_sums, (logits, highest.reshape(count, size, 3)))
    logits = logits.reshape(group, 3, vocab_cols)
    sums, cross = lax.psum((sums.reshape(group, 3), cross.reshape(group, 2)), "vocab")
    log_total = highest + jnp.log(sums)
    diverge = cross / sums[:, :1] - log_total[:, :1] + log_total[:, 1:]
    loss_sum, loss_count = lax.psum((jnp.sum(counted[:, None] * diverge), jnp.sum(counted)), "rows")
    loss_slope = slope_terms(logits, log_total, counted)
    dnormed = lax.psum_scatter(
        jnp.einsum(
            "yzq,qa->yza", loss_slope, unembedding_table, preferred_element_type=jnp.float32
        ),
        "vocab",
        scatter_dimension=0,
        tiled=True,
    )
    grads = []
    bias_grads = []
    for which in range(2):
        dlensed = pulls[which](dnormed[:, which])[0]
        bias_grads.append(jnp.sum(dlensed, 0))
        grads.append(
            jnp.einsum(
                "nd,ne->de",
                sources[which],
                dlensed.astype(jnp.bfloat16),
                preferred_element_type=jnp.float32,
            )
        )
    matrix_grad = (
        jnp.stack(grads).reshape(2, nblk, BS, nblk, BS).transpose(0, 1, 3, 2, 4).reshape(-1, BS, BS)
    )
    slot_grad = jnp.take(matrix_grad, owners, axis=0)
    bias_grad = jnp.stack(bias_grads)
    per_dev = master_matrix.shape[0]
    bias_cols = lens_bias.shape[1]
    slot_grad, bias_grad = lax.psum((slot_grad, bias_grad), ("rows", "vocab"))
    slot_grad = lax.dynamic_slice_in_dim(slot_grad, where * per_dev, per_dev, 0)
    bias_grad = lax.dynamic_slice_in_dim(bias_grad, where * bias_cols, bias_cols, 1)
    return slot_grad, bias_grad, loss_sum


def body(
    tokens, loss_position_mask, lengths, owners, embed_in, unembedding_table, frozen_qkv, frozen_out,
    frozen_up, frozen_down, frozen_bias, norm_gain, norm_shift, master_matrix, lens_bias, matrix_first,
    matrix_second, left_stat, right_stat, left_basis, right_basis, bias_first, bias_second,
):
    bf, f32, i32 = jnp.bfloat16, jnp.float32, jnp.int32
    shards, rows = lax.axis_size("vocab"), lax.axis_size("rows")
    where, row = lax.axis_index("vocab"), lax.axis_index("rows")
    group, width = tokens.shape[0], embed_in.shape[1]
    own = group // shards
    nblk = width // BS
    per = master_matrix.shape[0]
    blocks = shards * per
    chips = shards // 2
    vbits, rbits = chip_bits(shards), bits_of(rows)
    every = jnp.arange(shards, dtype=i32)

    chip, core = where // 2, where % 2
    entry_at = (chip - every // 2) % chips + chips * ((every % 2) ^ core)

    part_rows = per * BS // rows
    held = master_matrix.astype(bf).reshape(rows, part_rows, BS)
    held = lax.dynamic_index_in_dim(held, row, 0, keepdims=False)
    top = lens_bias.astype(bf)
    middle = (lens_bias - top.astype(f32)).astype(bf)
    low = (lens_bias - top.astype(f32) - middle.astype(f32)).astype(bf)
    flat = jnp.concatenate([jnp.pad(t.reshape(-1), (0, BS - lens_bias.size))[None] for t in (top, middle, low)], 0)
    held = jnp.concatenate([held, jnp.pad(flat, ((0, 13), (0, 0)))], 0)
    held = lax.all_gather(held, ("rows", "vocab"), axis=0)
    biases = jnp.sum(held[:shards, part_rows : part_rows + 3, : lens_bias.size].astype(f32), 1)
    biases = biases.reshape(shards, 2, -1).transpose(1, 0, 2).reshape(2, width)
    slots = held
    if per != rows:
        slots = held[:, :part_rows].reshape(rows, shards, part_rows, BS).transpose(1, 0, 2, 3)
        slots = slots.reshape(blocks, BS, BS)

    def by_class(a):
        return a.reshape(own, shards).T.reshape(-1)

    ids = by_class(tokens)
    index = by_class(jnp.arange(group, dtype=i32))
    mask = by_class(loss_position_mask)
    table_rows = embed_in.shape[0]
    owner = ids // table_rows
    local = ids - where * table_rows
    holds = (owner[:, None] == jnp.arange(shards, dtype=i32)[None, :]).astype(bf)
    before = (jnp.arange(group)[:, None] > jnp.arange(group)[None, :]).astype(bf)
    ahead = jnp.dot(before, holds, preferred_element_type=f32)
    rank = jnp.sum(ahead * holds.astype(f32), 1).astype(i32)
    take = 176 if group <= 1024 else 64

    def chunk():
        slot = jnp.arange(take, dtype=i32)[:, None]
        hit = (owner == where)[None, :] & (rank[None, :] == slot)
        picked = jnp.sum(jnp.where(hit, local[None, :], 0), 1)
        mine = jnp.take(embed_in, picked, axis=0, mode="clip")
        return mine

    def exchange(mine):
        near = [mine]
        for o in range(1, chips):
            near.append(lax.ppermute(mine, "vocab", [(i, (i + 2 * o) % shards) for i in range(shards)]))
        return near + [swap(piece, "vocab", 1) for piece in near]

    mine, mask = tie(chunk(), mask)
    pieces_in = exchange(mine)
    mask, index, seq_lens, rank, owner, owners = tie(pace(mask), index, lengths[0], rank, owner, owners)
    apart = (chip - owner // 2) % chips + chips * ((owner % 2) ^ core)
    column = jnp.where(rank < take, apart * take + rank, -1)
    most = jnp.max(jnp.sum(holds.astype(f32), 0)).astype(i32)
    shared = gather_xor(jnp.concatenate([mask, jnp.full((8,), most, i32)]), "rows", rbits)
    masks = shared[:, :group].reshape(rows, shards, own)
    most = jnp.max(shared[:, group:])


    segment, position = places(index, seq_lens)
    half = ROT // 2
    lane = jnp.arange(2 * HEAD_DIM) % HEAD_DIM
    freq = 10000.0 ** (-2.0 * (lane % half).astype(f32) / ROT)
    angle = position.astype(f32)[:, None] * freq[None, :]
    turns = (lane < ROT)[None, :]
    cosines = jnp.where(turns, jnp.cos(angle), 1.0)
    sines = jnp.where(turns, jnp.sin(angle) * jnp.where(lane < half, -1.0, 1.0)[None, :], 0.0)
    key_meta = jnp.concatenate([segment[None], index[None], jnp.zeros((6, group), i32)], 0)
    meta = jnp.stack([column, segment, index], 1)
    bias_row = frozen_bias.reshape(1, -1)
    spot = where.reshape(1)

    take_rows = max(16, 320 // shards)
    count = take_rows * shards
    mine_masks = lax.dynamic_index_in_dim(masks, where, 1, keepdims=False)
    per_row = jnp.sum(mine_masks, 1)
    lower = (row ^ jnp.arange(rows)) < row
    base = jnp.sum(jnp.where(lower, per_row, 0))
    dealt = base + jnp.cumsum(mine_masks[0]) - mine_masks[0]
    per_class = jnp.sum(masks, (0, 2))
    entry_chip = (chip - jnp.arange(chips)) % chips
    per_entry = jnp.concatenate(
        [jnp.take(per_class, entry_chip * 2 + core), jnp.take(per_class, entry_chip * 2 + (core ^ 1))]
    )
    share = (per_entry - row + rows - 1) // rows
    rounds = -(-jnp.max((per_class + rows - 1) // rows) // take_rows)

    numbers = jnp.arange(blocks, dtype=i32)
    pieces = max(1, rows // per)
    span = per * pieces // rows
    slot_of = jnp.sum(jnp.where(owners[None, :] == numbers[:, None], numbers[None, :], 0), 1)
    device, inner = slot_of // per, slot_of % per
    away_core = (device % 2) ^ core
    ahead_by = (device // 2 - chip) % chips
    piece = inner[:, None] * pieces + jnp.arange(pieces, dtype=i32)[None, :]
    part = (piece // span) ^ row
    half_chips = chips // 2
    dest = (away_core * 2 + ahead_by // half_chips)[:, None] * rows + part
    dest = (dest * half_chips + (ahead_by % half_chips)[:, None]) * span + piece % span
    loc = inner * shards + device if per == rows else slot_of

    def pick_of(k):
        target = jnp.arange(rows, dtype=i32) ^ row
        place = jnp.arange(take_rows, dtype=i32) + k * take_rows
        wanted = (place[None, :] * rows + target[:, None]).reshape(-1)
        return ((dealt[None, :] == wanted[:, None]) & (mine_masks[0] > 0)[None, :]).astype(bf)

    def across(sent):
        return add(sent[0], *[swap(sent[e], "rows", e) for e in range(1, rows)])

    def spread_out(sent):
        return spread_group(across(sent)).reshape(count, width)

    def share_stats(local):
        stats = local.reshape(6, 2, chips, take_rows)
        total = stats
        for o in range(1, chips):
            total = merge(total, jnp.roll(ring(stats, o), o, 2))
        return merge(total, jnp.flip(swap(total, "vocab", 1), 1)).reshape(6, count)

    def counted_in(k):
        place = jnp.arange(take_rows, dtype=i32)[None, :] + k * take_rows
        return (place < share[:, None]).reshape(-1).astype(f32)

    def with_loss(small, valid, stats):
        logtot = stats[:3] + jnp.log(stats[3:])
        loss = jnp.sum(valid * (logtot[1] + logtot[2] - 2.0 * logtot[0]))
        first_lane = (jnp.arange(width) == 0)[None, :] & (jnp.arange(8) == 2)[:, None]
        return small + jnp.where(first_lane & (where == 0), loss, 0.0)

    overflow = ((most > take) | (rounds > 1)).astype(i32)

    def dense(c):
        k, *given = tie(
            c[0], tokens, loss_position_mask, lengths, owners, embed_in, unembedding_table, frozen_qkv, frozen_out,
            frozen_up, frozen_down, frozen_bias, norm_gain, norm_shift, master_matrix, lens_bias,
        )
        grad, grad_bias, loss = dense_path(*given)
        turned_grad = jnp.take(grad.reshape(rows, -1, BS), jnp.arange(rows) ^ row, axis=0)
        return (k + 1, turned_grad, grad_bias, loss)

    pick = pick_of(jnp.int32(0))
    emb_own, *sent0 = place_call(rows, spot, pieces_in, meta, pick)
    got0 = across(sent0)
    k_all, v_all, q_own = project_call(
        own, spot, pieces_in, meta, cosines, sines, bias_row, norm_gain, norm_shift, frozen_qkv
    )
    got0, q_own = tie(got0, q_own)
    near0 = jnp.stack([got0] + [ring(got0, o) for o in range(1, chips)], 0)
    out_own, *sent1 = layer_call(
        rows, spot, k_all, v_all, q_own, emb_own, meta, key_meta, bias_row, norm_gain, norm_shift, pick,
        frozen_out, frozen_up, frozen_down,
    )
    near0, *sent1 = tie(near0, *sent1)
    x0 = jnp.stack([near0, swap(near0, "vocab", 1)], 0).reshape(count, width)
    got1 = across(sent1)
    held1, hats1, *kept = probe_call((0,), "start", unembedding_table, loc, x0, slots, biases, norm_gain, norm_shift)
    got1, kept[-1] = tie(got1, kept[-1])
    near1 = jnp.stack([got1] + [ring(got1, o) for o in range(1, chips)], 0)
    sums1, stats1 = probe_call((0,), "rest", unembedding_table, held1, *kept)
    near1, stats1 = tie(near1, stats1)
    x1 = jnp.stack([near1, swap(near1, "vocab", 1)], 0).reshape(count, width)
    sums02, stats02, hats02 = probe_call(
        (-1, 1), "all", unembedding_table, loc, x1, slots, biases, norm_gain, norm_shift
    )
    part_shape = (rows, span * BS // pieces, BS)
    done, stats02 = tie(jnp.int32(0), stats02)
    start = (done, jnp.zeros(part_shape, f32), jnp.zeros(lens_bias.shape, f32), jnp.float32(0.0))
    _, dense_parts, dense_bias, dense_loss = lax.while_loop(lambda c: c[0] < overflow, dense, start)
    stats02, dense_parts = tie(stats02, dense_parts)
    local_stats = jnp.concatenate([stats02[0:1], stats1[0:1], stats02[1:3], stats1[1:2], stats02[3:4]], 0)
    local_stats = local_stats[:, :count]
    stats = share_stats(local_stats)
    valid = counted_in(jnp.int32(0))
    scale = valid[None, :] * jnp.exp(local_stats[:3] - stats[:3]) / stats[3:]
    scale = jnp.pad(scale, ((0, 5), (0, -(-count // 128) * 128 - count)))
    *grads, small = grad_call(dest, x0, x1, sums1, sums02, scale, hats1, hats02, norm_gain, norm_shift)

    slot_parts, small = reduce_slots(grads, with_loss(small, valid, stats))
    full = jnp.where(overflow > 0, dense_parts, slot_parts.astype(f32))
    loss_count = jnp.sum(masks).astype(f32)

    loss_sum = jnp.where(overflow > 0, dense_loss, jnp.sum(small[2]))
    bias_grad = small[:2]
    bias_cols = lens_bias.shape[1]
    bias_grad = lax.dynamic_slice_in_dim(bias_grad, where * bias_cols, bias_cols, 1)
    bias_grad = jnp.where(overflow > 0, dense_bias, bias_grad)

    if per >= rows:
        slot_grad = full.reshape(per, BS, BS)
        turn = row * (per // rows)
    else:
        slot_grad = jnp.take(full, row ^ jnp.arange(rows), axis=0).reshape(per, BS, BS)
        turn = jnp.int32(0)

    (new_matrix, new_first, new_second, new_left, new_right, renewed_left_basis, new_rbasis) = soap_call(
        turn.reshape(1), master_matrix, slot_grad, matrix_first, matrix_second, left_stat, right_stat,
        left_basis, right_basis,
    )
    new_bias, new_bias_first, new_bias_second = adam_bias(lens_bias, bias_grad, bias_first, bias_second)
    return (
        loss_sum, loss_count, new_matrix, new_first, new_second, new_left, new_right, renewed_left_basis,
        new_rbasis, new_bias, new_bias_first, new_bias_second,
    )


def solution(mesh):
    in_specs = (
        P("rows"),
        P("rows"),
        P("rows", None),
        P(),
        P("vocab", None),
        P("vocab", None),
        P(),
        P(),
        P(),
        P(),
        P(),
        P(),
        P(),
        P("vocab", None, None),
        P(None, "vocab"),
        P("vocab", None, None),
        P("vocab", None, None),
        P("vocab", None, None),
        P("vocab", None, None),
        P("vocab", None, None),
        P("vocab", None, None),
        P(None, "vocab"),
        P(None, "vocab"),
    )
    out_specs = (
        P(),
        P(),
        P("vocab", None, None),
        P("vocab", None, None),
        P("vocab", None, None),
        P("vocab", None, None),
        P("vocab", None, None),
        P("vocab", None, None),
        P("vocab", None, None),
        P(None, "vocab"),
        P(None, "vocab"),
        P(None, "vocab"),
    )
    return jax.shard_map(body, mesh=mesh, in_specs=in_specs, out_specs=out_specs, check_vma=False)
```

```python
import functools

import jax
import jax.numpy as jnp
import numpy as np
from jax import lax
from jax.experimental import pallas as pl
from jax.experimental.pallas import tpu as pltpu
from jax.sharding import PartitionSpec as P

HEADS = 16
HEAD_DIM = 64
ROT = 16
BS = 256
STEP = 5

HIGHEST = lax.Precision.HIGHEST
NORM_EPS = 1e-05
BETA_ONE = 0.9
BETA_TWO = 0.999
BETA_STAT = 0.95
ADAM_EPS = 1e-08
MATRIX_RATE = 0.01
BIAS_RATE = 0.1
DECAY = 0.1
MASKED = -1e30
NB = 64
PIV = 2
VMEM_LIMIT = 56 * 2**20


def _mm(a,b,dims):
    return lax.dot_general(a,b,(dims,((),())),precision=HIGHEST,preferred_element_type=jnp.float32)
def mm_nn(a,b): return _mm(a,b,((1,),(0,)))
def mm_tn(a,b): return _mm(a,b,((0,),(0,)))
def mm_nt(a,b): return _mm(a,b,((1,),(1,)))
def _mb(a,b,dims):
    return lax.dot_general(a.astype(jnp.bfloat16),b.astype(jnp.bfloat16),(dims,((),())),preferred_element_type=jnp.float32)

def eliminate(rows, nb):
    rows=list(rows)
    def pick(i,c):
        return jnp.broadcast_to(rows[i][:,c:c+1],rows[i].shape)
    for j in range(0,nb,PIV):
        low=[[None]*PIV for _ in range(PIV)]
        roots=[None]*PIV
        inv=[[None]*PIV for _ in range(PIV)]
        cur=[[pick(j+p,j+q) if q<=p else None for q in range(PIV)] for p in range(PIV)]
        for q in range(PIV):
            guess=lax.rsqrt(cur[q][q])
            roots[q]=guess*(1.5-0.5*(cur[q][q]*guess)*guess)
            for p in range(q+1,PIV):
                low[p][q]=cur[p][q]*roots[q]
            for p in range(q+1,PIV):
                for t in range(q+1,p+1):
                    cur[p][t]=cur[p][t]-low[p][q]*low[t][q]
        lead=[]
        for p in range(PIV):
            acc=rows[j+p]
            for q in range(p):
                acc=acc-low[p][q]*lead[q]
            lead.append(acc*roots[p])
        back=[None]*PIV
        for p in reversed(range(PIV)):
            acc=lead[p]
            for q in range(p+1,PIV):
                acc=acc-low[q][p]*back[q]
            back[p]=acc*roots[p]
        for i in range(j+PIV,nb):
            cols=[pick(i,j+p) for p in range(PIV)]
            t=cols[0]*back[0]
            for p in range(1,PIV):
                t=t+cols[p]*back[p]
            rows[i]=rows[i]-t
        for p in range(PIV):
            rows[j+p]=lead[p]
    return rows

def soap_kernel(per, where_ref, w_ref,g_ref,first_ref,second_ref,left_ref,right_ref,lb_ref,rb_ref,
                nw_out,nf_out,ns_out,nl_out,nr_out,ql_ref,qr_ref,nw_ref,nf_ref,ns_ref,nl_ref,nr_ref,work,prods,stage,sems):
    xor=where_ref[0]
    nm=2*per
    nn=((1,),(0,)); tn=((0,),(0,)); nt=((1,),(1,))
    def slot(s,c):
        g=g_ref[s^xor].astype(jnp.float32)
        gb=g.astype(jnp.bfloat16)
        lb=lb_ref[s]; rb=rb_ref[s]
        lbb=lb.astype(jnp.bfloat16); rbb=rb.astype(jnp.bfloat16)
        rotated=_mb(_mb(lbb,gb,tn),rbb,nn)
        first=BETA_ONE*first_ref[s]+(1.0-BETA_ONE)*g
        second=BETA_TWO*second_ref[s]+(1.0-BETA_TWO)*rotated*rotated
        nf_ref[s]=first; ns_ref[s]=second
        moment=_mb(_mb(lbb,first,tn),rbb,nn)
        scaled=moment/(1.0-BETA_ONE**STEP)/(jnp.sqrt(second/(1.0-BETA_TWO**STEP))+ADAM_EPS)
        update=_mb(_mb(lbb,scaled,nn),rbb,nt)
        w=w_ref[s]
        nw_ref[s]=w-MATRIX_RATE*(update+DECAY*w)
        nl=BETA_STAT*left_ref[s]+(1.0-BETA_STAT)*_mb(gb,gb,nt)
        nr=BETA_STAT*right_ref[s]+(1.0-BETA_STAT)*_mb(gb,gb,tn)
        nl_ref[s]=nl; nr_ref[s]=nr
        pl_=mm_nn(nl,lb); pr_=mm_nn(nr,rb)
        prods[s]=pl_; prods[per+s]=pr_
        work[s]=mm_tn(pl_,pl_); work[per+s]=mm_tn(pr_,pr_)
        return c
    lax.fori_loop(0,per,slot,0,unroll=True)
    copies=[pltpu.make_async_copy(src,dst,sems.at[i]) for i,(src,dst) in enumerate(zip((nw_ref,nf_ref,ns_ref,nl_ref,nr_ref),(nw_out,nf_out,ns_out,nl_out,nr_out)))]
    for copy in copies:
        copy.start()
    lane=lax.broadcasted_iota(jnp.int32,(NB,128),1)
    row=lax.broadcasted_iota(jnp.int32,(NB,128),0)
    ident=(lane==row+NB).astype(jnp.float32)
    idrow=lax.broadcasted_iota(jnp.int32,(NB,BS),0)
    col=lax.broadcasted_iota(jnp.int32,(NB,BS),1)
    colw=lax.broadcasted_iota(jnp.int32,(BS,BS),1)
    upper=lax.broadcasted_iota(jnp.int32,(NB,NB),0)<=lax.broadcasted_iota(jnp.int32,(NB,NB),1)
    def fill(k):
        r0=k*NB
        for m in range(nm):
            d=work[m,r0:r0+NB,r0//128*128:r0//128*128+128]
            if r0%128: d=pltpu.roll(d,128-r0%128,axis=1)
            stage[m*NB:(m+1)*NB,:]=jnp.where(lane<NB,d,ident)
    def trail(k):
        r0=k*NB
        end=r0+NB
        lo=end//128*128
        inside=(col>=r0)&(col<end)
        ms=range(nm)
        linv=[stage[m*NB:(m+1)*NB,NB:2*NB] for m in ms]
        rows_m=[jnp.where(inside,(col==idrow+r0).astype(jnp.float32),work[m,r0:end,:]) for m in ms]
        b=[mm_nn(linv[m],rows_m[m]) for m in ms]
        if end<BS:
            up=[jnp.where(upper,stage[m*NB:(m+1)*NB,:NB],0.0) for m in ms]
            left=[rows_m[m][:,lo:]-mm_tn(up[m],b[m][:,lo:]) for m in ms]
            fix=[b[m][:,lo:]+mm_nn(linv[m],left[m]) for m in ms]
            b=[fix[m] if lo==0 else jnp.concatenate([b[m][:,:lo],fix[m]],1) for m in ms]
            cw=colw[:BS-end]
            rest=[mm_tn(b[m][:,lo:],b[m])[end-lo:] for m in ms]
            for m in ms:
                work[m,end:,:]=jnp.where((cw>=r0)&(cw<end),0.0,work[m,end:,:])-rest[m]
        for m in ms:
            work[m,r0:end,:]=b[m]
    def step(kb,c):
        for k in range(BS//NB):
            @pl.when(kb==k)
            def _(k=k):
                fill(k)
        rows=[stage[pl.ds(i,nm,stride=NB),:] for i in range(NB)]
        rows=eliminate(rows,NB)
        for i in range(NB):
            stage[pl.ds(i,nm,stride=NB),:]=rows[i]
        for k in range(BS//NB):
            @pl.when(kb==k)
            def _(k=k):
                trail(k)
        return c
    lax.fori_loop(0,BS//NB,step,0)
    roww=lax.broadcasted_iota(jnp.int32,(BS,BS),0)
    weight=jnp.where(roww>colw,1.0,jnp.where(roww==colw,0.5,0.0))
    unit=(roww==colw).astype(jnp.float32)
    outs=[(ql_ref,s) for s in range(per)]+[(qr_ref,s) for s in range(per)]
    bases=[mm_nt(prods[m],jnp.where(roww>=colw,work[m],0.0)) for m in range(nm)]
    for turn in range(2):
        gaps=[((mm_tn(q,q) if turn else _mb(q,q,tn))-unit)*weight for q in bases]
        bases=[q-_mb(q,gap,nt) for q,gap in zip(bases,gaps)]
    for (ref,s),q in zip(outs,bases):
        ref[s]=q
    for copy in copies:
        copy.wait()

def soap_call(xor,w,g,first,second,left,right,lb,rb):
    per=w.shape[0]
    sh=jax.ShapeDtypeStruct((per,BS,BS),jnp.float32)
    vm=pl.BlockSpec(memory_space=pltpu.VMEM)
    return pl.pallas_call(functools.partial(soap_kernel,per),
        out_shape=[sh]*7,
        in_specs=[pl.BlockSpec(memory_space=pltpu.SMEM)]+[vm]*8, out_specs=[pl.BlockSpec(memory_space=pl.ANY)]*5+[vm]*2,
        scratch_shapes=[pltpu.VMEM((per,BS,BS),jnp.float32)]*5+[pltpu.VMEM((2*per,BS,BS),jnp.float32),pltpu.VMEM((2*per,BS,BS),jnp.float32),pltpu.VMEM((2*per*NB,128),jnp.float32),pltpu.SemaphoreType.DMA((5,))],
        compiler_params=pltpu.CompilerParams(vmem_limit_bytes=48*2**20),
        name="soap_update")(xor,w,g,first,second,left,right,lb,rb)


def adam_bias(bias, grad, first, second):
    first_new = BETA_ONE * first + (1.0 - BETA_ONE) * grad
    second_new = BETA_TWO * second + (1.0 - BETA_TWO) * grad * grad
    scaled = (
        first_new
        / (1.0 - BETA_ONE**STEP)
        / (jnp.sqrt(second_new / (1.0 - BETA_TWO**STEP)) + ADAM_EPS)
    )
    return (bias - BIAS_RATE * scaled, first_new, second_new)


def places(index, seq_lens):
    ends = jnp.cumsum(seq_lens)
    segment = jnp.sum((index[:, None] >= ends[None, :]).astype(jnp.int32), 1)
    starts = ends - seq_lens
    picked = segment[:, None] == jnp.arange(seq_lens.shape[0], dtype=jnp.int32)[None, :]
    offset = jnp.sum(jnp.where(picked, starts[None, :], 0), 1)
    return (segment, index - offset)


def swap(x, axis, bit):
    size = lax.axis_size(axis)
    return lax.ppermute(x, axis, [(i, i ^ bit) for i in range(size)])


def gather_xor(x, axis, bits):
    out = x[None]
    for bit in bits:
        out = jnp.concatenate([out, swap(out, axis, bit)], 0)
    return out


def bits_of(size):
    return [1 << i for i in range(size.bit_length() - 1)]


def chip_bits(size):
    return bits_of(size)[1:][::-1] + [1]


def entry_ids(bits):
    ids = [0]
    for bit in bits:
        ids = ids + [i ^ bit for i in ids]
    return ids


def normalize(x, gain, shift):
    centred = x - jnp.mean(x, -1, keepdims=True)
    root = lax.rsqrt(jnp.mean(centred * centred, -1, keepdims=True) + NORM_EPS)
    return centred * root * gain + shift


def turned(x, cos, sin):
    width = x.shape[1]
    lane = lax.broadcasted_iota(jnp.int32, (1, width), 1)
    swapped = jnp.where(
        lane % HEAD_DIM < ROT // 2,
        pltpu.roll(x, width - ROT // 2, axis=1),
        pltpu.roll(x, ROT // 2, axis=1),
    )
    reps = width // cos.shape[1]
    return x * jnp.concatenate([cos] * reps, 1) + swapped * jnp.concatenate([sin] * reps, 1)


def fill_pool(bufs, pool, sems):
    take = bufs[0].shape[0]
    return [
        pltpu.make_async_copy(buf, pool.at[i * take : (i + 1) * take, :], sems.at[i])
        for i, buf in enumerate(bufs)
    ]


def placed(pool, column):
    spread = lax.broadcasted_iota(jnp.int32, (column.shape[0], pool.shape[0]), 1) == column
    return jnp.dot(spread.astype(jnp.bfloat16), pool[...], preferred_element_type=jnp.float32)


def deal(pick, x, outs):
    sent = jnp.dot(pick[...], x, preferred_element_type=jnp.float32).astype(jnp.bfloat16)
    n = sent.shape[0] // len(outs)
    for e, out in enumerate(outs):
        out[...] = sent[e * n : (e + 1) * n]


def place_kernel(parts, where_ref, *refs):
    bufs = refs[:parts]
    meta, pick, own_out, *sent_out, pool, sems = refs[parts:]
    own = own_out.shape[0]
    fills = fill_pool(bufs, pool, sems)
    for fill in fills:
        fill.start()
    for fill in fills:
        fill.wait()
    mine = pl.ds(pl.multiple_of(where_ref[0] * own, own), own)
    x = placed(pool, meta[mine, 0:1])
    x = x.astype(jnp.bfloat16)
    own_out[...] = x
    deal(pick, x, sent_out)


def place_call(dealt_to, where, bufs, meta, pick):
    take, width = bufs[0].shape
    parts = len(bufs)
    own = pick.shape[1]
    vm = pl.BlockSpec(memory_space=pltpu.VMEM)
    hbm = pl.BlockSpec(memory_space=pl.ANY)
    bf = jnp.bfloat16
    return pl.pallas_call(
        functools.partial(place_kernel, parts),
        out_shape=[
            jax.ShapeDtypeStruct((own, width), bf),
            *[jax.ShapeDtypeStruct((pick.shape[0] // dealt_to, width), bf)] * dealt_to,
        ],
        in_specs=[pl.BlockSpec(memory_space=pltpu.SMEM)] + [hbm] * parts + [vm, vm],
        out_specs=[vm] * (1 + dealt_to),
        scratch_shapes=[pltpu.VMEM((parts * take, width), bf), pltpu.SemaphoreType.DMA((parts,))],
        compiler_params=pltpu.CompilerParams(vmem_limit_bytes=VMEM_LIMIT),
        cost_estimate=pl.CostEstimate(flops=10**9, bytes_accessed=4 * 2**20, transcendentals=0),
        name="place_rows",
    )(where, *bufs, meta, pick)


def project_kernel(parts, where_ref, *refs):
    bufs = refs[:parts]
    (meta, cosines, sines, bias, gain, shift, qkv, k_out, v_out, q_out, pool, emb, w_qkv,
     sems) = refs[parts:]
    group, width = k_out.shape
    own = q_out.shape[0]
    fills = fill_pool(bufs, pool, sems)
    loads = [
        pltpu.make_async_copy(qkv.at[:, i * width : (i + 1) * width], w_qkv.at[i], sems.at[parts + i])
        for i in range(3)
    ]
    for fill in fills:
        fill.start()
    for i in (1, 2, 0):
        loads[i].start()
    for fill in fills:
        fill.wait()
    rows = 256

    def attn_in(x):
        return normalize(x.astype(jnp.float32), gain[0:1, :], shift[0:1, :]).astype(jnp.bfloat16)

    loads[1].wait()
    loads[2].wait()

    def project(i, c):
        at = pl.ds(pl.multiple_of(i * rows, rows), rows)

        x = placed(pool, meta[at, 0:1]).astype(jnp.bfloat16)
        emb[at, :] = x
        y = attn_in(x)
        k = jnp.dot(y, w_qkv[1], preferred_element_type=jnp.float32) + bias[:, width : 2 * width]
        k_out[at, :] = turned(k, cosines[at, :], sines[at, :]).astype(jnp.bfloat16)
        v = jnp.dot(y, w_qkv[2], preferred_element_type=jnp.float32)
        v_out[at, :] = (v + bias[:, 2 * width : 3 * width]).astype(jnp.bfloat16)
        return c

    lax.fori_loop(0, group // rows, project, 0)
    mine = pl.ds(pl.multiple_of(where_ref[0] * own, own), own)
    loads[0].wait()
    q = jnp.dot(attn_in(emb[mine, :]), w_qkv[0], preferred_element_type=jnp.float32)
    q = turned(q + bias[:, :width], cosines[mine, :], sines[mine, :])
    q_out[...] = q.astype(jnp.bfloat16)


def project_call(own, where, bufs, meta, cosines, sines, bias, gain, shift, qkv):
    group = meta.shape[0]
    take, width = bufs[0].shape
    parts = len(bufs)
    vm = pl.BlockSpec(memory_space=pltpu.VMEM)
    hbm = pl.BlockSpec(memory_space=pl.ANY)
    bf = jnp.bfloat16
    return pl.pallas_call(
        functools.partial(project_kernel, parts),
        out_shape=[
            jax.ShapeDtypeStruct((group, width), bf),
            jax.ShapeDtypeStruct((group, width), bf),
            jax.ShapeDtypeStruct((own, width), bf),
        ],
        in_specs=[pl.BlockSpec(memory_space=pltpu.SMEM)] + [hbm] * parts + [vm] * 6 + [hbm],
        out_specs=[vm] * 3,
        scratch_shapes=[
            pltpu.VMEM((parts * take, width), bf),
            pltpu.VMEM((group, width), bf),
            pltpu.VMEM((3, width, width), bf),
            pltpu.SemaphoreType.DMA((parts + 3,)),
        ],
        compiler_params=pltpu.CompilerParams(vmem_limit_bytes=VMEM_LIMIT),
        cost_estimate=pl.CostEstimate(flops=12 * 10**9, bytes_accessed=16 * 2**20, transcendentals=0),
        name="project_group",
    )(where, *bufs, meta, cosines, sines, bias, gain, shift, qkv)


def layer_kernel(
    chunks, where_ref, k_all, v_all, q_own, emb, meta, key_meta, bias, gain, shift, pick,
    w_out, w_up, w_down, out, *refs,
):
    *sent_out, wo, up, down, mix, sems = refs
    own, width = emb.shape
    units = w_up.shape[1]
    part = units // chunks
    nbuf = up.shape[0]

    def load(j):
        n = j % nbuf
        return (
            pltpu.make_async_copy(w_up.at[:, j * part : (j + 1) * part], up.at[n], sems.at[1 + n]),
            pltpu.make_async_copy(
                w_down.at[j * part : (j + 1) * part, :], down.at[n], sems.at[1 + nbuf + n]
            ),
        )

    load_out = pltpu.make_async_copy(w_out, wo, sems.at[0])
    load_out.start()
    for j in range(nbuf):
        for copy in load(j):
            copy.start()

    mine = pl.ds(pl.multiple_of(where_ref[0] * own, own), own)
    allowed = (meta[mine, 1:2] == key_meta[0:1, :]) & (key_meta[1:2, :] <= meta[mine, 2:3])
    half = lax.broadcasted_iota(jnp.int32, (1, 2 * HEAD_DIM), 1) // HEAD_DIM

    def pair(hp, c):
        at = pl.ds(pl.multiple_of(hp * 2 * HEAD_DIM, 2 * HEAD_DIM), 2 * HEAD_DIM)
        qp, kp, vp = q_own[:, at], k_all[:, at], v_all[:, at]
        outs = []
        for h in range(2):
            qh = jnp.where(half == h, qp, jnp.zeros((), jnp.bfloat16))
            scores = lax.dot_general(
                qh, kp, (((1,), (1,)), ((), ())), preferred_element_type=jnp.float32
            )
            scores = jnp.where(allowed, scores * HEAD_DIM ** (-0.5), MASKED)
            weights = jnp.exp(scores - jnp.max(scores, -1, keepdims=True))
            total = jnp.sum(weights, -1, keepdims=True)
            got = jnp.dot(weights.astype(jnp.bfloat16), vp, preferred_element_type=jnp.float32)
            outs.append(got / total)
        mix[:, at] = jnp.where(half == 0, outs[0], outs[1]).astype(jnp.bfloat16)
        return c

    lax.fori_loop(0, HEADS // 2, pair, 0, unroll=4)
    x_own = emb[...].astype(jnp.float32)
    load_out.wait()
    total = x_own + (
        jnp.dot(mix[...], wo[...], preferred_element_type=jnp.float32)
        + bias[:, 3 * width : 4 * width]
    )
    mlp_in = normalize(x_own, gain[1:2, :], shift[1:2, :]).astype(jnp.bfloat16)
    acc = jnp.zeros((own, width), jnp.float32)
    for j in range(chunks):
        for copy in load(j):
            copy.wait()
        lo = 4 * width + j * part
        pre = jnp.dot(mlp_in, up[j % nbuf], preferred_element_type=jnp.float32)
        pre = pre + bias[:, lo : lo + part]
        activ = (0.5 * pre * (1.0 + lax.erf(pre * 0.7071067811865476))).astype(jnp.bfloat16)
        acc = acc + jnp.dot(activ, down[j % nbuf], preferred_element_type=jnp.float32)
        if j + nbuf < chunks:
            for copy in load(j + nbuf):
                copy.start()
    low = (total + (acc + bias[:, 4 * width + units :])).astype(jnp.bfloat16)
    out[...] = low
    deal(pick, low, sent_out)


def layer_call(dealt_to, where, k, v, q, emb, meta, key_meta, bias, gain, shift, pick, w_out, w_up, w_down):
    group, width = k.shape
    own = emb.shape[0]
    units = w_up.shape[1]
    chunks = units // width
    nbuf = chunks if group <= 1024 else 2
    vm = pl.BlockSpec(memory_space=pltpu.VMEM)
    hbm = pl.BlockSpec(memory_space=pl.ANY)
    bf = jnp.bfloat16
    return pl.pallas_call(
        functools.partial(layer_kernel, chunks),
        out_shape=[
            jax.ShapeDtypeStruct((own, width), bf),
            *[jax.ShapeDtypeStruct((pick.shape[0] // dealt_to, width), bf)] * dealt_to,
        ],
        in_specs=[pl.BlockSpec(memory_space=pltpu.SMEM)] + [vm] * 10 + [hbm] * 3,
        out_specs=[vm] * (1 + dealt_to),
        scratch_shapes=[
            pltpu.VMEM((width, width), bf),
            pltpu.VMEM((nbuf, width, units // chunks), bf),
            pltpu.VMEM((nbuf, units // chunks, width), bf),
            pltpu.VMEM((own, width), bf),
            pltpu.SemaphoreType.DMA((1 + 2 * nbuf,)),
        ],
        compiler_params=pltpu.CompilerParams(vmem_limit_bytes=VMEM_LIMIT),
        cost_estimate=pl.CostEstimate(flops=12 * 10**9, bytes_accessed=24 * 2**20, transcendentals=0),
        name="frozen_layer",
    )(where, k, v, q, emb, meta, key_meta, bias, gain, shift, pick, w_out, w_up, w_down)


def probe_kernel(limit, sets, chunks, kind, first, *refs):
    if kind == "rest":
        sums_in, normed, peak_in, mass_in, table, sums, stats, peak, mass = refs
    elif kind == "start":
        loc_ref, x, slots, bias, gain, shift, table, sums, hats, normed, peak, mass = refs
    else:
        loc_ref, x, slots, bias, gain, shift, table, sums, stats, hats, normed, peak, mass = refs
    begins = pl.program_id(0) == 0
    step = pl.program_id(0) + first
    tile, width = table.shape
    steps = -(-limit // tile)
    count = chunks * normed.shape[1] // len(sets)
    nblk = width // BS
    size = count // chunks
    many = len(sets)

    def start():
        def save(i, rows, v):
            centred = v - jnp.mean(v, -1, keepdims=True)
            root = lax.rsqrt(jnp.mean(centred * centred, -1, keepdims=True) + NORM_EPS)
            hat = centred * root
            normed[rows // size, i * size : (i + 1) * size, :] = (
                hat * gain[2:3, :] + shift[2:3, :]
            ).astype(jnp.bfloat16)
            return hat, root

        for c in range(chunks):
            rows = c * size
            raw = x[rows : rows + size, :]
            v = raw.astype(jnp.float32)
            for i, k in enumerate(sets):
                if k < 0:
                    hat, root = save(i, rows, v)
                else:
                    cols = []
                    for j in range(nblk):
                        total = None
                        for b in range(nblk):
                            term = jnp.dot(
                                raw[:, b * BS : (b + 1) * BS],
                                slots[loc_ref[(k * nblk + b) * nblk + j], :BS, :],
                                preferred_element_type=jnp.float32,
                            )
                            total = term if total is None else total + term
                        cols.append(total)
                    hat, root = save(i, rows, v + jnp.concatenate(cols, 1) + bias[k : k + 1, :])
                hats[i, rows : rows + size, :width] = hat
                hats[i, rows : rows + size, width:] = jnp.broadcast_to(root, (size, 128))
        peak[...] = jnp.full(peak.shape, MASKED, jnp.float32)
        mass[...] = jnp.zeros(mass.shape, jnp.float32)
        sums[...] = jnp.zeros(sums.shape, jnp.float32)

    def resume():
        peak[...] = peak_in[...]
        mass[...] = mass_in[...]
        sums[...] = sums_in[...]

    pl.when(begins)(resume if kind == "rest" else start)

    def visit(last):
        w = table[...]
        if last:
            left = limit - step * tile
            at = lax.broadcasted_iota(jnp.int32, (1, tile), 1)
            down = lax.broadcasted_iota(jnp.int32, (tile, 1), 0)
            w = jnp.where(down < left, w, jnp.zeros((), jnp.bfloat16))

        def score(c):
            return lax.dot_general(
                normed[c], w, (((1,), (1,)), ((), ())), preferred_element_type=jnp.float32
            )

        ready = score(0)
        for c in range(chunks):
            logits = ready
            if c + 1 < chunks:
                ready = score(c + 1)
            if last:
                logits = jnp.where(at < left, logits, MASKED)
            old = peak[c]
            new = jnp.maximum(old, jnp.max(logits, -1, keepdims=True))
            fade = jnp.exp(old - new)
            powers = jnp.exp(logits - new)
            peak[c] = new
            mass[c] = mass[c] * fade + jnp.sum(powers, -1, keepdims=True)
            sums[c] = sums[c] * fade + jnp.dot(
                powers.astype(jnp.bfloat16), w, preferred_element_type=jnp.float32
            )

    def finish():
        visit(True)
        lanes = -(-count // 128) * 128
        at = lax.broadcasted_iota(jnp.int32, (lanes, 128), 1)
        packed = jnp.zeros((lanes, 128), jnp.float32)
        for i in range(many):
            for n, ref in ((i, peak), (many + i, mass)):
                col = [ref[c, i * size : (i + 1) * size, :] for c in range(chunks)]
                if lanes > count:
                    col.append(jnp.zeros((lanes - count, 1), jnp.float32))
                packed = jnp.where(at == n, jnp.concatenate(col, 0), packed)
        stats[...] = jnp.transpose(packed)[:8, :]

    if kind == "start":
        visit(False)
    else:
        pl.when(step < steps - 1)(lambda: visit(False))
        pl.when(step == steps - 1)(finish)


def probe_call(sets, kind, table, *given):
    vocab, width = table.shape
    tile = 1280
    steps = -(-vocab // tile)
    ahead = -(-steps // 2)
    first, todo = {"all": (0, steps), "start": (0, ahead), "rest": (ahead, steps - ahead)}[kind]
    many = len(sets)
    f32 = jnp.float32
    if kind == "rest":
        chunks, rows = given[0].shape[:2]
        size = rows // many
    else:
        count = given[1].shape[0]
        chunks = many if count % (16 * many) == 0 else 1
        size = count // chunks
    count = chunks * size
    vm = pl.BlockSpec(memory_space=pltpu.VMEM)
    column = (chunks, many * size, 1)
    sums = jax.ShapeDtypeStruct((chunks, many * size, width), f32)
    stats = jax.ShapeDtypeStruct((8, -(-count // 128) * 128), f32)
    hats = jax.ShapeDtypeStruct((many, count, width + 128), f32)
    scratch = [pltpu.VMEM(column, f32), pltpu.VMEM(column, f32)]
    if kind == "rest":
        outs, ins = [sums, stats], [vm] * 4
    else:
        ins = [pl.BlockSpec(memory_space=pltpu.SMEM)] + [vm] * 5
        normed = (chunks, many * size, width)
        if kind == "start":
            col = jax.ShapeDtypeStruct(column, f32)
            outs, scratch = [sums, hats, jax.ShapeDtypeStruct(normed, jnp.bfloat16), col, col], []
        else:
            outs, scratch = [sums, stats, hats], [pltpu.VMEM(normed, jnp.bfloat16)] + scratch
    return pl.pallas_call(
        functools.partial(probe_kernel, vocab, sets, chunks, kind, first),
        grid=(todo,),
        out_shape=outs,
        in_specs=ins + [pl.BlockSpec((tile, width), lambda i: (i + first, 0))],
        out_specs=[vm] * len(outs),
        scratch_shapes=scratch,
        compiler_params=pltpu.CompilerParams(vmem_limit_bytes=VMEM_LIMIT),
        cost_estimate=pl.CostEstimate(
            flops=(1 if kind == "all" else 20) * 4 * many * count * todo * tile * width, bytes_accessed=2 * todo * tile * width, transcendentals=0
        ),
        name="probe_" + kind,
    )(*given, table)


def grad_kernel(
    dest_ref, x0, x1, sums1, sums02, scale, hats1, hats02, gain, shift, stay, go, small,
    grads, sems,
):
    count, width = x0.shape
    nblk = width // BS
    pieces = dest_ref.shape[1]
    rows = BS // pieces
    chunks = sums02.shape[0]
    size = count // chunks
    cols = jnp.transpose(jnp.concatenate([scale[...]] * (128 // scale.shape[0]), 0))[:count]
    gain_row, shift_row = gain[2:3, :], shift[2:3, :]

    def normed(hat):
        return (hat * gain_row + shift_row).astype(jnp.bfloat16).astype(jnp.float32)

    def parts(n):
        return jnp.concatenate([sums02[c, n * size : (n + 1) * size, :] for c in range(chunks)], 0)

    base = parts(0) * cols[:, 0:1]
    target = normed(hats02[0, :, :width])
    spread = jnp.zeros((1, width), jnp.float32)
    for k in range(2):
        own = sums1[...].reshape(count, width) if k == 0 else parts(1)
        hats = hats1.at[0] if k == 0 else hats02.at[1]
        hat = hats[:, :width]
        root = hats[:, width : width + 1]
        spread = spread + jnp.sum(base * (target - normed(hat)), 0, keepdims=True)
        e = (own * cols[:, k + 1 : k + 2] - base) * gain_row
        pulled = e - jnp.mean(e, -1, keepdims=True)
        pulled = (pulled - hat * jnp.mean(e * hat, -1, keepdims=True)) * root
        small[k : k + 1, :] = jnp.sum(pulled, 0, keepdims=True)
        low = pulled.astype(jnp.bfloat16)
        x = x0 if k == 0 else x1
        for i in range(nblk):
            full = lax.dot_general(
                x[:, i * BS : (i + 1) * BS], low, (((0,), (0,)), ((), ())),
                preferred_element_type=jnp.float32,
            ).astype(jnp.bfloat16)
            for j in range(nblk):
                b = (k * nblk + i) * nblk + j
                for p in range(pieces):
                    piece = full[p * rows : (p + 1) * rows, j * BS : (j + 1) * BS]
                    grads[dest_ref[b, p]] = piece
    half = grads.shape[0] // 2
    copies = [
        pltpu.make_async_copy(grads.at[:half], stay, sems.at[0]),
        pltpu.make_async_copy(grads.at[half:], go, sems.at[1]),
    ]
    for copy in copies[::-1]:
        copy.start()
    small[2:3, :] = spread
    small[3:, :] = jnp.zeros((5, width), jnp.float32)
    for copy in copies:
        copy.wait()


def grad_call(dest, x0, x1, sums1, sums02, scale, hats1, hats02, gain, shift):
    width = x0.shape[1]
    pieces = dest.shape[1]
    vm = pl.BlockSpec(memory_space=pltpu.VMEM)
    hbm = pl.BlockSpec(memory_space=pl.ANY)
    half = jax.ShapeDtypeStruct((dest.shape[0] * pieces // 2, BS // pieces, BS), jnp.bfloat16)
    return pl.pallas_call(
        grad_kernel,
        out_shape=[
            half,
            half,
            jax.ShapeDtypeStruct((8, width), jnp.float32),
        ],
        in_specs=[pl.BlockSpec(memory_space=pltpu.SMEM)] + [vm] * 9,
        out_specs=[hbm, hbm, vm],
        scratch_shapes=[
            pltpu.VMEM((dest.shape[0] * pieces, BS // pieces, BS), jnp.bfloat16),
            pltpu.SemaphoreType.DMA((2,)),
        ],
        compiler_params=pltpu.CompilerParams(vmem_limit_bytes=VMEM_LIMIT),
        cost_estimate=pl.CostEstimate(flops=4 * 10**9, bytes_accessed=16 * 2**20, transcendentals=0),
        name="lens_gradient",
    )(dest, x0, x1, sums1, sums02, scale, hats1, hats02, gain, shift)


def merge(a, b):
    peak = jnp.maximum(a[:3], b[:3])
    return jnp.concatenate([peak, a[3:] * jnp.exp(a[:3] - peak) + b[3:] * jnp.exp(b[:3] - peak)], 0)


def ring(x, step):
    size = lax.axis_size("vocab")
    return lax.ppermute(x, "vocab", [(i, (i + 2 * step) % size) for i in range(size)])


def add(*terms):
    total = terms[0].astype(jnp.float32)
    for term in terms[1:]:
        total = total + term.astype(jnp.float32)
    return total.astype(terms[0].dtype)


def pace_kernel(x, out):
    out[...] = x[...]


def pace(x):
    vm = pl.BlockSpec(memory_space=pltpu.VMEM)
    return pl.pallas_call(
        pace_kernel,
        out_shape=jax.ShapeDtypeStruct((x.size // 128, 128), x.dtype),
        in_specs=[vm],
        out_specs=vm,
        cost_estimate=pl.CostEstimate(flops=6 * 10**10, bytes_accessed=2 * 10**8, transcendentals=0),
        name="pace",
    )(x.reshape(-1, 128)).reshape(x.shape)


def spread_group(x):
    chips = lax.axis_size("vocab") // 2
    near = jnp.stack([x] + [ring(x, o) for o in range(1, chips)], 0)
    return jnp.stack([near, swap(near, "vocab", 1)], 0)


def tie(*values):
    return lax.optimization_barrier(values)


def reduce_slots(grads, small):
    chips, rows = lax.axis_size("vocab") // 2, lax.axis_size("rows")
    bits = bits_of(rows)
    todo = [("rows", bit) for bit in bits] + [("vocab", bit) for bit in chip_bits(2 * chips)]

    def small_step(small):
        axis, bit = todo.pop(0)
        return small + swap(small, axis, bit)

    g = add(grads[0], swap(grads[1], "vocab", 1)).reshape(2, rows, chips // 2, -1, BS)
    g, small = tie(g, small)
    sides = [[g[side, e] for e in range(rows)] for side in range(2)]
    for at in range(len(bits)):
        for side in range(2):
            bit = (bits[::-1], bits)[side][at]
            h = sides[side]
            keep = [e for e in range(rows) if h[e] is not None and not e & bit]
            got = swap(jnp.stack([h[e | bit] for e in keep], 0), "rows", bit)
            sides[side] = [None] * rows
            for i, e in enumerate(keep):
                sides[side][e] = add(h[e], got[i])
        if todo:
            small = small_step(small)
        live = [[e for e in range(rows) if sides[side][e] is not None] for side in range(2)]
        flat = tie(small, *[sides[side][e] for side in range(2) for e in live[side]])
        small, flat = flat[0], list(flat[1:])
        for side in range(2):
            for e in live[side]:
                sides[side][e] = flat.pop(0)
    g = jnp.concatenate([sides[0][0], sides[1][0]], 0)
    mine = add(g[0], *[ring(g[o], o) for o in range(1, chips)])
    small = small_step(small)
    mine, small = tie(mine, small)
    parts = jnp.stack([mine] + [swap(mine, "rows", e) for e in range(1, rows)], 0)
    small = small_step(small)
    parts, small = tie(parts, small)
    while todo:
        small = small_step(small)
    return parts, small


def layer_norm(values, gain_row, shift_row):
    centred = values - jnp.mean(values, -1, keepdims=True)
    spread = jnp.mean(centred * centred, -1, keepdims=True)
    return centred * lax.rsqrt(spread + NORM_EPS) * gain_row + shift_row


def rotate(heads_in, position):
    half = ROT // 2
    freq = 10000.0 ** (-2.0 * jnp.arange(half, dtype=jnp.float32) / ROT)
    angle = position.astype(jnp.float32)[:, None] * freq[None, :]
    cosine = jnp.cos(angle)[:, None, :]
    sine = jnp.sin(angle)[:, None, :]
    first_half = heads_in[..., :half]
    second_half = heads_in[..., half:ROT]
    return jnp.concatenate(
        [
            first_half * cosine - second_half * sine,
            second_half * cosine + first_half * sine,
            heads_in[..., ROT:],
        ],
        -1,
    )


def partial_sums(logits, highest):
    shifted = jnp.exp(logits - highest[..., None])
    sums = jnp.sum(shifted, -1)
    cross = jnp.sum(shifted[..., :1, :] * (logits[..., :1, :] - logits[..., 1:, :]), -1)
    return (sums, cross)


def slope_terms(part_logits, part_norms, partition_count):
    target = jnp.exp(part_logits[:, :1] - part_norms[:, :1, None])
    probes = jnp.exp(part_logits[:, 1:] - part_norms[:, 1:, None])
    return (partition_count[:, None, None] * (probes - target)).astype(jnp.bfloat16)


def dense_path(
    tokens, loss_position_mask, lengths, owners, embed_in, unembedding_table, frozen_qkv, frozen_out,
    frozen_up, frozen_down, frozen_bias, norm_gain, norm_shift, master_matrix, lens_bias,
):
    width = embed_in.shape[1]
    shards = lax.axis_size("vocab")
    where = lax.axis_index("vocab")
    group = tokens.shape[0]
    own = group // shards
    units = frozen_up.shape[1]
    nblk = width // BS
    gathered, biases = (
        lax.all_gather(master_matrix, "vocab", axis=0, tiled=True),
        lax.all_gather(lens_bias, "vocab", axis=1, tiled=True),
    )
    order = jnp.argsort(owners)
    matrices = (
        jnp.take(gathered, order, axis=0)
        .reshape(2, nblk, nblk, BS, BS)
        .transpose(0, 1, 3, 2, 4)
        .reshape(2, width, width)
    )
    table_rows = embed_in.shape[0]
    local_ids = tokens - where * table_rows
    inside = (local_ids >= 0) & (local_ids < table_rows)
    looked = jnp.take(embed_in, jnp.clip(local_ids, 0, table_rows - 1), axis=0)
    looked = jnp.where(inside[:, None], looked, jnp.zeros((), jnp.bfloat16))
    embedded = lax.psum_scatter(looked, "vocab", scatter_dimension=0, tiled=True).astype(
        jnp.float32
    )
    seq_lens = lengths[0]
    index = where * own + jnp.arange(own, dtype=jnp.int32)
    segment, position = places(index, seq_lens)
    attn_in = layer_norm(embedded, norm_gain[0], norm_shift[0]).astype(jnp.bfloat16)
    mlp_in = layer_norm(embedded, norm_gain[1], norm_shift[1]).astype(jnp.bfloat16)
    projected = (
        jnp.dot(attn_in, frozen_qkv, preferred_element_type=jnp.float32) + frozen_bias[: 3 * width]
    )
    queries = rotate(projected[:, :width].reshape(own, HEADS, HEAD_DIM), position).astype(
        jnp.bfloat16
    )
    keys = rotate(projected[:, width : 2 * width].reshape(own, HEADS, HEAD_DIM), position).astype(
        jnp.bfloat16
    )
    values = projected[:, 2 * width :].astype(jnp.bfloat16)
    key_value = jnp.concatenate([keys.reshape(own, width), values], 1)
    piece = lax.all_gather(key_value, "vocab", axis=0, tiled=True)
    highest = jnp.full((HEADS, own), MASKED, jnp.float32)
    count = piece.shape[0]
    key_index = jnp.arange(count, dtype=jnp.int32)
    key_segment, _ = places(key_index, seq_lens)
    piece_keys = piece[:, :width].reshape(count, HEADS, HEAD_DIM)
    piece_values = piece[:, width:].reshape(count, HEADS, HEAD_DIM)
    attention_scores = jnp.einsum(
        "qhd,khd->hqk", queries, piece_keys, preferred_element_type=jnp.float32
    ) * HEAD_DIM ** (-0.5)
    allowed = (segment[:, None] == key_segment[None, :]) & (key_index[None, :] <= index[:, None])
    attention_scores = jnp.where(allowed[None], attention_scores, MASKED)
    new_high = jnp.maximum(highest, jnp.max(attention_scores, -1))
    weights = jnp.where(allowed[None], jnp.exp(attention_scores - new_high[..., None]), 0.0)
    totals = jnp.sum(weights, -1)
    accum = jnp.einsum(
        "hqk,khd->hqd",
        weights.astype(jnp.bfloat16),
        piece_values,
        preferred_element_type=jnp.float32,
    )
    highest, totals, accum = (new_high, totals, accum)
    mixed = (
        jnp.transpose(accum / totals[..., None], (1, 0, 2)).reshape(own, width).astype(jnp.bfloat16)
    )
    attn_out = (
        jnp.dot(mixed, frozen_out, preferred_element_type=jnp.float32)
        + frozen_bias[3 * width : 4 * width]
    )
    activ = jax.nn.gelu(
        jnp.dot(mlp_in, frozen_up, preferred_element_type=jnp.float32)
        + frozen_bias[4 * width : 4 * width + units],
        approximate=False,
    ).astype(jnp.bfloat16)
    layer_out = (
        embedded
        + attn_out
        + (
            jnp.dot(activ, frozen_down, preferred_element_type=jnp.float32)
            + frozen_bias[4 * width + units :]
        )
    )

    def final_norm(values_in):
        return layer_norm(values_in, norm_gain[2], norm_shift[2])

    sources = (embedded.astype(jnp.bfloat16), layer_out.astype(jnp.bfloat16))
    residual = (embedded, layer_out)
    normed = [final_norm(layer_out).astype(jnp.bfloat16)]
    pulls = []
    for which in range(2):
        product = jnp.dot(
            sources[which], matrices[which].astype(jnp.bfloat16), preferred_element_type=jnp.float32
        )
        lensed = residual[which] + product + biases[which]
        normed_out, pull = jax.vjp(final_norm, lensed)
        normed.append(normed_out.astype(jnp.bfloat16))
        pulls.append(pull)
    counted = loss_position_mask.astype(jnp.float32)
    vocab_cols = unembedding_table.shape[0]
    every = lax.all_gather(jnp.stack(normed), "vocab", axis=1, tiled=True)
    size = min(512, group)
    count = group // size
    blocks = every.reshape(3, count, size, width).transpose(1, 0, 2, 3)

    def block_high(normed_blk):
        logits_blk = jnp.einsum(
            "kbd,vd->bkv", normed_blk, unembedding_table, preferred_element_type=jnp.float32
        )
        return (logits_blk, jnp.max(logits_blk, -1))

    logits, highest = lax.map(block_high, blocks)
    highest = lax.pmax(highest.reshape(group, 3), "vocab")

    def block_sums(args):
        return partial_sums(args[0], args[1])

    sums, cross = lax.map(block_sums, (logits, highest.reshape(count, size, 3)))
    logits = logits.reshape(group, 3, vocab_cols)
    sums, cross = lax.psum((sums.reshape(group, 3), cross.reshape(group, 2)), "vocab")
    log_total = highest + jnp.log(sums)
    diverge = cross / sums[:, :1] - log_total[:, :1] + log_total[:, 1:]
    loss_sum, loss_count = lax.psum((jnp.sum(counted[:, None] * diverge), jnp.sum(counted)), "rows")
    loss_slope = slope_terms(logits, log_total, counted)
    dnormed = lax.psum_scatter(
        jnp.einsum(
            "yzq,qa->yza", loss_slope, unembedding_table, preferred_element_type=jnp.float32
        ),
        "vocab",
        scatter_dimension=0,
        tiled=True,
    )
    grads = []
    bias_grads = []
    for which in range(2):
        dlensed = pulls[which](dnormed[:, which])[0]
        bias_grads.append(jnp.sum(dlensed, 0))
        grads.append(
            jnp.einsum(
                "nd,ne->de",
                sources[which],
                dlensed.astype(jnp.bfloat16),
                preferred_element_type=jnp.float32,
            )
        )
    matrix_grad = (
        jnp.stack(grads).reshape(2, nblk, BS, nblk, BS).transpose(0, 1, 3, 2, 4).reshape(-1, BS, BS)
    )
    slot_grad = jnp.take(matrix_grad, owners, axis=0)
    bias_grad = jnp.stack(bias_grads)
    per_dev = master_matrix.shape[0]
    bias_cols = lens_bias.shape[1]
    slot_grad, bias_grad = lax.psum((slot_grad, bias_grad), ("rows", "vocab"))
    slot_grad = lax.dynamic_slice_in_dim(slot_grad, where * per_dev, per_dev, 0)
    bias_grad = lax.dynamic_slice_in_dim(bias_grad, where * bias_cols, bias_cols, 1)
    return slot_grad, bias_grad, loss_sum


def body(
    tokens, loss_position_mask, lengths, owners, embed_in, unembedding_table, frozen_qkv, frozen_out,
    frozen_up, frozen_down, frozen_bias, norm_gain, norm_shift, master_matrix, lens_bias, matrix_first,
    matrix_second, left_stat, right_stat, left_basis, right_basis, bias_first, bias_second,
):
    bf, f32, i32 = jnp.bfloat16, jnp.float32, jnp.int32
    shards, rows = lax.axis_size("vocab"), lax.axis_size("rows")
    where, row = lax.axis_index("vocab"), lax.axis_index("rows")
    group, width = tokens.shape[0], embed_in.shape[1]
    own = group // shards
    nblk = width // BS
    per = master_matrix.shape[0]
    blocks = shards * per
    chips = shards // 2
    vbits, rbits = chip_bits(shards), bits_of(rows)
    every = jnp.arange(shards, dtype=i32)

    chip, core = where // 2, where % 2
    entry_at = (chip - every // 2) % chips + chips * ((every % 2) ^ core)

    part_rows = per * BS // rows
    held = master_matrix.astype(bf).reshape(rows, part_rows, BS)
    held = lax.dynamic_index_in_dim(held, row, 0, keepdims=False)
    top = lens_bias.astype(bf)
    middle = (lens_bias - top.astype(f32)).astype(bf)
    low = (lens_bias - top.astype(f32) - middle.astype(f32)).astype(bf)
    flat = jnp.concatenate([jnp.pad(t.reshape(-1), (0, BS - lens_bias.size))[None] for t in (top, middle, low)], 0)
    held = jnp.concatenate([held, jnp.pad(flat, ((0, 13), (0, 0)))], 0)
    held = lax.all_gather(held, ("rows", "vocab"), axis=0)
    biases = jnp.sum(held[:shards, part_rows : part_rows + 3, : lens_bias.size].astype(f32), 1)
    biases = biases.reshape(shards, 2, -1).transpose(1, 0, 2).reshape(2, width)
    slots = held
    if per != rows:
        slots = held[:, :part_rows].reshape(rows, shards, part_rows, BS).transpose(1, 0, 2, 3)
        slots = slots.reshape(blocks, BS, BS)

    def by_class(a):
        return a.reshape(own, shards).T.reshape(-1)

    ids = by_class(tokens)
    index = by_class(jnp.arange(group, dtype=i32))
    mask = by_class(loss_position_mask)
    table_rows = embed_in.shape[0]
    owner = ids // table_rows
    local = ids - where * table_rows
    holds = (owner[:, None] == jnp.arange(shards, dtype=i32)[None, :]).astype(bf)
    before = (jnp.arange(group)[:, None] > jnp.arange(group)[None, :]).astype(bf)
    ahead = jnp.dot(before, holds, preferred_element_type=f32)
    rank = jnp.sum(ahead * holds.astype(f32), 1).astype(i32)
    take = 176 if group <= 1024 else 64

    def chunk():
        slot = jnp.arange(take, dtype=i32)[:, None]
        hit = (owner == where)[None, :] & (rank[None, :] == slot)
        picked = jnp.sum(jnp.where(hit, local[None, :], 0), 1)
        mine = jnp.take(embed_in, picked, axis=0, mode="clip")
        return mine

    def exchange(mine):
        near = [mine]
        for o in range(1, chips):
            near.append(lax.ppermute(mine, "vocab", [(i, (i + 2 * o) % shards) for i in range(shards)]))
        return near + [swap(piece, "vocab", 1) for piece in near]

    mine, mask = tie(chunk(), mask)
    pieces_in = exchange(mine)
    mask, index, seq_lens, rank, owner, owners = tie(pace(mask), index, lengths[0], rank, owner, owners)
    apart = (chip - owner // 2) % chips + chips * ((owner % 2) ^ core)
    column = jnp.where(rank < take, apart * take + rank, -1)
    most = jnp.max(jnp.sum(holds.astype(f32), 0)).astype(i32)
    shared = gather_xor(jnp.concatenate([mask, jnp.full((8,), most, i32)]), "rows", rbits)
    masks = shared[:, :group].reshape(rows, shards, own)
    most = jnp.max(shared[:, group:])


    segment, position = places(index, seq_lens)
    half = ROT // 2
    lane = jnp.arange(2 * HEAD_DIM) % HEAD_DIM
    freq = 10000.0 ** (-2.0 * (lane % half).astype(f32) / ROT)
    angle = position.astype(f32)[:, None] * freq[None, :]
    turns = (lane < ROT)[None, :]
    cosines = jnp.where(turns, jnp.cos(angle), 1.0)
    sines = jnp.where(turns, jnp.sin(angle) * jnp.where(lane < half, -1.0, 1.0)[None, :], 0.0)
    key_meta = jnp.concatenate([segment[None], index[None], jnp.zeros((6, group), i32)], 0)
    meta = jnp.stack([column, segment, index], 1)
    bias_row = frozen_bias.reshape(1, -1)
    spot = where.reshape(1)

    take_rows = max(16, 320 // shards)
    count = take_rows * shards
    mine_masks = lax.dynamic_index_in_dim(masks, where, 1, keepdims=False)
    per_row = jnp.sum(mine_masks, 1)
    lower = (row ^ jnp.arange(rows)) < row
    base = jnp.sum(jnp.where(lower, per_row, 0))
    dealt = base + jnp.cumsum(mine_masks[0]) - mine_masks[0]
    per_class = jnp.sum(masks, (0, 2))
    entry_chip = (chip - jnp.arange(chips)) % chips
    per_entry = jnp.concatenate(
        [jnp.take(per_class, entry_chip * 2 + core), jnp.take(per_class, entry_chip * 2 + (core ^ 1))]
    )
    share = (per_entry - row + rows - 1) // rows
    rounds = -(-jnp.max((per_class + rows - 1) // rows) // take_rows)

    numbers = jnp.arange(blocks, dtype=i32)
    pieces = max(1, rows // per)
    span = per * pieces // rows
    slot_of = jnp.sum(jnp.where(owners[None, :] == numbers[:, None], numbers[None, :], 0), 1)
    device, inner = slot_of // per, slot_of % per
    away_core = (device % 2) ^ core
    ahead_by = (device // 2 - chip) % chips
    piece = inner[:, None] * pieces + jnp.arange(pieces, dtype=i32)[None, :]
    part = (piece // span) ^ row
    half_chips = chips // 2
    dest = (away_core * 2 + ahead_by // half_chips)[:, None] * rows + part
    dest = (dest * half_chips + (ahead_by % half_chips)[:, None]) * span + piece % span
    loc = inner * shards + device if per == rows else slot_of

    def pick_of(k):
        target = jnp.arange(rows, dtype=i32) ^ row
        place = jnp.arange(take_rows, dtype=i32) + k * take_rows
        wanted = (place[None, :] * rows + target[:, None]).reshape(-1)
        return ((dealt[None, :] == wanted[:, None]) & (mine_masks[0] > 0)[None, :]).astype(bf)

    def across(sent):
        return add(sent[0], *[swap(sent[e], "rows", e) for e in range(1, rows)])

    def spread_out(sent):
        return spread_group(across(sent)).reshape(count, width)

    def share_stats(local):
        stats = local.reshape(6, 2, chips, take_rows)
        total = stats
        for o in range(1, chips):
            total = merge(total, jnp.roll(ring(stats, o), o, 2))
        return merge(total, jnp.flip(swap(total, "vocab", 1), 1)).reshape(6, count)

    def counted_in(k):
        place = jnp.arange(take_rows, dtype=i32)[None, :] + k * take_rows
        return (place < share[:, None]).reshape(-1).astype(f32)

    def with_loss(small, valid, stats):
        logtot = stats[:3] + jnp.log(stats[3:])
        loss = jnp.sum(valid * (logtot[1] + logtot[2] - 2.0 * logtot[0]))
        first_lane = (jnp.arange(width) == 0)[None, :] & (jnp.arange(8) == 2)[:, None]
        return small + jnp.where(first_lane & (where == 0), loss, 0.0)

    overflow = ((most > take) | (rounds > 1)).astype(i32)

    def dense(c):
        k, *given = tie(
            c[0], tokens, loss_position_mask, lengths, owners, embed_in, unembedding_table, frozen_qkv, frozen_out,
            frozen_up, frozen_down, frozen_bias, norm_gain, norm_shift, master_matrix, lens_bias,
        )
        grad, grad_bias, loss = dense_path(*given)
        turned_grad = jnp.take(grad.reshape(rows, -1, BS), jnp.arange(rows) ^ row, axis=0)
        return (k + 1, turned_grad.astype(bf), grad_bias, loss)

    pick = pick_of(jnp.int32(0))
    emb_own, *sent0 = place_call(rows, spot, pieces_in, meta, pick)
    got0 = across(sent0)
    k_all, v_all, q_own = project_call(
        own, spot, pieces_in, meta, cosines, sines, bias_row, norm_gain, norm_shift, frozen_qkv
    )
    got0, q_own = tie(got0, q_own)
    near0 = jnp.stack([got0] + [ring(got0, o) for o in range(1, chips)], 0)
    out_own, *sent1 = layer_call(
        rows, spot, k_all, v_all, q_own, emb_own, meta, key_meta, bias_row, norm_gain, norm_shift, pick,
        frozen_out, frozen_up, frozen_down,
    )
    near0, *sent1 = tie(near0, *sent1)
    x0 = jnp.stack([near0, swap(near0, "vocab", 1)], 0).reshape(count, width)
    sent1 = [sent1[0]] + [swap(sent1[e], "rows", e) for e in range(1, rows)]
    held1, hats1, *kept = probe_call((0,), "start", unembedding_table, loc, x0, slots, biases, norm_gain, norm_shift)
    *sent1, kept[-1] = tie(*sent1, kept[-1])
    got1 = add(*sent1)
    near1 = jnp.stack([got1] + [ring(got1, o) for o in range(1, chips)], 0)
    sums1, stats1 = probe_call((0,), "rest", unembedding_table, held1, *kept)
    near1, stats1 = tie(near1, stats1)
    x1 = jnp.stack([near1, swap(near1, "vocab", 1)], 0).reshape(count, width)
    sums02, stats02, hats02 = probe_call(
        (-1, 1), "all", unembedding_table, loc, x1, slots, biases, norm_gain, norm_shift
    )
    part_shape = (rows, span * BS // pieces, BS)
    done, stats02 = tie(jnp.int32(0), stats02)
    start = (done, jnp.zeros(part_shape, bf), jnp.zeros(lens_bias.shape, f32), jnp.float32(0.0))
    _, dense_parts, dense_bias, dense_loss = lax.while_loop(lambda c: c[0] < overflow, dense, start)
    stats02, dense_parts = tie(stats02, dense_parts)
    local_stats = jnp.concatenate([stats02[0:1], stats1[0:1], stats02[1:3], stats1[1:2], stats02[3:4]], 0)
    local_stats = local_stats[:, :count]
    stats = share_stats(local_stats)
    valid = counted_in(jnp.int32(0))
    scale = valid[None, :] * jnp.exp(local_stats[:3] - stats[:3]) / stats[3:]
    scale = jnp.pad(scale, ((0, 5), (0, -(-count // 128) * 128 - count)))
    *grads, small = grad_call(dest, x0, x1, sums1, sums02, scale, hats1, hats02, norm_gain, norm_shift)

    slot_parts, small = reduce_slots(grads, with_loss(small, valid, stats))
    full = jnp.where(overflow > 0, dense_parts, slot_parts)
    loss_count = jnp.sum(masks).astype(f32)

    loss_sum = jnp.where(overflow > 0, dense_loss, jnp.sum(small[2]))
    bias_grad = small[:2]
    bias_cols = lens_bias.shape[1]
    bias_grad = lax.dynamic_slice_in_dim(bias_grad, where * bias_cols, bias_cols, 1)
    bias_grad = jnp.where(overflow > 0, dense_bias, bias_grad)

    if per >= rows:
        slot_grad = full.reshape(per, BS, BS)
        turn = row * (per // rows)
    else:
        slot_grad = jnp.take(full, row ^ jnp.arange(rows), axis=0).reshape(per, BS, BS)
        turn = jnp.int32(0)

    (new_matrix, new_first, new_second, new_left, new_right, renewed_left_basis, new_rbasis) = soap_call(
        turn.reshape(1), master_matrix, slot_grad, matrix_first, matrix_second, left_stat, right_stat,
        left_basis, right_basis,
    )
    new_bias, new_bias_first, new_bias_second = adam_bias(lens_bias, bias_grad, bias_first, bias_second)
    return (
        loss_sum, loss_count, new_matrix, new_first, new_second, new_left, new_right, renewed_left_basis,
        new_rbasis, new_bias, new_bias_first, new_bias_second,
    )


def solution(mesh):
    in_specs = (
        P("rows"),
        P("rows"),
        P("rows", None),
        P(),
        P("vocab", None),
        P("vocab", None),
        P(),
        P(),
        P(),
        P(),
        P(),
        P(),
        P(),
        P("vocab", None, None),
        P(None, "vocab"),
        P("vocab", None, None),
        P("vocab", None, None),
        P("vocab", None, None),
        P("vocab", None, None),
        P("vocab", None, None),
        P("vocab", None, None),
        P(None, "vocab"),
        P(None, "vocab"),
    )
    out_specs = (
        P(),
        P(),
        P("vocab", None, None),
        P("vocab", None, None),
        P("vocab", None, None),
        P("vocab", None, None),
        P("vocab", None, None),
        P("vocab", None, None),
        P("vocab", None, None),
        P(None, "vocab"),
        P(None, "vocab"),
        P(None, "vocab"),
    )
    return jax.shard_map(body, mesh=mesh, in_specs=in_specs, out_specs=out_specs, check_vma=False)
```
